32 devices in a mesh: grp: 2 (over y), bx: 16 (over z, x, core).
Axes of the slice: x: 2, y: 2, z: 4, core: 2. Of those that a mesh axis runs over, the one named last changes fastest.
Arguments:
- density_map: float32 [128, 64, 256], P(('grp', 'bx')), parts along dimension 0, may hold values from -6 to 6
- amplitude: float32 [65536], P(('grp', 'bx')), parts along dimension 0, may hold values from 0.5 to 4
- fraction: float32 [3, 65536], P(None, ('grp', 'bx')), parts along dimension 1, may hold values from 0.25 to 0.75
- torsion_axis: float32 [3, 65536], P(None, ('grp', 'bx')), parts along dimension 1, may hold values from -4 to 4
- brick_owner: int32 [65536, 1], P(('grp', 'bx')), parts along dimension 0, may hold values from 0 to 15; in each aligned block of 2048 rows (0 to 2047, 2048 to 4095, ...) at most 384 rows name the same one
- plane_offset: int32 [65536], P(('grp', 'bx')), parts along dimension 0, may hold values from 0 to 3
- row_offset: int32 [65536], P(('grp', 'bx')), parts along dimension 0, may hold values from 0 to 63
- column_offset: int32 [65536], P(('grp', 'bx')), parts along dimension 0, may hold values from 0 to 255
- chain_index: int32 [65536], P(('grp', 'bx')), parts along dimension 0, may hold values from 0 to 7, never falling along the last dimension, each value on 1 to 16384 neighbouring positions
Outputs:
- torques: float32 [2, 65536], P(None, ('grp', 'bx')), parts along dimension 1
- atom_gradient: float32 [6, 65536], P(None, ('grp', 'bx')), parts along dimension 1
The draws below stay inside these ranges and needn't reach their ends.
There are 2 independent parts, one for each index of `grp`. The reference program is written for one: setup_inputs(seed, part) draws one part's arguments, and reference() takes and returns one part's arrays. A program takes and returns all parts, laid end to end along the dimension named above; each array names one. Nothing has to cross between parts.
Inputs may be any that keep to these rules, and one draw needn't show every extreme that they name: `brick_owner`: among the atoms of one device, at most 384 lie in one slab, and exactly 384 in some slab for some device. `chain_index`: never falls along the atoms, so each chain is one run of atoms; a chain may cover many devices.
All inputs are finite; a program needn't handle non-finite values.
Results may differ from the reference program's by a relative error of at most 0.0003.
Values sent between devices are 32-bit elements; how exact they have to be, the bound alone decides.
No kernel may reach another device: no remote copies, remote signals or barrier semaphores. Data moves between devices by JAX's collectives and lax.ppermute only.
A program may use at most 64 MiB of HBM per device.

```python
import math
import jax
import jax.numpy as jnp
import numpy as np
from jax import lax

PLANES = 4
ROWS = 64
COLUMNS = 256
ATOM_DEV = 2048
CAP = 384
NX = 64
ATOMS = 32768
N_BX = 16


def place_ends(entries, key, low, largest):
    longest = entries.shape.index(max(entries.shape))
    spots = []
    for shift in (0, 1):
        where = [jax.random.randint(jax.random.fold_in(key, axis), (), 0, length) for axis, length in enumerate(entries.shape)]
        where[longest] = (where[longest] + shift) % entries.shape[longest]
        spots.append(tuple(where))
    return entries.at[spots[0]].set(low).at[spots[1]].set(largest)


def steps_of(stream_key, dims, cuts, smallest, high):
    loudness, own = 1.0, jax.random.fold_in(stream_key, 6)
    for position, shards_of in cuts:
        steps = jnp.exp(jax.random.uniform(jax.random.fold_in(own, position), (shards_of,), jnp.float32, smallest / len(cuts), high / len(cuts)))
        loudness = loudness * jnp.repeat(steps, dims[position] // shards_of).reshape([-1 if axis == position else 1 for axis in range(len(dims))])
    return loudness


def profile(amount, total, reach, slope):
    weights = [(1 << 20) // math.isqrt(grade ** slope) + 1 for grade in range(2, amount + 1)]
    rest, counts = total - reach - (amount - 1), [1] * (amount - 1)
    while rest > 0:
        movable = [i for i in range(amount - 1) if counts[i] < reach]
        pool, remaining = sum([weights[i] for i in movable]), rest
        for i in movable:
            more = min(reach - counts[i], max(1, remaining * weights[i] // pool), rest)
            counts[i] = counts[i] + more
            rest = rest - more
    return np.array([reach] + counts)


def ragged_sizes(rng, count, total, reach, slope):
    if count == 2:
        one = jax.random.randint(rng, (), max(1, total - reach), min(reach, total - 1) + 1)
        return jnp.stack([one, total - one])
    tallies = jnp.asarray(profile(count, total, reach, slope), jnp.int32)
    pairs = (count - 1) // 2
    donor, taker = tallies[1:1 + 2 * pairs:2], tallies[2:2 + 2 * pairs:2]
    margin = jnp.minimum(donor - 1, reach - taker)
    shifted = jax.random.randint(jax.random.fold_in(rng, 1), (pairs,), 0, 1 << 20) % (margin + 1)
    tallies = tallies.at[1:1 + 2 * pairs:2].set(donor - shifted).at[2:2 + 2 * pairs:2].set(taker + shifted)
    return tallies[jax.random.permutation(jax.random.fold_in(rng, 2), count)]


def assign_block(stream_key, own, number, rows, count, top, limit, slope):
    ranking = jax.random.permutation(stream_key, count)
    crowded, common = shares(count, rows * top, limit, slope, True), shares(count, rows * top, limit, slope, False)
    places = jnp.arange(count)

    def named(sizes, turn):
        used = int((sizes > 0).sum())
        fixed = max(1, used // 4)
        shifted = fixed + (places - fixed + turn * (used - fixed)) % max(1, count - fixed)
        return jnp.zeros((count,), jnp.int32).at[ranking[jnp.where(places < fixed, places, shifted)]].set(jnp.asarray(sizes, jnp.int32))

    sizes = jnp.where(number % 4 == 0, named(crowded, number // 4), named(common, number - number // 4 - 1))
    mixed = jax.random.permutation(jax.random.fold_in(own, 3), count)
    source_of, taker = mixed[0:count // 2 * 2:2], mixed[1:count // 2 * 2:2]
    room = jnp.minimum(sizes[source_of] - 1, limit - sizes[taker]) // 2
    room = jnp.where((source_of == ranking[0]) | (taker == ranking[0]) | (sizes[taker] == 0), 0, jnp.maximum(room, 0))
    shifted = jax.random.randint(jax.random.fold_in(own, 4), (count // 2,), 0, 1 << 20) % (room + 1)
    sizes = sizes.at[source_of].add(-shifted).at[taker].add(shifted)
    items = jnp.searchsorted(jnp.cumsum(sizes), jnp.arange(rows * top), side="right").astype(jnp.int32)
    table = items.reshape(top, rows).T
    table = table[jax.random.permutation(jax.random.fold_in(own, 1), rows)]
    turn = jax.random.randint(jax.random.fold_in(own, 2), (rows, 1), 0, top)
    return jnp.take_along_axis(table, (jnp.arange(top)[None, :] + turn) % top, axis=1)


def shares(count, total, most, lean, full):
    portions = [(1 << 20) // math.isqrt(rank ** lean) + 1 for rank in range(1, count + 1)]
    largest = most if full else min(most, max(-(-total // count), total * portions[0] // sum(portions)))
    least = 1 if total - largest >= count - 1 else 0
    holding, surplus = [largest] + [least] * (count - 1), total - largest - least * (count - 1)
    while surplus > 0:
        movable = [i for i in range(1, count) if holding[i] < largest] or [i for i in range(1, count) if holding[i] < most]
        whole, left = sum([portions[i] for i in movable]), surplus
        for i in movable:
            addition = min(most - holding[i], max(1, left * portions[i] // whole), surplus)
            holding[i] = holding[i] + addition
            surplus = surplus - addition
    return np.array(holding)


def normal_values(key, dims, spread, most, split=(), held_as=jnp.bfloat16):
    values = spread * jax.random.normal(key, dims, jnp.float32)
    if split:
        values = values * steps_of(key, dims, split, -0.22, 0.18)
    return jnp.clip(values, -most, most).astype(held_as)


def setup_inputs(seed: int = 0, part: int = 0) -> dict:
    streams_of = jax.random.split(jax.random.key(seed), 10)
    part_splits = jax.random.split(jax.random.fold_in(streams_of[9], part), 10)
    density_map = normal_values(part_splits[0], (NX, ROWS, COLUMNS), 1.0, 6.0, ((0, 16),), jnp.float32)
    amplitude = jnp.clip(jnp.exp(math.log(4.0) - 2.0794415 * jax.random.uniform(part_splits[1], (ATOMS,), jnp.float32) ** steps_of(part_splits[1], (ATOMS,), ((0, 16),), -0.2, 0.2)), 0.5, 4.0)
    fraction = jnp.clip(0.25 + 0.5 * jax.random.uniform(part_splits[2], (3, ATOMS), jnp.float32) ** steps_of(part_splits[2], (3, ATOMS), ((1, 16),), -0.2, 0.2), 0.25, 0.75)
    torsion_axis = normal_values(part_splits[3], (3, ATOMS), 0.6, 4.0, ((1, 16),), jnp.float32)
    brick_owner_keys = jax.random.split(jax.random.fold_in(part_splits[4], 1), ATOMS // ATOM_DEV)
    brick_owner_turns = jax.random.permutation(jax.random.fold_in(part_splits[4], 3), ATOMS // ATOM_DEV)
    brick_owner = jax.vmap(lambda own, number: assign_block(jax.random.fold_in(part_splits[4], 2), own, number, ATOM_DEV, N_BX, 1, CAP, 2))(brick_owner_keys, brick_owner_turns).reshape((ATOMS, 1))
    plane_offset = place_ends(jax.random.randint(part_splits[5], (ATOMS,), 0, PLANES), jax.random.fold_in(part_splits[5], 1), 0, PLANES - 1).astype(jnp.int32)
    row_offset = place_ends(jax.random.randint(part_splits[6], (ATOMS,), 0, ROWS), jax.random.fold_in(part_splits[6], 1), 0, ROWS - 1).astype(jnp.int32)
    column_offset = place_ends(jax.random.randint(part_splits[7], (ATOMS,), 0, COLUMNS), jax.random.fold_in(part_splits[7], 1), 0, COLUMNS - 1).astype(jnp.int32)
    chain_index = jnp.searchsorted(jnp.cumsum(ragged_sizes(part_splits[8], N_BX // 2, ATOMS, 8 * ATOM_DEV, 2)), jnp.arange(ATOMS), side="right").astype(jnp.int32)
    return {"density_map": density_map, "amplitude": amplitude, "fraction": fraction, "torsion_axis": torsion_axis, "brick_owner": brick_owner, "plane_offset": plane_offset, "row_offset": row_offset, "column_offset": column_offset, "chain_index": chain_index}


side_tap = 0.25
middle_tap = 0.5
probe_step = 0.2

def blur_whole(volume):
    padded = jnp.pad(volume, ((1, 1), (0, 0), (0, 0)))
    volume = side_tap * padded[:-2] + middle_tap * padded[1:-1] + side_tap * padded[2:]
    volume = side_tap * jnp.roll(volume, 1, 1) + middle_tap * volume + side_tap * jnp.roll(volume, -1, 1)
    return side_tap * jnp.roll(volume, 1, 2) + middle_tap * volume + side_tap * jnp.roll(volume, -1, 2)

def corner_list(fraction, global_plane, row_offset, column_offset):
    listing = []
    for lift_x in (0, 1):
        for lift_y in (0, 1):
            for lift_z in (0, 1):
                weight_x = fraction[0] if lift_x else 1.0 - fraction[0]
                weight_y = fraction[1] if lift_y else 1.0 - fraction[1]
                weight_z = fraction[2] if lift_z else 1.0 - fraction[2]
                plane_at = global_plane + lift_x
                inside = (plane_at < NX).astype(jnp.float32)
                target = plane_at * (ROWS * COLUMNS) + (row_offset + lift_y) % ROWS * COLUMNS + (column_offset + lift_z) % COLUMNS
                target = jnp.where(plane_at < NX, target, 0).astype(jnp.int32)
                listing.append(((lift_x, lift_y, lift_z), (weight_x, weight_y, weight_z), target, inside))
    return listing

def evaluate_whole(fraction, amplitude, global_plane, row_offset, column_offset, density_map):
    listing = corner_list(fraction, global_plane, row_offset, column_offset)
    targets = jnp.concatenate([item[2] for item in listing])
    values = jnp.concatenate([amplitude * item[1][0] * item[1][1] * item[1][2] * item[3] for item in listing])
    density = jnp.zeros((NX * ROWS * COLUMNS,), jnp.float32).at[targets].add(values)
    density = density.reshape(NX, ROWS, COLUMNS)
    misfit = blur_whole(density) - density_map
    flat = blur_whole(misfit).reshape(-1)
    totals = [jnp.zeros_like(amplitude) for _ in range(3)]
    for lifts, weights, target, inside in listing:
        sampled = flat[target] * inside
        others = (weights[1] * weights[2], weights[0] * weights[2], weights[0] * weights[1])
        for which in range(3):
            sign = 1.0 if lifts[which] else -1.0
            totals[which] = totals[which] + sampled * sign * others[which]
    return jnp.stack([amplitude * item for item in totals])

def cross_rows(left, right):
    return jnp.stack([left[1] * right[2] - left[2] * right[1], left[2] * right[0] - left[0] * right[2], left[0] * right[1] - left[1] * right[0]])

def join_chain(earlier, later):
    return (later[0], later[1] + jnp.where(earlier[0] == later[0], earlier[1], 0.0))

def chain_suffix(values, chains):
    flipped = (chains[::-1][None, :], values[:, ::-1])
    result = lax.associative_scan(join_chain, flipped, axis=1)
    return result[1][:, ::-1]

def reference(density_map, amplitude, fraction, torsion_axis, brick_owner, plane_offset, row_offset, column_offset, chain_index):
    global_plane = (brick_owner[:, 0] * PLANES + plane_offset).astype(jnp.int32)
    first = evaluate_whole(fraction, amplitude, global_plane, row_offset, column_offset, density_map)
    moved = fraction - probe_step * jnp.tanh(first)
    second = evaluate_whole(moved, amplitude, global_plane, row_offset, column_offset, density_map)
    cells = jnp.stack([global_plane.astype(jnp.float32), row_offset.astype(jnp.float32), column_offset.astype(jnp.float32)])
    positions = (cells + fraction, cells + moved)
    gradients = (first, second)
    pieces = []
    for which in range(2):
        pieces.append(gradients[which])
        pieces.append(cross_rows(positions[which], gradients[which]))
    pieces.append(jnp.ones((1, amplitude.shape[0]), jnp.float32))
    totals = chain_suffix(jnp.concatenate(pieces, 0), chain_index)
    torques = []
    for which in range(2):
        force = totals[6 * which:6 * which + 3]
        moment = totals[6 * which + 3:6 * which + 6]
        arm = cross_rows(positions[which], force)
        torques.append(lax.optimization_barrier(jnp.sum(torsion_axis * (moment - arm), 0)) / (COLUMNS * jnp.sqrt(totals[12])))
    return (jnp.stack(torques), jnp.concatenate([first, second], 0))
```

```python
import functools

import jax
import jax.numpy as jnp
from jax import lax
from jax.experimental import pallas as pl
from jax.experimental.pallas import tpu as pltpu
from jax.sharding import PartitionSpec as P

side_tap = 0.25
middle_tap = 0.5
probe_step = 0.2
lanes = 128
fields = 8
f32, bf16 = jnp.float32, jnp.bfloat16
room = 48 * 1024 * 1024


def dot_nt(left, right):
    return lax.dot_general(left, right, (((1,), (1,)), ((), ())), preferred_element_type=f32)


def dot_nn(left, right):
    return lax.dot_general(left, right, (((1,), (0,)), ((), ())), preferred_element_type=f32)


def halves(x):
    high = x.astype(bf16)
    return high, (x - high.astype(f32)).astype(bf16)


def thirds(x):
    high, rest = x.astype(bf16), None
    rest = x - high.astype(f32)
    middle = rest.astype(bf16)
    return high, middle, (rest - middle.astype(f32)).astype(bf16)


def down_rows(count, width):
    return lax.broadcasted_iota(jnp.int32, (count, width), 0)


def spread(row, count):
    tile = jnp.broadcast_to(row, (16, row.shape[1])).astype(bf16)
    return jnp.concatenate([tile] * (count // 16), 0)


def counting(count, width):
    part = down_rows(count, lanes).astype(f32).astype(bf16)
    return jnp.concatenate([part] * (width // lanes), 1)


def pack_kernel(
    devices, sub, rows, owner_ref, plane_ref, row_ref, column_ref, chain_ref, amp_ref, frac_ref,
    message_ref, slot_ref,
):
    atoms = owner_ref.shape[1]
    blocks = atoms // lanes
    tiles = devices * sub
    owner = owner_ref[...]
    mine = down_rows(devices, atoms) == owner
    onehot = jnp.where(mine, 1.0, 0.0)
    stacked = jnp.concatenate(
        [onehot[:, j * lanes : (j + 1) * lanes] for j in range(blocks)], 0
    ).astype(bf16)
    k = lax.broadcasted_iota(jnp.int32, (lanes, 2 * lanes), 0)
    a = lax.broadcasted_iota(jnp.int32, (lanes, 2 * lanes), 1)
    before = jnp.where((k < a) | (a >= lanes), 1.0, 0.0).astype(bf16)
    counts = dot_nn(stacked, before)
    running = jnp.zeros((devices, lanes), f32)
    ranks = []
    for j in range(blocks):
        part = counts[j * devices : (j + 1) * devices]
        here = onehot[:, j * lanes : (j + 1) * lanes]
        ranks.append(jnp.sum((part[:, :lanes] + running) * here, 0, keepdims=True))
        running = running + part[:, lanes:]
    rank = jnp.concatenate(ranks, 1).astype(jnp.int32)
    tile = owner * sub + lax.shift_right_logical(rank, 7)
    lane = rank & (lanes - 1)
    slot_ref[...] = jnp.concatenate([tile, lane], 0)
    values = jnp.concatenate(
        [
            (plane_ref[...] * rows + row_ref[...]).astype(f32),
            column_ref[...].astype(f32),
            frac_ref[...],
            amp_ref[...],
            chain_ref[...].astype(f32),
            jnp.zeros((1, atoms), f32),
        ],
        0,
    )
    pieces = [piece.astype(f32) for piece in thirds(values)]
    width = 512
    for c in range(atoms // width):
        at = slice(c * width, (c + 1) * width)
        spot = jnp.where(down_rows(lanes, width) == lane[:, at], 1.0, 0.0).astype(bf16)
        which = jnp.broadcast_to(tile[:, at], (fields, width))
        picks = [which == t for t in range(tiles)]
        total = None
        for piece in pieces:
            part = piece[:, at]
            left = jnp.concatenate([jnp.where(pick, part, 0.0) for pick in picks], 0).astype(bf16)
            one = dot_nt(left, spot)
            total = one if total is None else total + one
        if c == 0:
            message_ref[...] = total
        else:
            message_ref[...] += total
    last = jnp.broadcast_to(chain_ref[:, atoms - 1 :].astype(f32), (1, lanes))
    for b in range(devices):
        message_ref[b * sub * fields + fields - 1 : b * sub * fields + fields, :] = last


def neighbours_of(state, rows, columns):
    cell, column = state[0:1], state[1:2]
    plane = jnp.floor(cell * (1.0 / rows))
    row = cell - plane * rows
    next_row = jnp.where(row == rows - 1.0, 0.0, row + 1.0)
    next_column = jnp.where(column == columns - 1.0, 0.0, column + 1.0)
    return plane, row, next_row, column, next_column


def density_part(state, planes, rows, columns):
    width = state.shape[1]
    plane, row, next_row, column, next_column = neighbours_of(state, rows, columns)
    fx, fy, fz, amplitude = (state[2 + i : 3 + i] for i in range(4))
    zero = jnp.zeros((), bf16)
    steps = counting(columns, width)
    here, there = steps == spread(column, columns), steps == spread(next_column, columns)

    def columns_of(near, far):
        return jnp.where(here, spread(near, columns), jnp.where(there, spread(far, columns), zero))

    near, far = halves(1.0 - fz), halves(fz)
    right_high = columns_of(near[0].astype(f32), far[0].astype(f32))
    right_low = columns_of(near[1].astype(f32), far[1].astype(f32))
    level = down_rows(fields, width).astype(f32)
    along = amplitude * jnp.where(level == plane, 1.0 - fx, jnp.where(level == plane + 1.0, fx, 0.0))
    near, far = halves(along * (1.0 - fy)), halves(along * fy)
    steps = counting(rows, width)
    here, there = steps == spread(row, rows), steps == spread(next_row, rows)
    lefts = []
    for grade in range(2):
        first, second = near[grade].astype(f32), far[grade].astype(f32)
        lefts.append(
            jnp.concatenate(
                [
                    jnp.where(
                        here,
                        spread(first[p : p + 1], rows),
                        jnp.where(there, spread(second[p : p + 1], rows), zero),
                    )
                    for p in range(planes + 1)
                ],
                0,
            )
        )
    return (
        dot_nt(lefts[0], right_high) + dot_nt(lefts[0], right_low) + dot_nt(lefts[1], right_high)
    )


def gradient_part(state, table_ref, planes, rows, columns):
    width = state.shape[1]
    plane, row, next_row, column, _ = neighbours_of(state, rows, columns)
    fx, fy, fz, amplitude = (state[2 + i : 3 + i] for i in range(4))
    spot = jnp.where(
        counting(columns, width) == spread(column, columns),
        jnp.ones((), bf16),
        jnp.zeros((), bf16),
    )
    sampled = dot_nn(table_ref[...], jnp.concatenate([spot, spot], 0))
    sheets = [sampled[i * rows : (i + 1) * rows] for i in range(2 * (planes + 1))]
    steps = down_rows(rows, width).astype(f32)
    at_plane = [jnp.broadcast_to(plane, (rows, width)) == float(p) for p in range(planes)]
    at_row = (steps == row, steps == next_row)
    corner = {}
    for e2 in range(2):
        for e0 in range(2):
            chosen = sheets[e2 * (planes + 1) + e0]
            for p in range(1, planes):
                chosen = jnp.where(at_plane[p], sheets[e2 * (planes + 1) + e0 + p], chosen)
            for e1 in range(2):
                corner[e0, e1, e2] = jnp.sum(jnp.where(at_row[e1], chosen, 0.0), 0, keepdims=True)
    wx, wy, wz = (1.0 - fx, fx), (1.0 - fy, fy), (1.0 - fz, fz)
    gx = gy = gz = 0.0
    for u in range(2):
        for v in range(2):
            gx = gx + wy[u] * wz[v] * (corner[1, u, v] - corner[0, u, v])
            gy = gy + wx[u] * wz[v] * (corner[u, 1, v] - corner[u, 0, v])
            gz = gz + wx[u] * wy[v] * (corner[u, v, 1] - corner[u, v, 0])
    return jnp.concatenate([amplitude * gx, amplitude * gy, amplitude * gz], 0)


def blur_sheet(sheet):
    rows, columns = sheet.shape
    sheet = middle_tap * sheet + side_tap * (pltpu.roll(sheet, 1, 0) + pltpu.roll(sheet, rows - 1, 0))
    return middle_tap * sheet + side_tap * (
        pltpu.roll(sheet, 1, 1) + pltpu.roll(sheet, columns - 1, 1)
    )


def blur_along(sheets):
    return [
        middle_tap * sheets[i] + side_tap * (sheets[i - 1] + sheets[i + 1])
        for i in range(1, len(sheets) - 1)
    ]


def make_table(
    place_ref, devices, planes, rows, columns, own_ref, below_ref, above_ref, map_ref, map_below_ref,
    map_above_ref, table_ref,
):
    not_first = jnp.where(place_ref[0] == 0, 0.0, 1.0)
    not_last = jnp.where(place_ref[0] == devices - 1, 0.0, 1.0)
    own = [own_ref[p * rows : (p + 1) * rows, :] for p in range(planes + 1)]
    below = [below_ref[p * rows : (p + 1) * rows, :] for p in range(3)]
    above = [above_ref[p * rows : (p + 1) * rows, :] for p in range(3)]
    own[0] = own[0] + below[2]
    own[planes] = own[planes] * not_last + above[0]
    density = blur_along(below[:2] + own + above[1:])
    observed = (
        [map_below_ref[0]] + [map_ref[p] for p in range(planes)] + [map_above_ref[0], map_above_ref[1]]
    )
    misfit = [blur_sheet(sheet) - seen for sheet, seen in zip(density, observed)]
    misfit[0] = misfit[0] * not_first
    misfit[planes + 1] = misfit[planes + 1] * not_last
    misfit[planes + 2] = misfit[planes + 2] * not_last
    pulled = [blur_sheet(sheet) for sheet in blur_along(misfit)]
    pulled[planes] = pulled[planes] * not_last
    for p in range(planes + 1):
        shifted = pltpu.roll(pulled[p], columns - 1, 1)
        for turn, sheet in enumerate((pulled[p], shifted)):
            high, low = halves(sheet)
            at = slice((turn * (planes + 1) + p) * rows, (turn * (planes + 1) + p + 1) * rows)
            table_ref[at, :columns] = high
            table_ref[at, columns:] = low


def load_tiles(ref, first, count):
    return jnp.concatenate(
        [
            ref[pl.ds(pl.multiple_of((first + i) * fields, fields), fields), :]
            for i in range(count)
        ],
        1,
    )


def store_tiles(ref, first, count, value):
    for i in range(count):
        ref[pl.ds(pl.multiple_of((first + i) * fields, fields), fields), :] = value[
            :, i * lanes : (i + 1) * lanes
        ]


def share_out(total_ref, planes, rows, own_ref, up_ref, down_ref):
    own_ref[...] = total_ref[...]
    up_ref[...] = total_ref[(planes - 2) * rows :, :]
    down_ref[...] = total_ref[: 3 * rows, :]


def density_kernel(planes, rows, columns, batch, message_ref, own_ref, up_ref, down_ref):
    tiles = message_ref.shape[0] // fields
    own_ref[...] = jnp.zeros_like(own_ref)

    def step(i, carry):
        state = load_tiles(message_ref, i * batch, batch)
        own_ref[...] += density_part(state, planes, rows, columns)
        return carry

    lax.fori_loop(0, tiles // batch, step, 0)
    up_ref[...] = own_ref[(planes - 2) * rows :, :]
    down_ref[...] = own_ref[: 3 * rows, :]


def middle_kernel(
    devices, planes, rows, columns, batch, place_ref, message_ref, was_ref, below_ref, above_ref,
    map_ref, map_below_ref, map_above_ref, moved_ref, first_ref, own_ref, up_ref, down_ref, table_ref,
):
    tiles = message_ref.shape[0] // fields
    make_table(
        place_ref, devices, planes, rows, columns, was_ref, below_ref, above_ref, map_ref,
        map_below_ref, map_above_ref, table_ref,
    )
    own_ref[...] = jnp.zeros_like(own_ref)

    def step(i, carry):
        state = load_tiles(message_ref, i * batch, batch)
        gradient = gradient_part(state, table_ref, planes, rows, columns)
        moved = jnp.concatenate(
            [state[0:2], state[2:5] - probe_step * jnp.tanh(gradient), state[5:8]], 0
        )
        store_tiles(moved_ref, i * batch, batch, moved)
        store_tiles(
            first_ref, i * batch, batch,
            jnp.concatenate([gradient, jnp.zeros((5, gradient.shape[1]), f32)], 0),
        )
        own_ref[...] += density_part(moved, planes, rows, columns)
        return carry

    lax.fori_loop(0, tiles // batch, step, 0)
    up_ref[...] = own_ref[(planes - 2) * rows :, :]
    down_ref[...] = own_ref[: 3 * rows, :]


def cross_list(left, right):
    return [
        left[1] * right[2] - left[2] * right[1],
        left[2] * right[0] - left[0] * right[2],
        left[0] * right[1] - left[1] * right[0],
    ]


def last_kernel(
    devices, sub, planes, rows, columns, batch, place_ref, message_ref, moved_ref, first_ref, was_ref,
    below_ref, above_ref, map_ref, map_below_ref, map_above_ref, reply_ref, table_ref, sums_ref,
):
    tiles = message_ref.shape[0] // fields
    make_table(
        place_ref, devices, planes, rows, columns, was_ref, below_ref, above_ref, map_ref,
        map_below_ref, map_above_ref, table_ref,
    )
    sums_ref[...] = jnp.zeros_like(sums_ref)
    last_of = jnp.concatenate(
        [
            message_ref[d * sub * fields + fields - 1 : d * sub * fields + fields, :]
            for d in range(devices)
        ],
        0,
    )
    width = batch * lanes
    last_of = jnp.concatenate([last_of] * batch, 1)
    receiver = down_rows(devices, width)
    slab_plane = (place_ref[0] * planes).astype(f32)

    def step(i, carry):
        state = load_tiles(message_ref, i * batch, batch)
        moved = load_tiles(moved_ref, i * batch, batch)
        first = load_tiles(first_ref, i * batch, batch)[0:3]
        second = gradient_part(moved, table_ref, planes, rows, columns)
        plane, row, _, column, _ = neighbours_of(state, rows, columns)
        base = (plane + slab_plane, row, column)
        pieces = []
        for gradient, offset in ((first, state), (second, moved)):
            g = [gradient[d : d + 1] for d in range(3)]
            pieces += g + cross_list([base[d] + offset[2 + d : 3 + d] for d in range(3)], g)
        pieces.append(jnp.where(state[5:6] > 0.0, 1.0, 0.0))
        pieces.append(jnp.zeros((3, width), f32))
        block = jnp.concatenate(pieces, 0)
        source = jnp.concatenate(
            [
                jnp.full((devices, lanes), (i * batch + t) // sub, jnp.int32)
                for t in range(batch)
            ],
            1,
        )
        chosen = jnp.where((source > receiver) & (last_of == state[6:7]), 1.0, 0.0).astype(bf16)
        part = sum(dot_nt(chosen, piece) for piece in thirds(block))
        sums_ref[:, : part.shape[1]] += part
        store_tiles(
            reply_ref, i * batch, batch,
            jnp.concatenate([first, second, jnp.zeros((2, width), f32)], 0),
        )
        return carry

    lax.fori_loop(0, tiles // batch, step, 0)
    for d in range(devices):
        reply_ref[d * sub * fields + fields - 1 : d * sub * fields + fields, :] = sums_ref[
            d : d + 1, :
        ]


def chain_kernel(
    devices, sub, planes, columns, reply_ref, slot_ref, owner_ref, plane_ref, row_ref, column_ref,
    chain_ref, chain_rows_ref, frac_ref, axis_ref, torque_ref, gradient_ref,
):
    atoms = owner_ref.shape[1]
    blocks = atoms // lanes
    tiles = devices * sub
    high, low = halves(reply_ref[...])
    left = jnp.concatenate([high, low], 1)
    width = 512
    found = []
    for c in range(atoms // width):
        at = slice(c * width, (c + 1) * width)
        spot = jnp.where(down_rows(lanes, width) == slot_ref[1:2, at], 1.0, 0.0).astype(bf16)
        picked = dot_nn(left, jnp.concatenate([spot, spot], 0))
        which = jnp.broadcast_to(slot_ref[0:1, at], (fields, width))
        total = jnp.zeros((fields, width), f32)
        for t in range(tiles):
            total = jnp.where(which == t, picked[t * fields : (t + 1) * fields], total)
        found.append(total)
    gradients = jnp.concatenate(found, 1)[0:6]
    gradient_ref[...] = gradients
    fraction = frac_ref[...]
    moved = fraction - probe_step * jnp.tanh(gradients[0:3])
    base = (
        (owner_ref[...] * planes + plane_ref[...]).astype(f32),
        row_ref[...].astype(f32),
        column_ref[...].astype(f32),
    )
    positions = [[base[d] + offset[d : d + 1] for d in range(3)] for offset in (fraction, moved)]
    pieces = []
    for e in range(2):
        g = [gradients[3 * e + d : 3 * e + d + 1] for d in range(3)]
        pieces += g + cross_list(positions[e], g)
    pieces.append(jnp.ones((1, atoms), f32))
    pieces.append(jnp.zeros((3, atoms), f32))
    stacked = jnp.concatenate(thirds(jnp.concatenate(pieces, 0)), 0)

    def joined(x):
        return x[0:16] + x[16:32] + x[32:48]

    chain = chain_ref[...].astype(f32)
    chain_rows = chain_rows_ref[...].astype(f32)
    ends = jnp.broadcast_to(chain_rows[:, lanes - 1 :], (blocks, atoms))
    later = lax.broadcasted_iota(jnp.int32, (blocks, atoms), 1) >= lanes * (
        down_rows(blocks, atoms) + 1
    )
    bridge = jnp.where(later & (ends == chain), 1.0, 0.0).astype(bf16)
    carries = joined(dot_nt(stacked, bridge))
    arrived = jnp.zeros((1, lanes), f32)
    for d in range(devices):
        arrived = arrived + reply_ref[d * sub * fields + fields - 1 : d * sub * fields + fields, :]
    diagonal = down_rows(16, lanes) == lax.broadcasted_iota(jnp.int32, (16, lanes), 1)
    arrived = jnp.sum(jnp.where(diagonal, arrived, 0.0), 1, keepdims=True)
    padded = jnp.concatenate([chain_rows, jnp.zeros((lanes - blocks, lanes), f32)], 0)
    down_chain = jnp.transpose(padded)
    not_before = down_rows(lanes, lanes) >= lax.broadcasted_iota(jnp.int32, (lanes, lanes), 1)
    closing = chain[:, atoms - 1 :]
    sums = []
    for j in range(blocks):
        at = slice(j * lanes, (j + 1) * lanes)
        mask = not_before & (down_chain[:, j : j + 1] == chain[:, at])
        local = joined(dot_nn(stacked[:, at], jnp.where(mask, 1.0, 0.0).astype(bf16)))
        end = chain[:, (j + 1) * lanes - 1 : (j + 1) * lanes]
        carry = carries[:, j : j + 1] + jnp.where(end == closing, arrived, 0.0)
        sums.append(local + jnp.where(chain[:, at] == end, carry, 0.0))
    totals = jnp.concatenate(sums, 1)
    scale = 1.0 / (columns * jnp.sqrt(totals[12:13]))
    torques = []
    for e in range(2):
        force = [totals[6 * e + d : 6 * e + d + 1] for d in range(3)]
        lever = cross_list(positions[e], force)
        turn = 0.0
        for d in range(3):
            turn = turn + axis_ref[d : d + 1] * (totals[6 * e + 3 + d : 6 * e + 4 + d] - lever[d])
        torques.append(turn * scale)
    torque_ref[...] = jnp.concatenate(torques, 0)


def whole(count):
    return [pl.BlockSpec(memory_space=pltpu.VMEM)] * count


def settings():
    return pltpu.CompilerParams(vmem_limit_bytes=room)


def shape_of(*dims, dtype=f32):
    return jax.ShapeDtypeStruct(dims, dtype)


def shift(value, by):
    count = lax.axis_size("bx")
    return lax.ppermute(value, "bx", [(i, i + by) for i in range(count) if 0 <= i + by < count])


def exchange(value):
    return lax.all_to_all(value, "bx", split_axis=0, concat_axis=0, tiled=True)


def shards(
    density_map,
    amplitude,
    fraction,
    torsion_axis,
    brick_owner,
    plane_offset,
    row_offset,
    column_offset,
    chain_index,
):
    planes, rows, columns = density_map.shape
    atoms = amplitude.shape[0]
    devices = lax.axis_size("bx")
    capacity = 3 * atoms // devices
    sub = -(-capacity // lanes)
    tiles = devices * sub
    batch = 4
    grid = (planes, rows, columns)
    place = lax.axis_index("bx").astype(jnp.int32).reshape(1)
    scalar = [pl.BlockSpec(memory_space=pltpu.SMEM)]

    map_below = shift(density_map[planes - 1 :], 1)
    map_above = shift(density_map[:2], -1)

    owner, plane, row, column, chain = (
        item.reshape(1, atoms)
        for item in (brick_owner, plane_offset, row_offset, column_offset, chain_index)
    )
    message, slot = pl.pallas_call(
        functools.partial(pack_kernel, devices, sub, rows),
        out_shape=(shape_of(tiles * fields, lanes), shape_of(2, atoms, dtype=jnp.int32)),
        in_specs=whole(7),
        out_specs=whole(2),
        compiler_params=settings(),
        name="pack",
    )(owner, plane, row, column, chain, amplitude.reshape(1, atoms), fraction)
    message = exchange(message)

    own_shape = shape_of((planes + 1) * rows, columns)
    edge_shape = shape_of(3 * rows, columns)
    own, up, down = pl.pallas_call(
        functools.partial(density_kernel, *grid, batch),
        out_shape=(own_shape, edge_shape, edge_shape),
        in_specs=whole(1),
        out_specs=whole(3),
        compiler_params=settings(),
        name="density",
    )(message)
    below, above = shift(up, 1), shift(down, -1)
    table = pltpu.VMEM((2 * (planes + 1) * rows, 2 * columns), bf16)
    moved, first, own, up, down = pl.pallas_call(
        functools.partial(middle_kernel, devices, *grid, batch),
        out_shape=(
            shape_of(tiles * fields, lanes),
            shape_of(tiles * fields, lanes),
            own_shape,
            edge_shape,
            edge_shape,
        ),
        in_specs=scalar + whole(7),
        out_specs=whole(5),
        scratch_shapes=[table],
        compiler_params=settings(),
        name="middle",
    )(place, message, own, below, above, density_map, map_below, map_above)
    below, above = shift(up, 1), shift(down, -1)
    reply = pl.pallas_call(
        functools.partial(last_kernel, devices, sub, *grid, batch),
        out_shape=shape_of(tiles * fields, lanes),
        in_specs=scalar + whole(9),
        out_specs=whole(1)[0],
        scratch_shapes=[table, pltpu.VMEM((devices, lanes), f32)],
        compiler_params=settings(),
        name="last",
    )(place, message, moved, first, own, below, above, density_map, map_below, map_above)
    reply = exchange(reply)
    torques, gradients = pl.pallas_call(
        functools.partial(chain_kernel, devices, sub, planes, columns),
        out_shape=(shape_of(2, atoms), shape_of(6, atoms)),
        in_specs=whole(10),
        out_specs=whole(2),
        compiler_params=settings(),
        name="chains",
    )(
        reply, slot, owner, plane, row, column, chain, chain_index.reshape(atoms // lanes, lanes),
        fraction, torsion_axis,
    )
    return torques, gradients


def solution(mesh):
    return jax.shard_map(
        shards,
        mesh=mesh,
        in_specs=(
            P(("grp", "bx"), None, None),
            P(("grp", "bx")),
            P(None, ("grp", "bx")),
            P(None, ("grp", "bx")),
            P(("grp", "bx"), None),
            P(("grp", "bx")),
            P(("grp", "bx")),
            P(("grp", "bx")),
            P(("grp", "bx")),
        ),
        out_specs=(P(None, ("grp", "bx")), P(None, ("grp", "bx"))),
        check_vma=False,
    )
```

```python
import functools

import jax
import jax.numpy as jnp
from jax import lax
from jax.experimental import pallas as pl
from jax.experimental.pallas import tpu as pltpu
from jax.sharding import PartitionSpec as P

side_tap = 0.25
middle_tap = 0.5
probe_step = 0.2
lanes = 128
fields = 8
f32, bf16 = jnp.float32, jnp.bfloat16
room = 48 * 1024 * 1024


def dot_nt(left, right):
    return lax.dot_general(left, right, (((1,), (1,)), ((), ())), preferred_element_type=f32)


def dot_nn(left, right):
    return lax.dot_general(left, right, (((1,), (0,)), ((), ())), preferred_element_type=f32)


def halves(x):
    high = x.astype(bf16)
    return high, (x - high.astype(f32)).astype(bf16)


def thirds(x):
    high, rest = x.astype(bf16), None
    rest = x - high.astype(f32)
    middle = rest.astype(bf16)
    return high, middle, (rest - middle.astype(f32)).astype(bf16)


def down_rows(count, width):
    return lax.broadcasted_iota(jnp.int32, (count, width), 0)


def spread(row, count):
    tile = jnp.broadcast_to(row, (16, row.shape[1])).astype(bf16)
    return jnp.concatenate([tile] * (count // 16), 0)


def counting(count, width):
    part = down_rows(count, lanes).astype(f32).astype(bf16)
    return jnp.concatenate([part] * (width // lanes), 1)


def pack_kernel(
    devices, sub, rows, owner_ref, plane_ref, row_ref, column_ref, chain_ref, amp_ref, frac_ref,
    message_ref, slot_ref,
):
    atoms = owner_ref.shape[1]
    blocks = atoms // lanes
    tiles = devices * sub
    owner = owner_ref[...]
    mine = down_rows(devices, atoms) == owner
    onehot = jnp.where(mine, 1.0, 0.0)
    stacked = jnp.concatenate(
        [onehot[:, j * lanes : (j + 1) * lanes] for j in range(blocks)], 0
    ).astype(bf16)
    k = lax.broadcasted_iota(jnp.int32, (lanes, 2 * lanes), 0)
    a = lax.broadcasted_iota(jnp.int32, (lanes, 2 * lanes), 1)
    before = jnp.where((k < a) | (a >= lanes), 1.0, 0.0).astype(bf16)
    counts = dot_nn(stacked, before)
    running = jnp.zeros((devices, lanes), f32)
    ranks = []
    for j in range(blocks):
        part = counts[j * devices : (j + 1) * devices]
        here = onehot[:, j * lanes : (j + 1) * lanes]
        ranks.append(jnp.sum((part[:, :lanes] + running) * here, 0, keepdims=True))
        running = running + part[:, lanes:]
    rank = jnp.concatenate(ranks, 1).astype(jnp.int32)
    tile = owner * sub + lax.shift_right_logical(rank, 7)
    lane = rank & (lanes - 1)
    slot_ref[...] = jnp.concatenate([tile, lane], 0)
    values = jnp.concatenate(
        [
            (plane_ref[...] * rows + row_ref[...]).astype(f32),
            column_ref[...].astype(f32),
            frac_ref[...],
            amp_ref[...],
            chain_ref[...].astype(f32),
            jnp.zeros((1, atoms), f32),
        ],
        0,
    )
    pieces = [piece.astype(f32) for piece in thirds(values)]
    width = 512
    for c in range(atoms // width):
        at = slice(c * width, (c + 1) * width)
        spot = jnp.where(down_rows(lanes, width) == lane[:, at], 1.0, 0.0).astype(bf16)
        which = jnp.broadcast_to(tile[:, at], (fields, width))
        picks = [which == t for t in range(tiles)]
        total = None
        for piece in pieces:
            part = piece[:, at]
            left = jnp.concatenate([jnp.where(pick, part, 0.0) for pick in picks], 0).astype(bf16)
            one = dot_nt(left, spot)
            total = one if total is None else total + one
        if c == 0:
            message_ref[...] = total
        else:
            message_ref[...] += total
    last = jnp.broadcast_to(chain_ref[:, atoms - 1 :].astype(f32), (1, lanes))
    for b in range(devices):
        message_ref[b * sub * fields + fields - 1 : b * sub * fields + fields, :] = last


def neighbours_of(state, rows, columns):
    cell, column = state[0:1], state[1:2]
    plane = jnp.floor(cell * (1.0 / rows))
    row = cell - plane * rows
    next_row = jnp.where(row == rows - 1.0, 0.0, row + 1.0)
    next_column = jnp.where(column == columns - 1.0, 0.0, column + 1.0)
    return plane, row, next_row, column, next_column


def density_part(state, planes, rows, columns):
    width = state.shape[1]
    plane, row, next_row, column, next_column = neighbours_of(state, rows, columns)
    fx, fy, fz, amplitude = (state[2 + i : 3 + i] for i in range(4))
    zero = jnp.zeros((), bf16)
    steps = counting(columns, width)
    here, there = steps == spread(column, columns), steps == spread(next_column, columns)

    def columns_of(near, far):
        return jnp.where(here, spread(near, columns), jnp.where(there, spread(far, columns), zero))

    near, far = halves(1.0 - fz), halves(fz)
    right_high = columns_of(near[0].astype(f32), far[0].astype(f32))
    right_low = columns_of(near[1].astype(f32), far[1].astype(f32))
    level = down_rows(fields, width).astype(f32)
    along = amplitude * jnp.where(level == plane, 1.0 - fx, jnp.where(level == plane + 1.0, fx, 0.0))
    near, far = halves(along * (1.0 - fy)), halves(along * fy)
    steps = counting(rows, width)
    here, there = steps == spread(row, rows), steps == spread(next_row, rows)
    lefts = []
    for grade in range(2):
        first, second = near[grade].astype(f32), far[grade].astype(f32)
        lefts.append(
            jnp.concatenate(
                [
                    jnp.where(
                        here,
                        spread(first[p : p + 1], rows),
                        jnp.where(there, spread(second[p : p + 1], rows), zero),
                    )
                    for p in range(planes + 1)
                ],
                0,
            )
        )
    return (
        dot_nt(lefts[0], right_high) + dot_nt(lefts[0], right_low) + dot_nt(lefts[1], right_high)
    )


def gradient_part(state, table_ref, planes, rows, columns):
    width = state.shape[1]
    plane, row, next_row, column, _ = neighbours_of(state, rows, columns)
    fx, fy, fz, amplitude = (state[2 + i : 3 + i] for i in range(4))
    spot = jnp.where(
        counting(columns, width) == spread(column, columns),
        jnp.ones((), bf16),
        jnp.zeros((), bf16),
    )
    sampled = dot_nn(table_ref[...], jnp.concatenate([spot, spot], 0))
    sheets = [sampled[i * rows : (i + 1) * rows] for i in range(2 * (planes + 1))]
    steps = down_rows(rows, width).astype(f32)
    at_plane = [jnp.broadcast_to(plane, (rows, width)) == float(p) for p in range(planes)]
    at_row = (steps == row, steps == next_row)
    corner = {}
    for e2 in range(2):
        for e0 in range(2):
            chosen = sheets[e2 * (planes + 1) + e0]
            for p in range(1, planes):
                chosen = jnp.where(at_plane[p], sheets[e2 * (planes + 1) + e0 + p], chosen)
            for e1 in range(2):
                corner[e0, e1, e2] = jnp.sum(jnp.where(at_row[e1], chosen, 0.0), 0, keepdims=True)
    wx, wy, wz = (1.0 - fx, fx), (1.0 - fy, fy), (1.0 - fz, fz)
    gx = gy = gz = 0.0
    for u in range(2):
        for v in range(2):
            gx = gx + wy[u] * wz[v] * (corner[1, u, v] - corner[0, u, v])
            gy = gy + wx[u] * wz[v] * (corner[u, 1, v] - corner[u, 0, v])
            gz = gz + wx[u] * wy[v] * (corner[u, v, 1] - corner[u, v, 0])
    return jnp.concatenate([amplitude * gx, amplitude * gy, amplitude * gz], 0)


def blur_sheet(sheet):
    rows, columns = sheet.shape
    sheet = middle_tap * sheet + side_tap * (pltpu.roll(sheet, 1, 0) + pltpu.roll(sheet, rows - 1, 0))
    return middle_tap * sheet + side_tap * (
        pltpu.roll(sheet, 1, 1) + pltpu.roll(sheet, columns - 1, 1)
    )


def blur_along(sheets):
    return [
        middle_tap * sheets[i] + side_tap * (sheets[i - 1] + sheets[i + 1])
        for i in range(1, len(sheets) - 1)
    ]


def edges(place_ref, devices):
    not_first = jnp.where(place_ref[0] == 0, 0.0, 1.0)
    not_last = jnp.where(place_ref[0] == devices - 1, 0.0, 1.0)
    return not_first, not_last


def share_misfit(place_ref, devices, planes, rows, total, map_ref, own_ref, up_ref, down_ref):
    _, not_last = edges(place_ref, devices)
    density = [total[p * rows : (p + 1) * rows] for p in range(planes + 1)]
    density[planes] = density[planes] * not_last
    zero = jnp.zeros_like(density[0])
    parts = [blur_sheet(sheet) for sheet in blur_along([zero, zero] + density + [zero, zero])]
    for p in range(planes):
        parts[p + 1] = parts[p + 1] - map_ref[p]
    for p in range(planes + 3):
        own_ref[p * rows : (p + 1) * rows, :] = parts[p]
    for p in range(3):
        up_ref[p * rows : (p + 1) * rows, :] = parts[planes + p]
        down_ref[p * rows : (p + 1) * rows, :] = parts[p]


def make_table(place_ref, devices, planes, rows, columns, own_ref, below_ref, above_ref, table_ref):
    not_first, not_last = edges(place_ref, devices)
    misfit = [own_ref[p * rows : (p + 1) * rows, :] for p in range(planes + 3)]
    for p in range(3):
        misfit[p] = misfit[p] + below_ref[p * rows : (p + 1) * rows, :]
        misfit[planes + p] = misfit[planes + p] + above_ref[p * rows : (p + 1) * rows, :]
    misfit[0] = misfit[0] * not_first
    misfit[planes + 1] = misfit[planes + 1] * not_last
    misfit[planes + 2] = misfit[planes + 2] * not_last
    pulled = [blur_sheet(sheet) for sheet in blur_along(misfit)]
    pulled[planes] = pulled[planes] * not_last
    for p in range(planes + 1):
        shifted = pltpu.roll(pulled[p], columns - 1, 1)
        for turn, sheet in enumerate((pulled[p], shifted)):
            high, low = halves(sheet)
            at = slice((turn * (planes + 1) + p) * rows, (turn * (planes + 1) + p + 1) * rows)
            table_ref[at, :columns] = high
            table_ref[at, columns:] = low


def load_tiles(ref, first, count):
    return jnp.concatenate(
        [
            ref[(first + i) * fields : (first + i + 1) * fields, :] for i in range(count)
        ],
        1,
    )


def store_tiles(ref, first, count, value):
    for i in range(count):
        ref[(first + i) * fields : (first + i + 1) * fields, :] = value[
            :, i * lanes : (i + 1) * lanes
        ]


def all_density(state_ref, planes, rows, columns, batch):
    tiles = state_ref.shape[0] // fields
    total = None
    for i in range(tiles // batch):
        part = density_part(load_tiles(state_ref, i * batch, batch), planes, rows, columns)
        total = part if total is None else total + part
    return total


def density_kernel(
    devices, planes, rows, columns, batch, place_ref, message_ref, map_ref, own_ref, up_ref, down_ref
):
    total = all_density(message_ref, planes, rows, columns, batch)
    share_misfit(place_ref, devices, planes, rows, total, map_ref, own_ref, up_ref, down_ref)


def middle_kernel(
    devices, planes, rows, columns, batch, place_ref, message_ref, was_ref, below_ref, above_ref,
    map_ref, moved_ref, first_ref, own_ref, up_ref, down_ref, table_ref,
):
    tiles = message_ref.shape[0] // fields
    make_table(
        place_ref, devices, planes, rows, columns, was_ref, below_ref, above_ref, table_ref
    )
    for i in range(tiles // batch):
        state = load_tiles(message_ref, i * batch, batch)
        gradient = gradient_part(state, table_ref, planes, rows, columns)
        moved = jnp.concatenate(
            [state[0:2], state[2:5] - probe_step * jnp.tanh(gradient), state[5:8]], 0
        )
        store_tiles(moved_ref, i * batch, batch, moved)
        store_tiles(
            first_ref, i * batch, batch,
            jnp.concatenate([gradient, jnp.zeros((5, gradient.shape[1]), f32)], 0),
        )
    total = all_density(moved_ref, planes, rows, columns, batch)
    share_misfit(place_ref, devices, planes, rows, total, map_ref, own_ref, up_ref, down_ref)


def cross_list(left, right):
    return [
        left[1] * right[2] - left[2] * right[1],
        left[2] * right[0] - left[0] * right[2],
        left[0] * right[1] - left[1] * right[0],
    ]


def last_kernel(
    devices, sub, planes, rows, columns, batch, place_ref, message_ref, moved_ref, first_ref, was_ref,
    below_ref, above_ref, reply_ref, table_ref, sums_ref,
):
    tiles = message_ref.shape[0] // fields
    make_table(
        place_ref, devices, planes, rows, columns, was_ref, below_ref, above_ref, table_ref
    )
    sums_ref[...] = jnp.zeros_like(sums_ref)
    last_of = jnp.concatenate(
        [
            message_ref[d * sub * fields + fields - 1 : d * sub * fields + fields, :]
            for d in range(devices)
        ],
        0,
    )
    width = batch * lanes
    last_of = jnp.concatenate([last_of] * batch, 1)
    receiver = down_rows(devices, width)
    slab_plane = (place_ref[0] * planes).astype(f32)

    for i in range(tiles // batch):
        state = load_tiles(message_ref, i * batch, batch)
        moved = load_tiles(moved_ref, i * batch, batch)
        first = load_tiles(first_ref, i * batch, batch)[0:3]
        second = gradient_part(moved, table_ref, planes, rows, columns)
        plane, row, _, column, _ = neighbours_of(state, rows, columns)
        base = (plane + slab_plane, row, column)
        pieces = []
        for gradient, offset in ((first, state), (second, moved)):
            g = [gradient[d : d + 1] for d in range(3)]
            pieces += g + cross_list([base[d] + offset[2 + d : 3 + d] for d in range(3)], g)
        pieces.append(jnp.where(state[5:6] > 0.0, 1.0, 0.0))
        pieces.append(jnp.zeros((3, width), f32))
        block = jnp.concatenate(pieces, 0)
        source = jnp.concatenate(
            [
                jnp.full((devices, lanes), (i * batch + t) // sub, jnp.int32)
                for t in range(batch)
            ],
            1,
        )
        chosen = jnp.where((source > receiver) & (last_of == state[6:7]), 1.0, 0.0).astype(bf16)
        part = sum(dot_nt(chosen, piece) for piece in thirds(block))
        sums_ref[:, : part.shape[1]] += part
        store_tiles(
            reply_ref, i * batch, batch,
            jnp.concatenate([first, second, jnp.zeros((2, width), f32)], 0),
        )
    for d in range(devices):
        reply_ref[d * sub * fields + fields - 1 : d * sub * fields + fields, :] = sums_ref[
            d : d + 1, :
        ]


def chain_kernel(
    devices, sub, planes, columns, reply_ref, slot_ref, owner_ref, plane_ref, row_ref, column_ref,
    chain_ref, chain_rows_ref, frac_ref, axis_ref, torque_ref, gradient_ref,
):
    atoms = owner_ref.shape[1]
    blocks = atoms // lanes
    tiles = devices * sub
    high, low = halves(reply_ref[...])
    left = jnp.concatenate([high, low], 1)
    width = 512
    found = []
    for c in range(atoms // width):
        at = slice(c * width, (c + 1) * width)
        spot = jnp.where(down_rows(lanes, width) == slot_ref[1:2, at], 1.0, 0.0).astype(bf16)
        picked = dot_nn(left, jnp.concatenate([spot, spot], 0))
        which = jnp.broadcast_to(slot_ref[0:1, at], (fields, width))
        total = jnp.zeros((fields, width), f32)
        for t in range(tiles):
            total = jnp.where(which == t, picked[t * fields : (t + 1) * fields], total)
        found.append(total)
    gradients = jnp.concatenate(found, 1)[0:6]
    gradient_ref[...] = gradients
    fraction = frac_ref[...]
    moved = fraction - probe_step * jnp.tanh(gradients[0:3])
    base = (
        (owner_ref[...] * planes + plane_ref[...]).astype(f32),
        row_ref[...].astype(f32),
        column_ref[...].astype(f32),
    )
    positions = [[base[d] + offset[d : d + 1] for d in range(3)] for offset in (fraction, moved)]
    pieces = []
    for e in range(2):
        g = [gradients[3 * e + d : 3 * e + d + 1] for d in range(3)]
        pieces += g + cross_list(positions[e], g)
    pieces.append(jnp.ones((1, atoms), f32))
    pieces.append(jnp.zeros((3, atoms), f32))
    stacked = jnp.concatenate(thirds(jnp.concatenate(pieces, 0)), 0)

    def joined(x):
        return x[0:16] + x[16:32] + x[32:48]

    chain = chain_ref[...].astype(f32)
    chain_rows = chain_rows_ref[...].astype(f32)
    ends = jnp.broadcast_to(chain_rows[:, lanes - 1 :], (blocks, atoms))
    later = lax.broadcasted_iota(jnp.int32, (blocks, atoms), 1) >= lanes * (
        down_rows(blocks, atoms) + 1
    )
    bridge = jnp.where(later & (ends == chain), 1.0, 0.0).astype(bf16)
    carries = joined(dot_nt(stacked, bridge))
    arrived = jnp.zeros((1, lanes), f32)
    for d in range(devices):
        arrived = arrived + reply_ref[d * sub * fields + fields - 1 : d * sub * fields + fields, :]
    diagonal = down_rows(16, lanes) == lax.broadcasted_iota(jnp.int32, (16, lanes), 1)
    arrived = jnp.sum(jnp.where(diagonal, arrived, 0.0), 1, keepdims=True)
    padded = jnp.concatenate([chain_rows, jnp.zeros((lanes - blocks, lanes), f32)], 0)
    down_chain = jnp.transpose(padded)
    not_before = down_rows(lanes, lanes) >= lax.broadcasted_iota(jnp.int32, (lanes, lanes), 1)
    closing = chain[:, atoms - 1 :]
    sums = []
    for j in range(blocks):
        at = slice(j * lanes, (j + 1) * lanes)
        mask = not_before & (down_chain[:, j : j + 1] == chain[:, at])
        local = joined(dot_nn(stacked[:, at], jnp.where(mask, 1.0, 0.0).astype(bf16)))
        end = chain[:, (j + 1) * lanes - 1 : (j + 1) * lanes]
        carry = carries[:, j : j + 1] + jnp.where(end == closing, arrived, 0.0)
        sums.append(local + jnp.where(chain[:, at] == end, carry, 0.0))
    totals = jnp.concatenate(sums, 1)
    scale = 1.0 / (columns * jnp.sqrt(totals[12:13]))
    torques = []
    for e in range(2):
        force = [totals[6 * e + d : 6 * e + d + 1] for d in range(3)]
        lever = cross_list(positions[e], force)
        turn = 0.0
        for d in range(3):
            turn = turn + axis_ref[d : d + 1] * (totals[6 * e + 3 + d : 6 * e + 4 + d] - lever[d])
        torques.append(turn * scale)
    torque_ref[...] = jnp.concatenate(torques, 0)


def whole(count):
    return [pl.BlockSpec(memory_space=pltpu.VMEM)] * count


def settings():
    return pltpu.CompilerParams(vmem_limit_bytes=room)


def shape_of(*dims, dtype=f32):
    return jax.ShapeDtypeStruct(dims, dtype)


def shift(value, by):
    count = lax.axis_size("bx")
    return lax.ppermute(value, "bx", [(i, i + by) for i in range(count) if 0 <= i + by < count])


def exchange(value):
    return lax.all_to_all(value, "bx", split_axis=0, concat_axis=0, tiled=True)


def shards(
    density_map,
    amplitude,
    fraction,
    torsion_axis,
    brick_owner,
    plane_offset,
    row_offset,
    column_offset,
    chain_index,
):
    planes, rows, columns = density_map.shape
    atoms = amplitude.shape[0]
    devices = lax.axis_size("bx")
    capacity = 3 * atoms // devices
    sub = -(-capacity // lanes)
    tiles = devices * sub
    batch = max(b for b in range(1, 25) if tiles % b == 0)
    grid = (planes, rows, columns)
    place = lax.axis_index("bx").astype(jnp.int32).reshape(1)
    scalar = [pl.BlockSpec(memory_space=pltpu.SMEM)]

    owner, plane, row, column, chain = (
        item.reshape(1, atoms)
        for item in (brick_owner, plane_offset, row_offset, column_offset, chain_index)
    )
    message, slot = pl.pallas_call(
        functools.partial(pack_kernel, devices, sub, rows),
        out_shape=(shape_of(tiles * fields, lanes), shape_of(2, atoms, dtype=jnp.int32)),
        in_specs=whole(7),
        out_specs=whole(2),
        compiler_params=settings(),
        name="pack",
    )(owner, plane, row, column, chain, amplitude.reshape(1, atoms), fraction)
    message = exchange(message)

    own_shape = shape_of((planes + 3) * rows, columns)
    edge_shape = shape_of(3 * rows, columns)
    own, up, down = pl.pallas_call(
        functools.partial(density_kernel, devices, *grid, batch),
        out_shape=(own_shape, edge_shape, edge_shape),
        in_specs=scalar + whole(2),
        out_specs=whole(3),
        compiler_params=settings(),
        name="density",
    )(place, message, density_map)
    below, above = shift(up, 1), shift(down, -1)
    table = pltpu.VMEM((2 * (planes + 1) * rows, 2 * columns), bf16)
    moved, first, own, up, down = pl.pallas_call(
        functools.partial(middle_kernel, devices, *grid, batch),
        out_shape=(
            shape_of(tiles * fields, lanes),
            shape_of(tiles * fields, lanes),
            own_shape,
            edge_shape,
            edge_shape,
        ),
        in_specs=scalar + whole(5),
        out_specs=whole(5),
        scratch_shapes=[table],
        compiler_params=settings(),
        name="middle",
    )(place, message, own, below, above, density_map)
    below, above = shift(up, 1), shift(down, -1)
    reply = pl.pallas_call(
        functools.partial(last_kernel, devices, sub, *grid, batch),
        out_shape=shape_of(tiles * fields, lanes),
        in_specs=scalar + whole(6),
        out_specs=whole(1)[0],
        scratch_shapes=[table, pltpu.VMEM((devices, lanes), f32)],
        compiler_params=settings(),
        name="last",
    )(place, message, moved, first, own, below, above)
    reply = exchange(reply)
    torques, gradients = pl.pallas_call(
        functools.partial(chain_kernel, devices, sub, planes, columns),
        out_shape=(shape_of(2, atoms), shape_of(6, atoms)),
        in_specs=whole(10),
        out_specs=whole(2),
        compiler_params=settings(),
        name="chains",
    )(
        reply, slot, owner, plane, row, column, chain, chain_index.reshape(atoms // lanes, lanes),
        fraction, torsion_axis,
    )
    return torques, gradients


def solution(mesh):
    return jax.shard_map(
        shards,
        mesh=mesh,
        in_specs=(
            P(("grp", "bx"), None, None),
            P(("grp", "bx")),
            P(None, ("grp", "bx")),
            P(None, ("grp", "bx")),
            P(("grp", "bx"), None),
            P(("grp", "bx")),
            P(("grp", "bx")),
            P(("grp", "bx")),
            P(("grp", "bx")),
        ),
        out_specs=(P(None, ("grp", "bx")), P(None, ("grp", "bx"))),
        check_vma=False,
    )
```

```python
import functools

import jax
import jax.numpy as jnp
from jax import lax
from jax.experimental import pallas as pl
from jax.experimental.pallas import tpu as pltpu
from jax.sharding import PartitionSpec as P

side_tap = 0.25
middle_tap = 0.5
probe_step = 0.2
lanes = 128
fields = 8
f32, bf16 = jnp.float32, jnp.bfloat16
room = 48 * 1024 * 1024


def dot_nt(left, right):
    return lax.dot_general(left, right, (((1,), (1,)), ((), ())), preferred_element_type=f32)


def dot_nn(left, right):
    return lax.dot_general(left, right, (((1,), (0,)), ((), ())), preferred_element_type=f32)


def halves(x):
    high = x.astype(bf16)
    return high, (x - high.astype(f32)).astype(bf16)


def thirds(x):
    high, rest = x.astype(bf16), None
    rest = x - high.astype(f32)
    middle = rest.astype(bf16)
    return high, middle, (rest - middle.astype(f32)).astype(bf16)


def down_rows(count, width):
    return lax.broadcasted_iota(jnp.int32, (count, width), 0)


def spread(row, count):
    tile = jnp.broadcast_to(row, (16, row.shape[1])).astype(bf16)
    return jnp.concatenate([tile] * (count // 16), 0)


def counting(count, width):
    part = down_rows(count, lanes).astype(f32).astype(bf16)
    return jnp.concatenate([part] * (width // lanes), 1)


def pack_kernel(devices, sub, planes, rows, across, *refs):
    hbm, (message_ref, slot_ref, home_ref), held = refs[:8], refs[8:11], refs[11:19]
    semaphores = refs[19]
    copies = [
        pltpu.make_async_copy(source, target, semaphores.at[i])
        for i, (source, target) in enumerate(zip(hbm, held))
    ]
    for copy in copies:
        copy.start()
    for copy in copies:
        copy.wait()
    owner_ref, plane_ref, row_ref, column_ref, chain_ref, amp_ref, frac_ref, axis_ref = held
    atoms = owner_ref.shape[1]
    blocks = atoms // lanes
    tiles = devices * sub
    owner, plane = owner_ref[...], plane_ref[...]
    chain = chain_ref[...].astype(f32)
    home_ref[0:1, :] = (owner * planes + plane).astype(f32)
    owner = seat(owner, across)
    home_ref[1:2, :] = row_ref[...].astype(f32)
    home_ref[2:3, :] = column_ref[...].astype(f32)
    home_ref[3:6, :] = frac_ref[...]
    home_ref[6:7, :] = chain
    home_ref[7:10, :] = axis_ref[...]
    groups = planes * devices
    mine = down_rows(groups, atoms) == plane * devices + owner
    onehot = jnp.where(mine, 1.0, 0.0)
    stacked = jnp.concatenate(
        [onehot[:, j * lanes : (j + 1) * lanes] for j in range(blocks)], 0
    ).astype(bf16)
    k = lax.broadcasted_iota(jnp.int32, (lanes, 2 * lanes), 0)
    a = lax.broadcasted_iota(jnp.int32, (lanes, 2 * lanes), 1)
    before = jnp.where((k < a) | (a >= lanes), 1.0, 0.0).astype(bf16)
    counts = dot_nn(stacked, before)
    parts = [counts[j * groups : (j + 1) * groups] for j in range(blocks)]
    total = parts[0][:, lanes:]
    for part in parts[1:]:
        total = total + part[:, lanes:]
    held_by = [total[p * devices : (p + 1) * devices] for p in range(planes)]
    half = planes // 2
    none = jnp.zeros((devices, lanes), f32)
    offsets = [sum(held_by[:p], none) for p in range(half)]
    offsets += [sum(held_by[p + 1 :], none) for p in range(half, planes)]
    running = jnp.concatenate(offsets, 0)
    ranks = []
    for j, part in enumerate(parts):
        here = onehot[:, j * lanes : (j + 1) * lanes]
        ranks.append(jnp.sum((part[:, :lanes] + running) * here, 0, keepdims=True))
        running = running + part[:, lanes:]
    rank = jnp.concatenate(ranks, 1).astype(jnp.int32)
    rank = jnp.where(plane < half, rank, sub * lanes - 1 - rank)
    tile = owner * sub + lax.shift_right_logical(rank, 7)
    lane = rank & (lanes - 1)
    slot_ref[...] = jnp.concatenate([tile, lane], 0)
    values = jnp.concatenate(
        [
            (plane * rows + row_ref[...]).astype(f32),
            column_ref[...].astype(f32),
            frac_ref[...],
            amp_ref[...],
            chain,
            jnp.zeros((1, atoms), f32),
        ],
        0,
    )
    pieces = [piece.astype(f32) for piece in thirds(values)]
    width = 512
    for c in range(atoms // width):
        at = slice(c * width, (c + 1) * width)
        spot = jnp.where(down_rows(lanes, width) == lane[:, at], 1.0, 0.0).astype(bf16)
        which = jnp.broadcast_to(tile[:, at], (fields, width))
        picks = [which == t for t in range(tiles)]
        total = None
        for piece in pieces:
            part = piece[:, at]
            left = jnp.concatenate([jnp.where(pick, part, 0.0) for pick in picks], 0).astype(bf16)
            one = dot_nt(left, spot)
            total = one if total is None else total + one
        if c == 0:
            message_ref[...] = total
        else:
            message_ref[...] += total
    last = jnp.broadcast_to(chain[:, atoms - 1 :], (1, lanes))
    for b in range(devices):
        message_ref[b * sub * fields + fields - 1 : b * sub * fields + fields, :] = last
    if sorted_buckets(planes, sub):
        fits = 1.0
        lower, upper = held_by[0] + held_by[1], held_by[2] + held_by[3]
        limits = (lower, 2.0 * lanes), (upper, 2.0 * lanes), (held_by[0], lanes), (held_by[3], lanes)
        for amount, limit in limits:
            fits = fits * jnp.where(amount <= limit, 1.0, 0.0)
        for b in range(devices):
            row = (b * sub + 1) * fields + fields - 1
            message_ref[row : row + 1, :] = fits[b : b + 1]


def sorted_buckets(planes, sub):
    return planes == 4 and sub == 3


def neighbours_of(state, rows, columns):
    cell, column = state[0:1], state[1:2]
    plane = jnp.floor(cell * (1.0 / rows))
    row = cell - plane * rows
    next_row = jnp.where(row == rows - 1.0, 0.0, row + 1.0)
    next_column = jnp.where(column == columns - 1.0, 0.0, column + 1.0)
    return plane, row, next_row, column, next_column


def density_part(state, base, span, rows, columns):
    width = state.shape[1]
    plane, row, next_row, column, next_column = neighbours_of(state, rows, columns)
    fx, fy, fz, amplitude = (state[2 + i : 3 + i] for i in range(4))
    zero = jnp.zeros((), bf16)
    steps = counting(columns, width)
    here, there = steps == spread(column, columns), steps == spread(next_column, columns)

    def columns_of(near, far):
        return jnp.where(here, spread(near, columns), jnp.where(there, spread(far, columns), zero))

    near, far = halves(1.0 - fz), halves(fz)
    right_high = columns_of(near[0].astype(f32), far[0].astype(f32))
    right_low = columns_of(near[1].astype(f32), far[1].astype(f32))
    level = down_rows(fields, width).astype(f32) + float(base)
    along = amplitude * jnp.where(level == plane, 1.0 - fx, jnp.where(level == plane + 1.0, fx, 0.0))
    near, far = halves(along * (1.0 - fy)), halves(along * fy)
    steps = counting(rows, width)
    here, there = steps == spread(row, rows), steps == spread(next_row, rows)
    lefts = []
    for grade in range(2):
        first, second = near[grade].astype(f32), far[grade].astype(f32)
        lefts.append(
            jnp.concatenate(
                [
                    jnp.where(
                        here,
                        spread(first[p : p + 1], rows),
                        jnp.where(there, spread(second[p : p + 1], rows), zero),
                    )
                    for p in range(span + 1)
                ],
                0,
            )
        )
    return (
        dot_nt(lefts[0], right_high) + dot_nt(lefts[0], right_low) + dot_nt(lefts[1], right_high)
    )


def gradient_part(state, table_ref, base, span, planes, rows, columns):
    width = state.shape[1]
    plane, row, next_row, column, _ = neighbours_of(state, rows, columns)
    fx, fy, fz, amplitude = (state[2 + i : 3 + i] for i in range(4))
    spot = jnp.where(
        counting(columns, width) == spread(column, columns),
        jnp.ones((), bf16),
        jnp.zeros((), bf16),
    )
    table = jnp.concatenate(
        [
            table_ref[(e2 * (planes + 1) + base) * rows : (e2 * (planes + 1) + base + span + 1) * rows, :]
            for e2 in range(2)
        ],
        0,
    )
    sampled = dot_nn(table, jnp.concatenate([spot, spot], 0))
    sheets = [sampled[i * rows : (i + 1) * rows] for i in range(2 * (span + 1))]
    steps = down_rows(rows, width).astype(f32)
    at_plane = [jnp.broadcast_to(plane, (rows, width)) == float(base + p) for p in range(span)]
    at_row = (steps == row, steps == next_row)
    corner = {}
    for e2 in range(2):
        for e0 in range(2):
            chosen = sheets[e2 * (span + 1) + e0]
            for p in range(1, span):
                chosen = jnp.where(at_plane[p], sheets[e2 * (span + 1) + e0 + p], chosen)
            for e1 in range(2):
                corner[e0, e1, e2] = jnp.sum(jnp.where(at_row[e1], chosen, 0.0), 0, keepdims=True)
    wx, wy, wz = (1.0 - fx, fx), (1.0 - fy, fy), (1.0 - fz, fz)
    gx = gy = gz = 0.0
    for u in range(2):
        for v in range(2):
            gx = gx + wy[u] * wz[v] * (corner[1, u, v] - corner[0, u, v])
            gy = gy + wx[u] * wz[v] * (corner[u, 1, v] - corner[u, 0, v])
            gz = gz + wx[u] * wy[v] * (corner[u, v, 1] - corner[u, v, 0])
    return jnp.concatenate([amplitude * gx, amplitude * gy, amplitude * gz], 0)


def blur_sheet(sheet):
    rows, columns = sheet.shape
    sheet = middle_tap * sheet + side_tap * (pltpu.roll(sheet, 1, 0) + pltpu.roll(sheet, rows - 1, 0))
    return middle_tap * sheet + side_tap * (
        pltpu.roll(sheet, 1, 1) + pltpu.roll(sheet, columns - 1, 1)
    )


def blur_along(sheets):
    return [
        middle_tap * sheets[i] + side_tap * (sheets[i - 1] + sheets[i + 1])
        for i in range(1, len(sheets) - 1)
    ]


def edges(place_ref, devices):
    not_first = jnp.where(place_ref[0] == 0, 0.0, 1.0)
    not_last = jnp.where(place_ref[0] == devices - 1, 0.0, 1.0)
    return not_first, not_last


def share_misfit(place_ref, devices, planes, rows, density, map_ref, own_ref, near_ref, far_ref):
    _, not_last = edges(place_ref, devices)
    density[planes] = density[planes] * not_last
    zero = jnp.zeros_like(density[0])
    parts = [blur_sheet(sheet) for sheet in blur_along([zero, zero] + density + [zero, zero])]
    for p in range(planes):
        parts[p + 1] = parts[p + 1] - map_ref[p]
    for p in range(planes + 3):
        own_ref[p * rows : (p + 1) * rows, :] = parts[p]
    even = place_ref[0] % 2 == 0
    for p in range(3):
        up, down = parts[planes + p], parts[p]
        near_ref[p * rows : (p + 1) * rows, :] = jnp.where(even, up, down)
        far_ref[p * rows : (p + 1) * rows, :] = jnp.where(even, down, up)


def make_table(place_ref, devices, planes, rows, columns, own_ref, near_ref, far_ref, table_ref):
    not_first, not_last = edges(place_ref, devices)
    misfit = [own_ref[p * rows : (p + 1) * rows, :] for p in range(planes + 3)]
    even = place_ref[0] % 2 == 0
    for p in range(3):
        near = near_ref[p * rows : (p + 1) * rows, :]
        far = far_ref[p * rows : (p + 1) * rows, :]
        misfit[p] = misfit[p] + jnp.where(even, far, near)
        misfit[planes + p] = misfit[planes + p] + jnp.where(even, near, far)
    misfit[0] = misfit[0] * not_first
    misfit[planes + 1] = misfit[planes + 1] * not_last
    misfit[planes + 2] = misfit[planes + 2] * not_last
    pulled = [blur_sheet(sheet) for sheet in blur_along(misfit)]
    pulled[planes] = pulled[planes] * not_last
    for p in range(planes + 1):
        shifted = pltpu.roll(pulled[p], columns - 1, 1)
        for turn, sheet in enumerate((pulled[p], shifted)):
            high, low = halves(sheet)
            at = slice((turn * (planes + 1) + p) * rows, (turn * (planes + 1) + p + 1) * rows)
            table_ref[at, :columns] = high
            table_ref[at, columns:] = low


def load_tiles(ref, tiles):
    return jnp.concatenate([ref[t * fields : (t + 1) * fields, :] for t in tiles], 1)


def store_tiles(ref, tiles, value):
    for i, t in enumerate(tiles):
        ref[t * fields : (t + 1) * fields, :] = value[:, i * lanes : (i + 1) * lanes]


def chunks(devices, sub, planes, ordered):
    if ordered:
        return [([b * sub + k for b in range(devices)], k, 2) for k in range(sub)]
    tiles = devices * sub
    batch = max(b for b in range(1, 25) if tiles % b == 0)
    return [(range(i, i + batch), 0, planes) for i in range(0, tiles, batch)]


def in_order(message_ref, devices, sub):
    rows = [(b * sub + 1) * fields + fields - 1 for b in range(devices)]
    flags = jnp.concatenate([message_ref[row : row + 1, :] for row in rows], 0)
    return jnp.min(flags) > 0.5


def either(ordered_ref, planes, sub, work):
    if not sorted_buckets(planes, sub):
        work(False)
        return
    ordered = ordered_ref[0] == 1

    @pl.when(ordered)
    def _():
        work(True)

    @pl.when(jnp.logical_not(ordered))
    def _():
        work(False)


def all_density(state_ref, devices, sub, planes, rows, columns, ordered):
    sheets = [None] * (planes + 1)
    for tiles, base, span in chunks(devices, sub, planes, ordered):
        part = density_part(load_tiles(state_ref, tiles), base, span, rows, columns)
        for p in range(span + 1):
            sheet = part[p * rows : (p + 1) * rows]
            sheets[base + p] = sheet if sheets[base + p] is None else sheets[base + p] + sheet
    return sheets


def density_kernel(
    devices, sub, planes, rows, columns, place_ref, message_ref, map_ref, own_ref, near_ref, far_ref,
    ordered_ref,
):
    if sorted_buckets(planes, sub):
        ordered_ref[0] = jnp.where(in_order(message_ref, devices, sub), 1, 0)
    else:
        ordered_ref[0] = 0

    def work(ordered):
        sheets = all_density(message_ref, devices, sub, planes, rows, columns, ordered)
        share_misfit(place_ref, devices, planes, rows, sheets, map_ref, own_ref, near_ref, far_ref)

    either(ordered_ref, planes, sub, work)


def middle_kernel(
    devices, sub, planes, rows, columns, place_ref, ordered_ref, message_ref, was_ref, from_near_ref,
    from_far_ref, map_ref, moved_ref, first_ref, own_ref, near_ref, far_ref, table_ref,
):
    make_table(
        place_ref, devices, planes, rows, columns, was_ref, from_near_ref, from_far_ref, table_ref
    )

    def work(ordered):
        for tiles, base, span in chunks(devices, sub, planes, ordered):
            state = load_tiles(message_ref, tiles)
            gradient = gradient_part(state, table_ref, base, span, planes, rows, columns)
            moved = jnp.concatenate(
                [state[0:2], state[2:5] - probe_step * jnp.tanh(gradient), state[5:8]], 0
            )
            store_tiles(moved_ref, tiles, moved)
            store_tiles(
                first_ref, tiles,
                jnp.concatenate([gradient, jnp.zeros((5, gradient.shape[1]), f32)], 0),
            )
        sheets = all_density(moved_ref, devices, sub, planes, rows, columns, ordered)
        share_misfit(place_ref, devices, planes, rows, sheets, map_ref, own_ref, near_ref, far_ref)

    either(ordered_ref, planes, sub, work)


def cross_list(left, right):
    return [
        left[1] * right[2] - left[2] * right[1],
        left[2] * right[0] - left[0] * right[2],
        left[0] * right[1] - left[1] * right[0],
    ]


def last_kernel(
    devices, sub, planes, rows, columns, place_ref, ordered_ref, message_ref, moved_ref, first_ref,
    was_ref, from_near_ref, from_far_ref, reply_ref, table_ref,
):
    make_table(
        place_ref, devices, planes, rows, columns, was_ref, from_near_ref, from_far_ref, table_ref
    )
    last_of = jnp.concatenate(
        [
            message_ref[d * sub * fields + fields - 1 : d * sub * fields + fields, :]
            for d in range(devices)
        ],
        0,
    )
    slab_plane = (place_ref[0] * planes).astype(f32)

    def work(ordered):
        sums = jnp.zeros((devices, 16), f32)
        for tiles, base, span in chunks(devices, sub, planes, ordered):
            state = load_tiles(message_ref, tiles)
            moved = load_tiles(moved_ref, tiles)
            first = load_tiles(first_ref, tiles)[0:3]
            second = gradient_part(moved, table_ref, base, span, planes, rows, columns)
            width = state.shape[1]
            plane, row, _, column, _ = neighbours_of(state, rows, columns)
            cells = (plane + slab_plane, row, column)
            pieces = []
            for gradient, offset in ((first, state), (second, moved)):
                g = [gradient[d : d + 1] for d in range(3)]
                pieces += g + cross_list([cells[d] + offset[2 + d : 3 + d] for d in range(3)], g)
            pieces.append(jnp.where(state[5:6] > 0.0, 1.0, 0.0))
            pieces.append(jnp.zeros((3, width), f32))
            block = jnp.concatenate(pieces, 0)
            receiver = down_rows(devices, lanes)
            chosen = jnp.concatenate(
                [
                    jnp.where(
                        (receiver < t // sub)
                        & (last_of == state[6:7, i * lanes : (i + 1) * lanes]),
                        1.0,
                        0.0,
                    )
                    for i, t in enumerate(tiles)
                ],
                1,
            ).astype(bf16)
            sums = sums + sum(dot_nt(chosen, piece) for piece in thirds(block))
            store_tiles(
                reply_ref, tiles,
                jnp.concatenate([first, second, jnp.zeros((2, width), f32)], 0),
            )
        sums = jnp.concatenate([sums, jnp.zeros((devices, lanes - 16), f32)], 1)
        for d in range(devices):
            reply_ref[d * sub * fields + fields - 1 : d * sub * fields + fields, :] = sums[d : d + 1]

    either(ordered_ref, planes, sub, work)


def chain_kernel(
    devices, sub, planes, columns, reply_ref, slot_ref, home_ref, torque_ref, gradient_ref
):
    atoms = slot_ref.shape[1]
    blocks = atoms // lanes
    tiles = devices * sub
    high, low = halves(reply_ref[...])
    left = jnp.concatenate([high, low], 1)
    width = 512
    found = []
    for c in range(atoms // width):
        at = slice(c * width, (c + 1) * width)
        spot = jnp.where(down_rows(lanes, width) == slot_ref[1:2, at], 1.0, 0.0).astype(bf16)
        picked = dot_nn(left, jnp.concatenate([spot, spot], 0))
        which = jnp.broadcast_to(slot_ref[0:1, at], (fields, width))
        total = jnp.zeros((fields, width), f32)
        for t in range(tiles):
            total = jnp.where(which == t, picked[t * fields : (t + 1) * fields], total)
        found.append(total)
    gradients = jnp.concatenate(found, 1)[0:6]
    gradient_ref[...] = gradients
    fraction = home_ref[3:6, :]
    moved = fraction - probe_step * jnp.tanh(gradients[0:3])
    base = [home_ref[d : d + 1, :] for d in range(3)]
    axis = [home_ref[7 + d : 8 + d, :] for d in range(3)]
    positions = [[base[d] + offset[d : d + 1] for d in range(3)] for offset in (fraction, moved)]
    pieces = []
    for e in range(2):
        g = [gradients[3 * e + d : 3 * e + d + 1] for d in range(3)]
        pieces += g + cross_list(positions[e], g)
    pieces.append(jnp.ones((1, atoms), f32))
    pieces.append(jnp.zeros((3, atoms), f32))
    stacked = jnp.concatenate(thirds(jnp.concatenate(pieces, 0)), 0)

    def joined(x):
        return x[0:16] + x[16:32] + x[32:48]

    chain = home_ref[6:7, :]
    chain_rows = jnp.concatenate([chain[:, j * lanes : (j + 1) * lanes] for j in range(blocks)], 0)
    ends = jnp.broadcast_to(chain_rows[:, lanes - 1 :], (blocks, atoms))
    later = lax.broadcasted_iota(jnp.int32, (blocks, atoms), 1) >= lanes * (
        down_rows(blocks, atoms) + 1
    )
    bridge = jnp.where(later & (ends == chain), 1.0, 0.0).astype(bf16)
    carries = joined(dot_nt(stacked, bridge))
    arrived = jnp.zeros((1, lanes), f32)
    for d in range(devices):
        arrived = arrived + reply_ref[d * sub * fields + fields - 1 : d * sub * fields + fields, :]
    diagonal = down_rows(16, lanes) == lax.broadcasted_iota(jnp.int32, (16, lanes), 1)
    arrived = jnp.sum(jnp.where(diagonal, arrived, 0.0), 1, keepdims=True)
    padded = jnp.concatenate([chain_rows, jnp.zeros((lanes - blocks, lanes), f32)], 0)
    down_chain = jnp.transpose(padded)
    not_before = down_rows(lanes, lanes) >= lax.broadcasted_iota(jnp.int32, (lanes, lanes), 1)
    closing = chain[:, atoms - 1 :]
    sums = []
    for j in range(blocks):
        at = slice(j * lanes, (j + 1) * lanes)
        mask = not_before & (down_chain[:, j : j + 1] == chain[:, at])
        local = joined(dot_nn(stacked[:, at], jnp.where(mask, 1.0, 0.0).astype(bf16)))
        end = chain[:, (j + 1) * lanes - 1 : (j + 1) * lanes]
        carry = carries[:, j : j + 1] + jnp.where(end == closing, arrived, 0.0)
        sums.append(local + jnp.where(chain[:, at] == end, carry, 0.0))
    totals = jnp.concatenate(sums, 1)
    scale = 1.0 / (columns * jnp.sqrt(totals[12:13]))
    torques = []
    for e in range(2):
        force = [totals[6 * e + d : 6 * e + d + 1] for d in range(3)]
        lever = cross_list(positions[e], force)
        turn = 0.0
        for d in range(3):
            turn = turn + axis[d] * (totals[6 * e + 3 + d : 6 * e + 4 + d] - lever[d])
        torques.append(turn * scale)
    torque_ref[...] = jnp.concatenate(torques, 0)


def whole(count):
    return [pl.BlockSpec(memory_space=pltpu.VMEM)] * count


def settings():
    return pltpu.CompilerParams(vmem_limit_bytes=room)


def shape_of(*dims, dtype=f32):
    return jax.ShapeDtypeStruct(dims, dtype)


def seat(slab, across):
    turned = (slab // (2 * across)) % 2
    return slab ^ (turned * (2 * across - 2))


def seats_across(mesh):
    devices = mesh.devices[0]
    count = len(devices)
    if not all(hasattr(device, "coords") for device in devices):
        return count
    across = len({device.coords[0] for device in devices})
    if across & (across - 1) or count % (4 * across):
        return count
    first = devices[0].coords
    for i, device in enumerate(devices):
        x, z = i // 2 % across, i // (2 * across)
        if device.coords[0] - first[0] != x or device.coords[2] - first[2] != z:
            return count
    return across


def swap_near(value, across):
    count = lax.axis_size("bx")
    pairs = [(seat(i, across), seat(i ^ 1, across)) for i in range(count)]
    return lax.ppermute(value, "bx", pairs)


def swap_far(value, across):
    count = lax.axis_size("bx")
    pairs = []
    for i in range(1, count - 1, 2):
        pairs += [(seat(i, across), seat(i + 1, across)), (seat(i + 1, across), seat(i, across))]
    return lax.ppermute(value, "bx", pairs)


def exchange(value):
    return lax.all_to_all(value, "bx", split_axis=0, concat_axis=0, tiled=True)


def shards(
    across,
    density_map,
    amplitude,
    fraction,
    torsion_axis,
    brick_owner,
    plane_offset,
    row_offset,
    column_offset,
    chain_index,
):
    planes, rows, columns = density_map.shape
    atoms = amplitude.shape[0]
    devices = lax.axis_size("bx")
    capacity = 3 * atoms // devices
    sub = -(-capacity // lanes)
    tiles = devices * sub
    grid = (planes, rows, columns)
    place = seat(lax.axis_index("bx").astype(jnp.int32), across).reshape(1)
    moves = [(i, seat(i, across)) for i in range(devices)]
    if any(i != j for i, j in moves):
        density_map = lax.ppermute(density_map, "bx", moves)
    scalar = [pl.BlockSpec(memory_space=pltpu.SMEM)]

    owner, plane, row, column, chain = (
        item.reshape(1, atoms)
        for item in (brick_owner, plane_offset, row_offset, column_offset, chain_index)
    )
    held = [pltpu.VMEM((1, atoms), jnp.int32)] * 5
    held += [pltpu.VMEM((1, atoms), f32)] + [pltpu.VMEM((3, atoms), f32)] * 2
    message, slot, home = pl.pallas_call(
        functools.partial(pack_kernel, devices, sub, planes, rows, across),
        out_shape=(
            shape_of(tiles * fields, lanes),
            shape_of(2, atoms, dtype=jnp.int32),
            shape_of(10, atoms),
        ),
        in_specs=[pl.BlockSpec(memory_space=pltpu.HBM)] * 8,
        out_specs=whole(3),
        scratch_shapes=held + [pltpu.SemaphoreType.DMA((8,))],
        name="pack",
    )(owner, plane, row, column, chain, amplitude.reshape(1, atoms), fraction, torsion_axis)
    message = exchange(message)

    own_shape = shape_of((planes + 3) * rows, columns)
    edge_shape = shape_of(3 * rows, columns)
    own, near, far, ordered = pl.pallas_call(
        functools.partial(density_kernel, devices, sub, *grid),
        out_shape=(own_shape, edge_shape, edge_shape, shape_of(1, dtype=jnp.int32)),
        in_specs=scalar + whole(2),
        out_specs=whole(3) + scalar,
        compiler_params=settings(),
        name="density",
    )(place, message, density_map)
    near, far = swap_near(near, across), swap_far(far, across)
    table = pltpu.VMEM((2 * (planes + 1) * rows, 2 * columns), bf16)
    moved, first, own, near, far = pl.pallas_call(
        functools.partial(middle_kernel, devices, sub, *grid),
        out_shape=(
            shape_of(tiles * fields, lanes),
            shape_of(tiles * fields, lanes),
            own_shape,
            edge_shape,
            edge_shape,
        ),
        in_specs=scalar * 2 + whole(5),
        out_specs=whole(5),
        scratch_shapes=[table],
        compiler_params=settings(),
        name="middle",
    )(place, ordered, message, own, near, far, density_map)
    near, far = swap_near(near, across), swap_far(far, across)
    reply = pl.pallas_call(
        functools.partial(last_kernel, devices, sub, *grid),
        out_shape=shape_of(tiles * fields, lanes),
        in_specs=scalar * 2 + whole(6),
        out_specs=whole(1)[0],
        scratch_shapes=[table],
        compiler_params=settings(),
        name="last",
    )(place, ordered, message, moved, first, own, near, far)
    reply = exchange(reply)
    torques, gradients = pl.pallas_call(
        functools.partial(chain_kernel, devices, sub, planes, columns),
        out_shape=(shape_of(2, atoms), shape_of(6, atoms)),
        in_specs=whole(3),
        out_specs=whole(2),
        compiler_params=settings(),
        name="chains",
    )(reply, slot, home)
    return torques, gradients


def solution(mesh):
    return jax.shard_map(
        functools.partial(shards, seats_across(mesh)),
        mesh=mesh,
        in_specs=(
            P(("grp", "bx"), None, None),
            P(("grp", "bx")),
            P(None, ("grp", "bx")),
            P(None, ("grp", "bx")),
            P(("grp", "bx"), None),
            P(("grp", "bx")),
            P(("grp", "bx")),
            P(("grp", "bx")),
            P(("grp", "bx")),
        ),
        out_specs=(P(None, ("grp", "bx")), P(None, ("grp", "bx"))),
        check_vma=False,
    )
```

```python
import functools

import jax
import jax.numpy as jnp
from jax import lax
from jax.experimental import pallas as pl
from jax.experimental.pallas import tpu as pltpu
from jax.sharding import PartitionSpec as P

side_tap = 0.25
middle_tap = 0.5
probe_step = 0.2
lanes = 128
fields = 8
f32, bf16 = jnp.float32, jnp.bfloat16
room = 48 * 1024 * 1024


def dot_nt(left, right):
    return lax.dot_general(left, right, (((1,), (1,)), ((), ())), preferred_element_type=f32)


def dot_nn(left, right):
    return lax.dot_general(left, right, (((1,), (0,)), ((), ())), preferred_element_type=f32)


def halves(x):
    high = x.astype(bf16)
    return high, (x - high.astype(f32)).astype(bf16)


def thirds(x):
    high, rest = x.astype(bf16), None
    rest = x - high.astype(f32)
    middle = rest.astype(bf16)
    return high, middle, (rest - middle.astype(f32)).astype(bf16)


def down_rows(count, width):
    return lax.broadcasted_iota(jnp.int32, (count, width), 0)


def spread(row, count):
    tile = jnp.broadcast_to(row, (16, row.shape[1])).astype(bf16)
    return jnp.concatenate([tile] * (count // 16), 0)


def counting(count, width):
    part = down_rows(count, lanes).astype(f32).astype(bf16)
    return jnp.concatenate([part] * (width // lanes), 1)


def pack_kernel(devices, sub, planes, rows, across, *refs):
    hbm, (message_ref, slot_ref, home_ref), held = refs[:8], refs[8:11], refs[11:19]
    semaphores = refs[19]
    copies = [
        pltpu.make_async_copy(source, target, semaphores.at[i])
        for i, (source, target) in enumerate(zip(hbm, held))
    ]
    for copy in copies:
        copy.start()
    for copy in copies:
        copy.wait()
    owner_ref, plane_ref, row_ref, column_ref, chain_ref, amp_ref, frac_ref, axis_ref = held
    atoms = owner_ref.shape[1]
    blocks = atoms // lanes
    tiles = devices * sub
    owner, plane = owner_ref[...], plane_ref[...]
    chain = chain_ref[...].astype(f32)
    home_ref[0:1, :] = (owner * planes + plane).astype(f32)
    owner = seat(owner, across)
    home_ref[1:2, :] = row_ref[...].astype(f32)
    home_ref[2:3, :] = column_ref[...].astype(f32)
    home_ref[3:6, :] = frac_ref[...]
    home_ref[6:7, :] = chain
    home_ref[7:10, :] = axis_ref[...]
    groups = planes * devices
    mine = down_rows(groups, atoms) == plane * devices + owner
    onehot = jnp.where(mine, 1.0, 0.0)
    stacked = jnp.concatenate(
        [onehot[:, j * lanes : (j + 1) * lanes] for j in range(blocks)], 0
    ).astype(bf16)
    k = lax.broadcasted_iota(jnp.int32, (lanes, 2 * lanes), 0)
    a = lax.broadcasted_iota(jnp.int32, (lanes, 2 * lanes), 1)
    before = jnp.where((k < a) | (a >= lanes), 1.0, 0.0).astype(bf16)
    counts = dot_nn(stacked, before)
    parts = [counts[j * groups : (j + 1) * groups] for j in range(blocks)]
    total = parts[0][:, lanes:]
    for part in parts[1:]:
        total = total + part[:, lanes:]
    held_by = [total[p * devices : (p + 1) * devices] for p in range(planes)]
    half = planes // 2
    none = jnp.zeros((devices, lanes), f32)
    offsets = [sum(held_by[:p], none) for p in range(half)]
    offsets += [sum(held_by[p + 1 :], none) for p in range(half, planes)]
    running = jnp.concatenate(offsets, 0)
    ranks = []
    for j, part in enumerate(parts):
        here = onehot[:, j * lanes : (j + 1) * lanes]
        ranks.append(jnp.sum((part[:, :lanes] + running) * here, 0, keepdims=True))
        running = running + part[:, lanes:]
    rank = jnp.concatenate(ranks, 1).astype(jnp.int32)
    rank = jnp.where(plane < half, rank, sub * lanes - 1 - rank)
    tile = owner * sub + lax.shift_right_logical(rank, 7)
    lane = rank & (lanes - 1)
    slot_ref[...] = jnp.concatenate([tile, lane], 0)
    values = jnp.concatenate(
        [
            (plane * rows + row_ref[...]).astype(f32),
            column_ref[...].astype(f32),
            frac_ref[...],
            amp_ref[...],
            chain,
            jnp.zeros((1, atoms), f32),
        ],
        0,
    )
    pieces = [piece.astype(f32) for piece in halves(values)]
    width = 512
    for c in range(atoms // width):
        at = slice(c * width, (c + 1) * width)
        spot = jnp.where(down_rows(lanes, width) == lane[:, at], 1.0, 0.0).astype(bf16)
        which = jnp.broadcast_to(tile[:, at], (fields, width))
        picks = [which == t for t in range(tiles)]
        total = None
        for piece in pieces:
            part = piece[:, at]
            left = jnp.concatenate([jnp.where(pick, part, 0.0) for pick in picks], 0).astype(bf16)
            one = dot_nt(left, spot)
            total = one if total is None else total + one
        if c == 0:
            message_ref[...] = total
        else:
            message_ref[...] += total
    last = jnp.broadcast_to(chain[:, atoms - 1 :], (1, lanes))
    for b in range(devices):
        message_ref[b * sub * fields + fields - 1 : b * sub * fields + fields, :] = last
    if sorted_buckets(planes, sub):
        fits = 1.0
        lower, upper = held_by[0] + held_by[1], held_by[2] + held_by[3]
        limits = (lower, 2.0 * lanes), (upper, 2.0 * lanes), (held_by[0], lanes), (held_by[3], lanes)
        for amount, limit in limits:
            fits = fits * jnp.where(amount <= limit, 1.0, 0.0)
        for b in range(devices):
            row = (b * sub + 1) * fields + fields - 1
            message_ref[row : row + 1, :] = fits[b : b + 1]


def sorted_buckets(planes, sub):
    return planes == 4 and sub == 3


def neighbours_of(state, rows, columns):
    cell, column = state[0:1], state[1:2]
    plane = jnp.floor(cell * (1.0 / rows))
    row = cell - plane * rows
    next_row = jnp.where(row == rows - 1.0, 0.0, row + 1.0)
    next_column = jnp.where(column == columns - 1.0, 0.0, column + 1.0)
    return plane, row, next_row, column, next_column


def density_part(state, base, span, rows, columns):
    width = state.shape[1]
    plane, row, next_row, column, next_column = neighbours_of(state, rows, columns)
    fx, fy, fz, amplitude = (state[2 + i : 3 + i] for i in range(4))
    zero = jnp.zeros((), bf16)
    steps = counting(columns, width)
    here, there = steps == spread(column, columns), steps == spread(next_column, columns)

    def columns_of(near, far):
        return jnp.where(here, spread(near, columns), jnp.where(there, spread(far, columns), zero))

    near, far = halves(1.0 - fz), halves(fz)
    right_high = columns_of(near[0].astype(f32), far[0].astype(f32))
    right_low = columns_of(near[1].astype(f32), far[1].astype(f32))
    level = down_rows(fields, width).astype(f32) + float(base)
    along = amplitude * jnp.where(level == plane, 1.0 - fx, jnp.where(level == plane + 1.0, fx, 0.0))
    near, far = halves(along * (1.0 - fy)), halves(along * fy)
    steps = counting(rows, width)
    here, there = steps == spread(row, rows), steps == spread(next_row, rows)
    lefts = []
    for grade in range(2):
        first, second = near[grade].astype(f32), far[grade].astype(f32)
        lefts.append(
            jnp.concatenate(
                [
                    jnp.where(
                        here,
                        spread(first[p : p + 1], rows),
                        jnp.where(there, spread(second[p : p + 1], rows), zero),
                    )
                    for p in range(span + 1)
                ],
                0,
            )
        )
    both = dot_nt(jnp.concatenate(lefts, 0), right_high)
    count = lefts[0].shape[0]
    return both[:count] + both[count:] + dot_nt(lefts[0], right_low)


def gradient_part(state, table_ref, base, span, planes, rows, columns):
    width = state.shape[1]
    plane, row, next_row, column, _ = neighbours_of(state, rows, columns)
    fx, fy, fz, amplitude = (state[2 + i : 3 + i] for i in range(4))
    spot = jnp.where(
        counting(columns, width) == spread(column, columns),
        jnp.ones((), bf16),
        jnp.zeros((), bf16),
    )
    table = jnp.concatenate(
        [
            table_ref[(e2 * (planes + 1) + base) * rows : (e2 * (planes + 1) + base + span + 1) * rows, :]
            for e2 in range(2)
        ],
        0,
    )
    sampled = dot_nn(table, jnp.concatenate([spot, spot], 0))

    def eight(x):
        return jnp.broadcast_to(x, (8, width))

    level = down_rows(8, width).astype(f32)
    at_plane = [eight(plane) == float(base + p) for p in range(span)]
    eighths = [jnp.floor(at * 0.125) for at in (row, next_row)]
    at_eighth = [[eight(part) == float(j) for j in range(rows // 8)] for part in eighths]
    corner = {}
    for e2 in range(2):
        for e0 in range(2):
            chosen = []
            for j in range(rows // 8):
                at = (e2 * (span + 1) + e0) * rows + 8 * j
                pick = sampled[at : at + 8]
                for p in range(1, span):
                    pick = jnp.where(at_plane[p], sampled[at + p * rows : at + p * rows + 8], pick)
                chosen.append(pick)
            for e1 in range(2):
                pick = chosen[0]
                for j in range(1, rows // 8):
                    pick = jnp.where(at_eighth[e1][j], chosen[j], pick)
                corner[e0, e1, e2] = pick
    fx, fz = eight(fx), eight(fz)
    weights = (amplitude * (1.0 - fy), amplitude * fy)
    gx = gy = gz = 0.0
    for e1 in range(2):
        here = level == eight((row, next_row)[e1] - 8.0 * eighths[e1])
        weight = jnp.where(here, eight(weights[e1]), 0.0)
        signed = jnp.where(here, eight(amplitude), 0.0)
        drop = [corner[e0, e1, 1] - corner[e0, e1, 0] for e0 in range(2)]
        value = [corner[e0, e1, 0] + fz * drop[e0] for e0 in range(2)]
        slope = value[1] - value[0]
        gx = gx + weight * slope
        gz = gz + weight * (drop[0] + fx * (drop[1] - drop[0]))
        middle = signed * (value[0] + fx * slope)
        gy = gy + middle if e1 else gy - middle
    return jnp.concatenate([jnp.sum(g, 0, keepdims=True) for g in (gx, gy, gz)], 0)


def blur_sheet(sheet):
    rows, columns = sheet.shape
    sheet = middle_tap * sheet + side_tap * (pltpu.roll(sheet, 1, 0) + pltpu.roll(sheet, rows - 1, 0))
    return middle_tap * sheet + side_tap * (
        pltpu.roll(sheet, 1, 1) + pltpu.roll(sheet, columns - 1, 1)
    )


def blur_along(sheets):
    return [
        middle_tap * sheets[i] + side_tap * (sheets[i - 1] + sheets[i + 1])
        for i in range(1, len(sheets) - 1)
    ]


def edges(place_ref, devices):
    not_first = jnp.where(place_ref[0] == 0, 0.0, 1.0)
    not_last = jnp.where(place_ref[0] == devices - 1, 0.0, 1.0)
    return not_first, not_last


def share_misfit(place_ref, devices, planes, rows, density, map_ref, own_ref, near_ref, far_ref):
    _, not_last = edges(place_ref, devices)
    density[planes] = density[planes] * not_last
    zero = jnp.zeros_like(density[0])
    parts = [blur_sheet(sheet) for sheet in blur_along([zero, zero] + density + [zero, zero])]
    for p in range(planes):
        parts[p + 1] = parts[p + 1] - map_ref[p]
    for p in range(planes + 3):
        own_ref[p * rows : (p + 1) * rows, :] = parts[p]
    even = place_ref[0] % 2 == 0
    for p in range(3):
        up, down = parts[planes + p], parts[p]
        near_ref[p * rows : (p + 1) * rows, :] = jnp.where(even, up, down)
        far_ref[p * rows : (p + 1) * rows, :] = jnp.where(even, down, up)


def make_table(place_ref, devices, planes, rows, columns, own_ref, near_ref, far_ref, table_ref):
    not_first, not_last = edges(place_ref, devices)
    misfit = [own_ref[p * rows : (p + 1) * rows, :] for p in range(planes + 3)]
    even = place_ref[0] % 2 == 0
    for p in range(3):
        near = near_ref[p * rows : (p + 1) * rows, :]
        far = far_ref[p * rows : (p + 1) * rows, :]
        misfit[p] = misfit[p] + jnp.where(even, far, near)
        misfit[planes + p] = misfit[planes + p] + jnp.where(even, near, far)
    misfit[0] = misfit[0] * not_first
    misfit[planes + 1] = misfit[planes + 1] * not_last
    misfit[planes + 2] = misfit[planes + 2] * not_last
    pulled = [blur_sheet(sheet) for sheet in blur_along(misfit)]
    pulled[planes] = pulled[planes] * not_last
    for p in range(planes + 1):
        shifted = pltpu.roll(pulled[p], columns - 1, 1)
        for turn, sheet in enumerate((pulled[p], shifted)):
            high, low = halves(sheet)
            at = slice((turn * (planes + 1) + p) * rows, (turn * (planes + 1) + p + 1) * rows)
            table_ref[at, :columns] = high
            table_ref[at, columns:] = low


def load_tiles(ref, tiles):
    return jnp.concatenate([ref[t * fields : (t + 1) * fields, :] for t in tiles], 1)


def store_tiles(ref, tiles, value):
    for i, t in enumerate(tiles):
        ref[t * fields : (t + 1) * fields, :] = value[:, i * lanes : (i + 1) * lanes]


def chunks(devices, sub, planes, ordered):
    if ordered:
        return [([b * sub + k for b in range(devices)], k, 2) for k in range(sub)]
    tiles = devices * sub
    batch = max(b for b in range(1, 25) if tiles % b == 0)
    return [(range(i, i + batch), 0, planes) for i in range(0, tiles, batch)]


def in_order(message_ref, devices, sub):
    rows = [(b * sub + 1) * fields + fields - 1 for b in range(devices)]
    flags = jnp.concatenate([message_ref[row : row + 1, :] for row in rows], 0)
    return jnp.min(flags) > 0.5


def either(ordered_ref, planes, sub, work):
    if not sorted_buckets(planes, sub):
        work(False)
        return
    ordered = ordered_ref[0] == 1

    @pl.when(ordered)
    def _():
        work(True)

    @pl.when(jnp.logical_not(ordered))
    def _():
        work(False)


def add_density(sheets, state, base, span, rows, columns):
    part = density_part(state, base, span, rows, columns)
    for p in range(span + 1):
        sheet = part[p * rows : (p + 1) * rows]
        sheets[base + p] = sheet if sheets[base + p] is None else sheets[base + p] + sheet


def density_kernel(
    devices, sub, planes, rows, columns, place_ref, message_ref, map_ref, own_ref, near_ref, far_ref,
    ordered_ref,
):
    if sorted_buckets(planes, sub):
        ordered_ref[0] = jnp.where(in_order(message_ref, devices, sub), 1, 0)
    else:
        ordered_ref[0] = 0

    def work(ordered):
        sheets = [None] * (planes + 1)
        for tiles, base, span in chunks(devices, sub, planes, ordered):
            add_density(sheets, load_tiles(message_ref, tiles), base, span, rows, columns)
        share_misfit(place_ref, devices, planes, rows, sheets, map_ref, own_ref, near_ref, far_ref)

    either(ordered_ref, planes, sub, work)


def middle_kernel(
    devices, sub, planes, rows, columns, place_ref, ordered_ref, message_ref, was_ref, from_near_ref,
    from_far_ref, map_ref, moved_ref, first_ref, own_ref, near_ref, far_ref, table_ref,
):
    make_table(
        place_ref, devices, planes, rows, columns, was_ref, from_near_ref, from_far_ref, table_ref
    )

    def work(ordered):
        sheets, waiting = [None] * (planes + 1), None
        for tiles, base, span in chunks(devices, sub, planes, ordered):
            state = load_tiles(message_ref, tiles)
            gradient = gradient_part(state, table_ref, base, span, planes, rows, columns)
            moved = jnp.concatenate(
                [state[0:2], state[2:5] - probe_step * jnp.tanh(gradient), state[5:8]], 0
            )
            store_tiles(moved_ref, tiles, moved)
            store_tiles(
                first_ref, tiles,
                jnp.concatenate([gradient, jnp.zeros((5, gradient.shape[1]), f32)], 0),
            )
            if waiting is not None:
                add_density(sheets, *waiting, rows, columns)
            waiting = (moved, base, span)
        add_density(sheets, *waiting, rows, columns)
        share_misfit(place_ref, devices, planes, rows, sheets, map_ref, own_ref, near_ref, far_ref)

    either(ordered_ref, planes, sub, work)


def cross_list(left, right):
    return [
        left[1] * right[2] - left[2] * right[1],
        left[2] * right[0] - left[0] * right[2],
        left[0] * right[1] - left[1] * right[0],
    ]


def last_kernel(
    devices, sub, planes, rows, columns, place_ref, ordered_ref, message_ref, moved_ref, first_ref,
    was_ref, from_near_ref, from_far_ref, reply_ref, table_ref,
):
    make_table(
        place_ref, devices, planes, rows, columns, was_ref, from_near_ref, from_far_ref, table_ref
    )
    last_of = jnp.concatenate(
        [
            message_ref[d * sub * fields + fields - 1 : d * sub * fields + fields, :]
            for d in range(devices)
        ],
        0,
    )
    slab_plane = (place_ref[0] * planes).astype(f32)

    def work(ordered):
        sums = jnp.zeros((devices, 16), f32)
        for tiles, base, span in chunks(devices, sub, planes, ordered):
            state = load_tiles(message_ref, tiles)
            moved = load_tiles(moved_ref, tiles)
            first = load_tiles(first_ref, tiles)[0:3]
            second = gradient_part(moved, table_ref, base, span, planes, rows, columns)
            width = state.shape[1]
            plane, row, _, column, _ = neighbours_of(state, rows, columns)
            cells = (plane + slab_plane, row, column)
            pieces = []
            for gradient, offset in ((first, state), (second, moved)):
                g = [gradient[d : d + 1] for d in range(3)]
                pieces += g + cross_list([cells[d] + offset[2 + d : 3 + d] for d in range(3)], g)
            pieces.append(jnp.where(state[5:6] > 0.0, 1.0, 0.0))
            pieces.append(jnp.zeros((3, width), f32))
            block = jnp.concatenate(pieces, 0)
            receiver = down_rows(devices, lanes)
            chosen = jnp.concatenate(
                [
                    jnp.where(
                        (receiver < t // sub)
                        & (last_of == state[6:7, i * lanes : (i + 1) * lanes]),
                        1.0,
                        0.0,
                    )
                    for i, t in enumerate(tiles)
                ],
                1,
            ).astype(bf16)
            sums = sums + sum(dot_nt(chosen, piece) for piece in thirds(block))
            store_tiles(
                reply_ref, tiles,
                jnp.concatenate([first, second, jnp.zeros((2, width), f32)], 0),
            )
        sums = jnp.concatenate([sums, jnp.zeros((devices, lanes - 16), f32)], 1)
        for d in range(devices):
            reply_ref[d * sub * fields + fields - 1 : d * sub * fields + fields, :] = sums[d : d + 1]

    either(ordered_ref, planes, sub, work)


def chain_kernel(
    devices, sub, planes, columns, reply_ref, slot_ref, home_ref, torque_ref, gradient_ref
):
    atoms = slot_ref.shape[1]
    blocks = atoms // lanes
    tiles = devices * sub
    high, low = halves(reply_ref[...])
    left = jnp.concatenate([high, low], 1)
    width = 512
    found = []
    for c in range(atoms // width):
        at = slice(c * width, (c + 1) * width)
        spot = jnp.where(down_rows(lanes, width) == slot_ref[1:2, at], 1.0, 0.0).astype(bf16)
        picked = dot_nn(left, jnp.concatenate([spot, spot], 0))
        which = jnp.broadcast_to(slot_ref[0:1, at], (fields, width))
        total = jnp.zeros((fields, width), f32)
        for t in range(tiles):
            total = jnp.where(which == t, picked[t * fields : (t + 1) * fields], total)
        found.append(total)
    gradients = jnp.concatenate(found, 1)[0:6]
    gradient_ref[...] = gradients
    fraction = home_ref[3:6, :]
    moved = fraction - probe_step * jnp.tanh(gradients[0:3])
    base = [home_ref[d : d + 1, :] for d in range(3)]
    axis = [home_ref[7 + d : 8 + d, :] for d in range(3)]
    positions = [[base[d] + offset[d : d + 1] for d in range(3)] for offset in (fraction, moved)]
    pieces = []
    for e in range(2):
        g = [gradients[3 * e + d : 3 * e + d + 1] for d in range(3)]
        pieces += g + cross_list(positions[e], g)
    pieces.append(jnp.ones((1, atoms), f32))
    pieces.append(jnp.zeros((3, atoms), f32))
    stacked = jnp.concatenate(thirds(jnp.concatenate(pieces, 0)), 0)

    def joined(x):
        return x[0:16] + x[16:32] + x[32:48]

    chain = home_ref[6:7, :]
    chain_rows = jnp.concatenate([chain[:, j * lanes : (j + 1) * lanes] for j in range(blocks)], 0)
    ends = jnp.broadcast_to(chain_rows[:, lanes - 1 :], (blocks, atoms))
    later = lax.broadcasted_iota(jnp.int32, (blocks, atoms), 1) >= lanes * (
        down_rows(blocks, atoms) + 1
    )
    bridge = jnp.where(later & (ends == chain), 1.0, 0.0).astype(bf16)
    carries = joined(dot_nt(stacked, bridge))
    arrived = jnp.zeros((1, lanes), f32)
    for d in range(devices):
        arrived = arrived + reply_ref[d * sub * fields + fields - 1 : d * sub * fields + fields, :]
    diagonal = down_rows(16, lanes) == lax.broadcasted_iota(jnp.int32, (16, lanes), 1)
    arrived = jnp.sum(jnp.where(diagonal, arrived, 0.0), 1, keepdims=True)
    padded = jnp.concatenate([chain_rows, jnp.zeros((lanes - blocks, lanes), f32)], 0)
    down_chain = jnp.transpose(padded)
    not_before = down_rows(lanes, lanes) >= lax.broadcasted_iota(jnp.int32, (lanes, lanes), 1)
    closing = chain[:, atoms - 1 :]
    sums = []
    for j in range(blocks):
        at = slice(j * lanes, (j + 1) * lanes)
        mask = not_before & (down_chain[:, j : j + 1] == chain[:, at])
        local = joined(dot_nn(stacked[:, at], jnp.where(mask, 1.0, 0.0).astype(bf16)))
        end = chain[:, (j + 1) * lanes - 1 : (j + 1) * lanes]
        carry = carries[:, j : j + 1] + jnp.where(end == closing, arrived, 0.0)
        sums.append(local + jnp.where(chain[:, at] == end, carry, 0.0))
    totals = jnp.concatenate(sums, 1)
    scale = 1.0 / (columns * jnp.sqrt(totals[12:13]))
    torques = []
    for e in range(2):
        force = [totals[6 * e + d : 6 * e + d + 1] for d in range(3)]
        lever = cross_list(positions[e], force)
        turn = 0.0
        for d in range(3):
            turn = turn + axis[d] * (totals[6 * e + 3 + d : 6 * e + 4 + d] - lever[d])
        torques.append(turn * scale)
    torque_ref[...] = jnp.concatenate(torques, 0)


def whole(count):
    return [pl.BlockSpec(memory_space=pltpu.VMEM)] * count


def settings():
    return pltpu.CompilerParams(vmem_limit_bytes=room)


def shape_of(*dims, dtype=f32):
    return jax.ShapeDtypeStruct(dims, dtype)


def seat(slab, across):
    turned = (slab // (2 * across)) % 2
    return slab ^ (turned * (2 * across - 2))


def seats_across(mesh):
    devices = mesh.devices[0]
    count = len(devices)
    if not all(hasattr(device, "coords") for device in devices):
        return count
    across = len({device.coords[0] for device in devices})
    if across & (across - 1) or count % (4 * across):
        return count
    first = devices[0].coords
    for i, device in enumerate(devices):
        x, z = i // 2 % across, i // (2 * across)
        if device.coords[0] - first[0] != x or device.coords[2] - first[2] != z:
            return count
    return across


def swap_near(value, across):
    count = lax.axis_size("bx")
    pairs = [(seat(i, across), seat(i ^ 1, across)) for i in range(count)]
    return lax.ppermute(value, "bx", pairs)


def swap_far(value, across):
    count = lax.axis_size("bx")
    pairs = []
    for i in range(1, count - 1, 2):
        pairs += [(seat(i, across), seat(i + 1, across)), (seat(i + 1, across), seat(i, across))]
    return lax.ppermute(value, "bx", pairs)


def exchange(value):
    return lax.all_to_all(value, "bx", split_axis=0, concat_axis=0, tiled=True)


def shards(
    across,
    density_map,
    amplitude,
    fraction,
    torsion_axis,
    brick_owner,
    plane_offset,
    row_offset,
    column_offset,
    chain_index,
):
    planes, rows, columns = density_map.shape
    atoms = amplitude.shape[0]
    devices = lax.axis_size("bx")
    capacity = 3 * atoms // devices
    sub = -(-capacity // lanes)
    tiles = devices * sub
    grid = (planes, rows, columns)
    place = seat(lax.axis_index("bx").astype(jnp.int32), across).reshape(1)
    moves = [(i, seat(i, across)) for i in range(devices)]
    if any(i != j for i, j in moves):
        density_map = lax.ppermute(density_map, "bx", moves)
    scalar = [pl.BlockSpec(memory_space=pltpu.SMEM)]

    owner, plane, row, column, chain = (
        item.reshape(1, atoms)
        for item in (brick_owner, plane_offset, row_offset, column_offset, chain_index)
    )
    held = [pltpu.VMEM((1, atoms), jnp.int32)] * 5
    held += [pltpu.VMEM((1, atoms), f32)] + [pltpu.VMEM((3, atoms), f32)] * 2
    message, slot, home = pl.pallas_call(
        functools.partial(pack_kernel, devices, sub, planes, rows, across),
        out_shape=(
            shape_of(tiles * fields, lanes),
            shape_of(2, atoms, dtype=jnp.int32),
            shape_of(10, atoms),
        ),
        in_specs=[pl.BlockSpec(memory_space=pltpu.HBM)] * 8,
        out_specs=whole(3),
        scratch_shapes=held + [pltpu.SemaphoreType.DMA((8,))],
        name="pack",
    )(owner, plane, row, column, chain, amplitude.reshape(1, atoms), fraction, torsion_axis)
    message = exchange(message)

    own_shape = shape_of((planes + 3) * rows, columns)
    edge_shape = shape_of(3 * rows, columns)
    own, near, far, ordered = pl.pallas_call(
        functools.partial(density_kernel, devices, sub, *grid),
        out_shape=(own_shape, edge_shape, edge_shape, shape_of(1, dtype=jnp.int32)),
        in_specs=scalar + whole(2),
        out_specs=whole(3) + scalar,
        compiler_params=settings(),
        name="density",
    )(place, message, density_map)
    near, far = swap_near(near, across), swap_far(far, across)
    table = pltpu.VMEM((2 * (planes + 1) * rows, 2 * columns), bf16)
    moved, first, own, near, far = pl.pallas_call(
        functools.partial(middle_kernel, devices, sub, *grid),
        out_shape=(
            shape_of(tiles * fields, lanes),
            shape_of(tiles * fields, lanes),
            own_shape,
            edge_shape,
            edge_shape,
        ),
        in_specs=scalar * 2 + whole(5),
        out_specs=whole(5),
        scratch_shapes=[table],
        compiler_params=settings(),
        name="middle",
    )(place, ordered, message, own, near, far, density_map)
    near, far = swap_near(near, across), swap_far(far, across)
    reply = pl.pallas_call(
        functools.partial(last_kernel, devices, sub, *grid),
        out_shape=shape_of(tiles * fields, lanes),
        in_specs=scalar * 2 + whole(6),
        out_specs=whole(1)[0],
        scratch_shapes=[table],
        compiler_params=settings(),
        name="last",
    )(place, ordered, message, moved, first, own, near, far)
    reply = exchange(reply)
    torques, gradients = pl.pallas_call(
        functools.partial(chain_kernel, devices, sub, planes, columns),
        out_shape=(shape_of(2, atoms), shape_of(6, atoms)),
        in_specs=whole(3),
        out_specs=whole(2),
        compiler_params=settings(),
        name="chains",
    )(reply, slot, home)
    return torques, gradients


def solution(mesh):
    return jax.shard_map(
        functools.partial(shards, seats_across(mesh)),
        mesh=mesh,
        in_specs=(
            P(("grp", "bx"), None, None),
            P(("grp", "bx")),
            P(None, ("grp", "bx")),
            P(None, ("grp", "bx")),
            P(("grp", "bx"), None),
            P(("grp", "bx")),
            P(("grp", "bx")),
            P(("grp", "bx")),
            P(("grp", "bx")),
        ),
        out_specs=(P(None, ("grp", "bx")), P(None, ("grp", "bx"))),
        check_vma=False,
    )
```

```python
import functools

import jax
import jax.numpy as jnp
from jax import lax
from jax.experimental import pallas as pl
from jax.experimental.pallas import tpu as pltpu
from jax.sharding import PartitionSpec as P

side_tap = 0.25
middle_tap = 0.5
probe_step = 0.2
lanes = 128
fields = 8
f32, bf16 = jnp.float32, jnp.bfloat16
room = 48 * 1024 * 1024


def dot_nt(left, right):
    return lax.dot_general(left, right, (((1,), (1,)), ((), ())), preferred_element_type=f32)


def dot_nn(left, right):
    return lax.dot_general(left, right, (((1,), (0,)), ((), ())), preferred_element_type=f32)


def halves(x):
    high = x.astype(bf16)
    return high, (x - high.astype(f32)).astype(bf16)


def thirds(x):
    high, rest = x.astype(bf16), None
    rest = x - high.astype(f32)
    middle = rest.astype(bf16)
    return high, middle, (rest - middle.astype(f32)).astype(bf16)


def down_rows(count, width):
    return lax.broadcasted_iota(jnp.int32, (count, width), 0)


def spread(row, count):
    tile = jnp.broadcast_to(row, (16, row.shape[1])).astype(bf16)
    return jnp.concatenate([tile] * (count // 16), 0)


def counting(count, width):
    part = down_rows(count, lanes).astype(f32).astype(bf16)
    return jnp.concatenate([part] * (width // lanes), 1)


def pack_kernel(devices, sub, planes, rows, *refs):
    hbm, (message_ref, slot_ref, home_ref), held = refs[:8], refs[8:11], refs[11:19]
    semaphores = refs[19]
    copies = [
        pltpu.make_async_copy(source, target, semaphores.at[i])
        for i, (source, target) in enumerate(zip(hbm, held))
    ]
    for copy in copies:
        copy.start()
    for copy in copies:
        copy.wait()
    owner_ref, plane_ref, row_ref, column_ref, chain_ref, amp_ref, frac_ref, axis_ref = held
    atoms = owner_ref.shape[1]
    blocks = atoms // lanes
    tiles = devices * sub
    owner, plane = owner_ref[...], plane_ref[...]
    chain = chain_ref[...].astype(f32)
    home_ref[0:1, :] = (owner * planes + plane).astype(f32)
    home_ref[1:2, :] = row_ref[...].astype(f32)
    home_ref[2:3, :] = column_ref[...].astype(f32)
    home_ref[3:6, :] = frac_ref[...]
    home_ref[6:7, :] = chain
    home_ref[7:10, :] = axis_ref[...]
    groups = planes * devices
    mine = down_rows(groups, atoms) == plane * devices + owner
    onehot = jnp.where(mine, 1.0, 0.0)
    stacked = jnp.concatenate(
        [onehot[:, j * lanes : (j + 1) * lanes] for j in range(blocks)], 0
    ).astype(bf16)
    k = lax.broadcasted_iota(jnp.int32, (lanes, 2 * lanes), 0)
    a = lax.broadcasted_iota(jnp.int32, (lanes, 2 * lanes), 1)
    before = jnp.where((k < a) | (a >= lanes), 1.0, 0.0).astype(bf16)
    counts = dot_nn(stacked, before)
    parts = [counts[j * groups : (j + 1) * groups] for j in range(blocks)]
    total = parts[0][:, lanes:]
    for part in parts[1:]:
        total = total + part[:, lanes:]
    held_by = [total[p * devices : (p + 1) * devices] for p in range(planes)]
    half = planes // 2
    none = jnp.zeros((devices, lanes), f32)
    offsets = [sum(held_by[:p], none) for p in range(half)]
    offsets += [sum(held_by[p + 1 :], none) for p in range(half, planes)]
    running = jnp.concatenate(offsets, 0)
    ranks = []
    for j, part in enumerate(parts):
        here = onehot[:, j * lanes : (j + 1) * lanes]
        ranks.append(jnp.sum((part[:, :lanes] + running) * here, 0, keepdims=True))
        running = running + part[:, lanes:]
    rank = jnp.concatenate(ranks, 1).astype(jnp.int32)
    rank = jnp.where(plane < half, rank, sub * lanes - 1 - rank)
    tile = owner * sub + lax.shift_right_logical(rank, 7)
    lane = rank & (lanes - 1)
    slot_ref[...] = jnp.concatenate([tile, lane], 0)
    values = jnp.concatenate(
        [
            (plane * rows + row_ref[...]).astype(f32),
            column_ref[...].astype(f32),
            frac_ref[...],
            amp_ref[...],
            chain,
            jnp.zeros((1, atoms), f32),
        ],
        0,
    )
    pieces = [piece.astype(f32) for piece in halves(values)]
    width = 512
    pair = lax.shift_right_logical(tile, 1)
    inside = (tile & 1) * lanes + lane
    total = None
    for c in range(atoms // width):
        at = slice(c * width, (c + 1) * width)
        spot = jnp.where(down_rows(2 * lanes, width) == inside[:, at], 1.0, 0.0).astype(bf16)
        which = jnp.broadcast_to(pair[:, at], (fields, width))
        picks = [which == t for t in range(tiles // 2)]
        left = jnp.concatenate(
            [jnp.where(pick, piece[:, at], 0.0) for piece in pieces for pick in picks], 0
        ).astype(bf16)
        one = dot_nt(left, spot)
        one = one[: one.shape[0] // 2] + one[one.shape[0] // 2 :]
        total = one if total is None else total + one
    for t in range(tiles):
        message_ref[t * fields : (t + 1) * fields, :] = total[
            t // 2 * fields : (t // 2 + 1) * fields, t % 2 * lanes : (t % 2 + 1) * lanes
        ]
    last = jnp.broadcast_to(chain[:, atoms - 1 :], (1, lanes))
    for b in range(devices):
        message_ref[b * sub * fields + fields - 1 : b * sub * fields + fields, :] = last
    if sorted_buckets(planes, sub):
        fits = 1.0
        lower, upper = held_by[0] + held_by[1], held_by[2] + held_by[3]
        limits = (lower, 2.0 * lanes), (upper, 2.0 * lanes), (held_by[0], lanes), (held_by[3], lanes)
        for amount, limit in limits:
            fits = fits * jnp.where(amount <= limit, 1.0, 0.0)
        for b in range(devices):
            row = (b * sub + 1) * fields + fields - 1
            message_ref[row : row + 1, :] = fits[b : b + 1]


def sorted_buckets(planes, sub):
    return planes == 4 and sub == 3


def neighbours_of(state, rows, columns):
    cell, column = state[0:1], state[1:2]
    plane = jnp.floor(cell * (1.0 / rows))
    row = cell - plane * rows
    next_row = jnp.where(row == rows - 1.0, 0.0, row + 1.0)
    next_column = jnp.where(column == columns - 1.0, 0.0, column + 1.0)
    return plane, row, next_row, column, next_column


def density_part(state, base, span, rows, columns):
    width = state.shape[1]
    plane, row, next_row, column, next_column = neighbours_of(state, rows, columns)
    fx, fy, fz, amplitude = (state[2 + i : 3 + i] for i in range(4))
    zero = jnp.zeros((), bf16)
    steps = counting(columns, width)
    here, there = steps == spread(column, columns), steps == spread(next_column, columns)

    def columns_of(near, far):
        return jnp.where(here, spread(near, columns), jnp.where(there, spread(far, columns), zero))

    near, far = halves(1.0 - fz), halves(fz)
    right_high = columns_of(near[0].astype(f32), far[0].astype(f32))
    right_low = columns_of(near[1].astype(f32), far[1].astype(f32))
    level = down_rows(fields, width).astype(f32) + float(base)
    along = amplitude * jnp.where(level == plane, 1.0 - fx, jnp.where(level == plane + 1.0, fx, 0.0))
    near, far = halves(along * (1.0 - fy)), halves(along * fy)
    steps = counting(rows, width)
    here, there = steps == spread(row, rows), steps == spread(next_row, rows)
    lefts = []
    for grade in range(2):
        first, second = near[grade].astype(f32), far[grade].astype(f32)
        lefts.append(
            jnp.concatenate(
                [
                    jnp.where(
                        here,
                        spread(first[p : p + 1], rows),
                        jnp.where(there, spread(second[p : p + 1], rows), zero),
                    )
                    for p in range(span + 1)
                ],
                0,
            )
        )
    both = dot_nt(jnp.concatenate(lefts, 0), right_high)
    count = lefts[0].shape[0]
    return both[:count] + both[count:] + dot_nt(lefts[0], right_low)


def gradient_part(state, table_ref, base, span, planes, rows, columns):
    width = state.shape[1]
    plane, row, next_row, column, _ = neighbours_of(state, rows, columns)
    fx, fy, fz, amplitude = (state[2 + i : 3 + i] for i in range(4))
    spot = jnp.where(
        counting(columns, width) == spread(column, columns),
        jnp.ones((), bf16),
        jnp.zeros((), bf16),
    )
    table = jnp.concatenate(
        [
            table_ref[(e2 * (planes + 1) + base) * rows : (e2 * (planes + 1) + base + span + 1) * rows, :]
            for e2 in range(2)
        ],
        0,
    )
    sampled = dot_nn(table, jnp.concatenate([spot, spot], 0))

    def eight(x):
        return jnp.broadcast_to(x, (8, width))

    level = down_rows(8, width).astype(f32)
    at_plane = [eight(plane) == float(base + p) for p in range(span)]
    eighths = [jnp.floor(at * 0.125) for at in (row, next_row)]
    at_eighth = [[eight(part) == float(j) for j in range(rows // 8)] for part in eighths]
    corner = {}
    for e2 in range(2):
        for e0 in range(2):
            chosen = []
            for j in range(rows // 8):
                at = (e2 * (span + 1) + e0) * rows + 8 * j
                pick = sampled[at : at + 8]
                for p in range(1, span):
                    pick = jnp.where(at_plane[p], sampled[at + p * rows : at + p * rows + 8], pick)
                chosen.append(pick)
            for e1 in range(2):
                pick = chosen[0]
                for j in range(1, rows // 8):
                    pick = jnp.where(at_eighth[e1][j], chosen[j], pick)
                corner[e0, e1, e2] = pick
    fx, fz = eight(fx), eight(fz)
    weights = (amplitude * (1.0 - fy), amplitude * fy)
    gx = gy = gz = 0.0
    for e1 in range(2):
        here = level == eight((row, next_row)[e1] - 8.0 * eighths[e1])
        weight = jnp.where(here, eight(weights[e1]), 0.0)
        signed = jnp.where(here, eight(amplitude), 0.0)
        drop = [corner[e0, e1, 1] - corner[e0, e1, 0] for e0 in range(2)]
        value = [corner[e0, e1, 0] + fz * drop[e0] for e0 in range(2)]
        slope = value[1] - value[0]
        gx = gx + weight * slope
        gz = gz + weight * (drop[0] + fx * (drop[1] - drop[0]))
        middle = signed * (value[0] + fx * slope)
        gy = gy + middle if e1 else gy - middle
    return jnp.concatenate([jnp.sum(g, 0, keepdims=True) for g in (gx, gy, gz)], 0)


def blur_sheet(sheet):
    rows, columns = sheet.shape
    sheet = middle_tap * sheet + side_tap * (pltpu.roll(sheet, 1, 0) + pltpu.roll(sheet, rows - 1, 0))
    return middle_tap * sheet + side_tap * (
        pltpu.roll(sheet, 1, 1) + pltpu.roll(sheet, columns - 1, 1)
    )


def blur_along(sheets):
    return [
        middle_tap * sheets[i] + side_tap * (sheets[i - 1] + sheets[i + 1])
        for i in range(1, len(sheets) - 1)
    ]


def edges(place_ref, devices):
    not_first = jnp.where(place_ref[0] == 0, 0.0, 1.0)
    not_last = jnp.where(place_ref[0] == devices - 1, 0.0, 1.0)
    return not_first, not_last


def share_misfit(place_ref, devices, planes, rows, density, map_ref, own_ref, near_ref, far_ref):
    _, not_last = edges(place_ref, devices)
    density[planes] = density[planes] * not_last
    zero = jnp.zeros_like(density[0])
    parts = [blur_sheet(sheet) for sheet in blur_along([zero, zero] + density + [zero, zero])]
    for p in range(planes):
        parts[p + 1] = parts[p + 1] - map_ref[p]
    for p in range(planes + 3):
        own_ref[p * rows : (p + 1) * rows, :] = parts[p]
    even = place_ref[0] % 2 == 0
    for p in range(3):
        up, down = parts[planes + p], parts[p]
        near_ref[p * rows : (p + 1) * rows, :] = jnp.where(even, up, down)
        far_ref[p * rows : (p + 1) * rows, :] = jnp.where(even, down, up)


def make_table(place_ref, devices, planes, rows, columns, own_ref, near_ref, far_ref, table_ref):
    not_first, not_last = edges(place_ref, devices)
    misfit = [own_ref[p * rows : (p + 1) * rows, :] for p in range(planes + 3)]
    even = place_ref[0] % 2 == 0
    for p in range(3):
        near = near_ref[p * rows : (p + 1) * rows, :]
        far = far_ref[p * rows : (p + 1) * rows, :]
        misfit[p] = misfit[p] + jnp.where(even, far, near)
        misfit[planes + p] = misfit[planes + p] + jnp.where(even, near, far)
    misfit[0] = misfit[0] * not_first
    misfit[planes + 1] = misfit[planes + 1] * not_last
    misfit[planes + 2] = misfit[planes + 2] * not_last
    pulled = [blur_sheet(sheet) for sheet in blur_along(misfit)]
    pulled[planes] = pulled[planes] * not_last
    for p in range(planes + 1):
        shifted = pltpu.roll(pulled[p], columns - 1, 1)
        for turn, sheet in enumerate((pulled[p], shifted)):
            high, low = halves(sheet)
            at = slice((turn * (planes + 1) + p) * rows, (turn * (planes + 1) + p + 1) * rows)
            table_ref[at, :columns] = high
            table_ref[at, columns:] = low


def load_tiles(ref, tiles):
    return jnp.concatenate([ref[t * fields : (t + 1) * fields, :] for t in tiles], 1)


def store_tiles(ref, tiles, value):
    for i, t in enumerate(tiles):
        ref[t * fields : (t + 1) * fields, :] = value[:, i * lanes : (i + 1) * lanes]


def chunks(devices, sub, planes, ordered):
    if ordered:
        return [([b * sub + k for b in range(devices)], k, 2) for k in range(sub)]
    tiles = devices * sub
    batch = max(b for b in range(1, 25) if tiles % b == 0)
    return [(range(i, i + batch), 0, planes) for i in range(0, tiles, batch)]


def in_order(message_ref, devices, sub):
    rows = [(b * sub + 1) * fields + fields - 1 for b in range(devices)]
    flags = jnp.concatenate([message_ref[row : row + 1, :] for row in rows], 0)
    return jnp.min(flags) > 0.5


def either(ordered_ref, planes, sub, work):
    if not sorted_buckets(planes, sub):
        work(False)
        return
    ordered = ordered_ref[0] == 1

    @pl.when(ordered)
    def _():
        work(True)

    @pl.when(jnp.logical_not(ordered))
    def _():
        work(False)


def add_density(sheets, state, base, span, rows, columns):
    part = density_part(state, base, span, rows, columns)
    for p in range(span + 1):
        sheet = part[p * rows : (p + 1) * rows]
        sheets[base + p] = sheet if sheets[base + p] is None else sheets[base + p] + sheet


def density_kernel(
    devices, sub, planes, rows, columns, place_ref, message_ref, map_ref, own_ref, near_ref, far_ref,
    ordered_ref,
):
    if sorted_buckets(planes, sub):
        ordered_ref[0] = jnp.where(in_order(message_ref, devices, sub), 1, 0)
    else:
        ordered_ref[0] = 0

    def work(ordered):
        sheets = [None] * (planes + 1)
        for tiles, base, span in chunks(devices, sub, planes, ordered):
            add_density(sheets, load_tiles(message_ref, tiles), base, span, rows, columns)
        share_misfit(place_ref, devices, planes, rows, sheets, map_ref, own_ref, near_ref, far_ref)

    either(ordered_ref, planes, sub, work)


def middle_kernel(
    devices, sub, planes, rows, columns, place_ref, ordered_ref, message_ref, was_ref, from_near_ref,
    from_far_ref, map_ref, moved_ref, first_ref, own_ref, near_ref, far_ref, table_ref,
):
    make_table(
        place_ref, devices, planes, rows, columns, was_ref, from_near_ref, from_far_ref, table_ref
    )

    def work(ordered):
        sheets, waiting = [None] * (planes + 1), None
        for tiles, base, span in chunks(devices, sub, planes, ordered):
            state = load_tiles(message_ref, tiles)
            gradient = gradient_part(state, table_ref, base, span, planes, rows, columns)
            moved = jnp.concatenate(
                [state[0:2], state[2:5] - probe_step * jnp.tanh(gradient), state[5:8]], 0
            )
            store_tiles(moved_ref, tiles, moved)
            store_tiles(
                first_ref, tiles,
                jnp.concatenate([gradient, jnp.zeros((5, gradient.shape[1]), f32)], 0),
            )
            if waiting is not None:
                add_density(sheets, *waiting, rows, columns)
            waiting = (moved, base, span)
        add_density(sheets, *waiting, rows, columns)
        share_misfit(place_ref, devices, planes, rows, sheets, map_ref, own_ref, near_ref, far_ref)

    either(ordered_ref, planes, sub, work)


def cross_list(left, right):
    return [
        left[1] * right[2] - left[2] * right[1],
        left[2] * right[0] - left[0] * right[2],
        left[0] * right[1] - left[1] * right[0],
    ]


def last_kernel(
    devices, sub, planes, rows, columns, place_ref, ordered_ref, message_ref, moved_ref, first_ref,
    was_ref, from_near_ref, from_far_ref, reply_ref, table_ref,
):
    make_table(
        place_ref, devices, planes, rows, columns, was_ref, from_near_ref, from_far_ref, table_ref
    )
    last_of = jnp.concatenate(
        [
            message_ref[d * sub * fields + fields - 1 : d * sub * fields + fields, :]
            for d in range(devices)
        ],
        0,
    )
    slab_plane = (place_ref[0] * planes).astype(f32)

    def work(ordered):
        sums = jnp.zeros((devices, 16), f32)
        for tiles, base, span in chunks(devices, sub, planes, ordered):
            state = load_tiles(message_ref, tiles)
            moved = load_tiles(moved_ref, tiles)
            first = load_tiles(first_ref, tiles)[0:3]
            second = gradient_part(moved, table_ref, base, span, planes, rows, columns)
            width = state.shape[1]
            plane, row, _, column, _ = neighbours_of(state, rows, columns)
            cells = (plane + slab_plane, row, column)
            pieces = []
            for gradient, offset in ((first, state), (second, moved)):
                g = [gradient[d : d + 1] for d in range(3)]
                pieces += g + cross_list([cells[d] + offset[2 + d : 3 + d] for d in range(3)], g)
            pieces.append(jnp.where(state[5:6] > 0.0, 1.0, 0.0))
            pieces.append(jnp.zeros((3, width), f32))
            block = jnp.concatenate(pieces, 0)
            receiver = down_rows(devices, lanes)
            chosen = jnp.concatenate(
                [
                    jnp.where(
                        (receiver < t // sub)
                        & (last_of == state[6:7, i * lanes : (i + 1) * lanes]),
                        1.0,
                        0.0,
                    )
                    for i, t in enumerate(tiles)
                ],
                1,
            ).astype(bf16)
            sums = sums + sum(dot_nt(chosen, piece) for piece in thirds(block))
            store_tiles(
                reply_ref, tiles,
                jnp.concatenate([first, second, jnp.zeros((2, width), f32)], 0),
            )
        sums = jnp.concatenate([sums, jnp.zeros((devices, lanes - 16), f32)], 1)
        for d in range(devices):
            reply_ref[d * sub * fields + fields - 1 : d * sub * fields + fields, :] = sums[d : d + 1]

    either(ordered_ref, planes, sub, work)


def chain_kernel(
    devices, sub, planes, columns, reply_ref, slot_ref, home_ref, torque_ref, gradient_ref
):
    atoms = slot_ref.shape[1]
    blocks = atoms // lanes
    tiles = devices * sub
    high, low = halves(reply_ref[...])
    left = jnp.concatenate([high, low], 1)
    width = 512
    found = []
    for c in range(atoms // width):
        at = slice(c * width, (c + 1) * width)
        spot = jnp.where(down_rows(lanes, width) == slot_ref[1:2, at], 1.0, 0.0).astype(bf16)
        picked = dot_nn(left, jnp.concatenate([spot, spot], 0))
        which = jnp.broadcast_to(slot_ref[0:1, at], (fields, width))
        total = jnp.zeros((fields, width), f32)
        for t in range(tiles):
            total = jnp.where(which == t, picked[t * fields : (t + 1) * fields], total)
        found.append(total)
    gradients = jnp.concatenate(found, 1)[0:6]
    gradient_ref[...] = gradients
    fraction = home_ref[3:6, :]
    moved = fraction - probe_step * jnp.tanh(gradients[0:3])
    base = [home_ref[d : d + 1, :] for d in range(3)]
    axis = [home_ref[7 + d : 8 + d, :] for d in range(3)]
    positions = [[base[d] + offset[d : d + 1] for d in range(3)] for offset in (fraction, moved)]
    pieces = []
    for e in range(2):
        g = [gradients[3 * e + d : 3 * e + d + 1] for d in range(3)]
        pieces += g + cross_list(positions[e], g)
    pieces.append(jnp.ones((1, atoms), f32))
    pieces.append(jnp.zeros((3, atoms), f32))
    stacked = jnp.concatenate(thirds(jnp.concatenate(pieces, 0)), 0)

    def joined(x):
        return x[0:16] + x[16:32] + x[32:48]

    chain = home_ref[6:7, :]
    chain_rows = jnp.concatenate([chain[:, j * lanes : (j + 1) * lanes] for j in range(blocks)], 0)
    ends = jnp.broadcast_to(chain_rows[:, lanes - 1 :], (blocks, atoms))
    later = lax.broadcasted_iota(jnp.int32, (blocks, atoms), 1) >= lanes * (
        down_rows(blocks, atoms) + 1
    )
    bridge = jnp.where(later & (ends == chain), 1.0, 0.0).astype(bf16)
    carries = joined(dot_nt(stacked, bridge))
    arrived = jnp.zeros((1, lanes), f32)
    for d in range(devices):
        arrived = arrived + reply_ref[d * sub * fields + fields - 1 : d * sub * fields + fields, :]
    diagonal = down_rows(16, lanes) == lax.broadcasted_iota(jnp.int32, (16, lanes), 1)
    arrived = jnp.sum(jnp.where(diagonal, arrived, 0.0), 1, keepdims=True)
    padded = jnp.concatenate([chain_rows, jnp.zeros((lanes - blocks, lanes), f32)], 0)
    down_chain = jnp.transpose(padded)
    not_before = down_rows(lanes, lanes) >= lax.broadcasted_iota(jnp.int32, (lanes, lanes), 1)
    closing = chain[:, atoms - 1 :]
    sums = []
    for j in range(blocks):
        at = slice(j * lanes, (j + 1) * lanes)
        mask = not_before & (down_chain[:, j : j + 1] == chain[:, at])
        local = joined(dot_nn(stacked[:, at], jnp.where(mask, 1.0, 0.0).astype(bf16)))
        end = chain[:, (j + 1) * lanes - 1 : (j + 1) * lanes]
        carry = carries[:, j : j + 1] + jnp.where(end == closing, arrived, 0.0)
        sums.append(local + jnp.where(chain[:, at] == end, carry, 0.0))
    totals = jnp.concatenate(sums, 1)
    scale = 1.0 / (columns * jnp.sqrt(totals[12:13]))
    torques = []
    for e in range(2):
        force = [totals[6 * e + d : 6 * e + d + 1] for d in range(3)]
        lever = cross_list(positions[e], force)
        turn = 0.0
        for d in range(3):
            turn = turn + axis[d] * (totals[6 * e + 3 + d : 6 * e + 4 + d] - lever[d])
        torques.append(turn * scale)
    torque_ref[...] = jnp.concatenate(torques, 0)


def whole(count):
    return [pl.BlockSpec(memory_space=pltpu.VMEM)] * count


def settings():
    return pltpu.CompilerParams(vmem_limit_bytes=room)


def shape_of(*dims, dtype=f32):
    return jax.ShapeDtypeStruct(dims, dtype)


def swap_near(value):
    count = lax.axis_size("bx")
    return lax.ppermute(value, "bx", [(i, i ^ 1) for i in range(count)])


def swap_far(value):
    count = lax.axis_size("bx")
    pairs = []
    for i in range(1, count - 1, 2):
        pairs += [(i, i + 1), (i + 1, i)]
    return lax.ppermute(value, "bx", pairs)


def exchange(value):
    return lax.all_to_all(value, "bx", split_axis=0, concat_axis=0, tiled=True)


def shards(
    density_map,
    amplitude,
    fraction,
    torsion_axis,
    brick_owner,
    plane_offset,
    row_offset,
    column_offset,
    chain_index,
):
    planes, rows, columns = density_map.shape
    atoms = amplitude.shape[0]
    devices = lax.axis_size("bx")
    capacity = 3 * atoms // devices
    sub = -(-capacity // lanes)
    tiles = devices * sub
    grid = (planes, rows, columns)
    place = lax.axis_index("bx").astype(jnp.int32).reshape(1)
    scalar = [pl.BlockSpec(memory_space=pltpu.SMEM)]

    owner, plane, row, column, chain = (
        item.reshape(1, atoms)
        for item in (brick_owner, plane_offset, row_offset, column_offset, chain_index)
    )
    held = [pltpu.VMEM((1, atoms), jnp.int32)] * 5
    held += [pltpu.VMEM((1, atoms), f32)] + [pltpu.VMEM((3, atoms), f32)] * 2
    message, slot, home = pl.pallas_call(
        functools.partial(pack_kernel, devices, sub, planes, rows),
        out_shape=(
            shape_of(tiles * fields, lanes),
            shape_of(2, atoms, dtype=jnp.int32),
            shape_of(10, atoms),
        ),
        in_specs=[pl.BlockSpec(memory_space=pltpu.HBM)] * 8,
        out_specs=whole(3),
        scratch_shapes=held + [pltpu.SemaphoreType.DMA((8,))],
        name="pack",
    )(owner, plane, row, column, chain, amplitude.reshape(1, atoms), fraction, torsion_axis)
    message = exchange(message)

    own_shape = shape_of((planes + 3) * rows, columns)
    edge_shape = shape_of(3 * rows, columns)
    own, near, far, ordered = pl.pallas_call(
        functools.partial(density_kernel, devices, sub, *grid),
        out_shape=(own_shape, edge_shape, edge_shape, shape_of(1, dtype=jnp.int32)),
        in_specs=scalar + whole(2),
        out_specs=whole(3) + scalar,
        compiler_params=settings(),
        name="density",
    )(place, message, density_map)
    near, far = swap_near(near), swap_far(far)
    table = pltpu.VMEM((2 * (planes + 1) * rows, 2 * columns), bf16)
    moved, first, own, near, far = pl.pallas_call(
        functools.partial(middle_kernel, devices, sub, *grid),
        out_shape=(
            shape_of(tiles * fields, lanes),
            shape_of(tiles * fields, lanes),
            own_shape,
            edge_shape,
            edge_shape,
        ),
        in_specs=scalar * 2 + whole(5),
        out_specs=whole(5),
        scratch_shapes=[table],
        compiler_params=settings(),
        name="middle",
    )(place, ordered, message, own, near, far, density_map)
    near, far = swap_near(near), swap_far(far)
    reply = pl.pallas_call(
        functools.partial(last_kernel, devices, sub, *grid),
        out_shape=shape_of(tiles * fields, lanes),
        in_specs=scalar * 2 + whole(6),
        out_specs=whole(1)[0],
        scratch_shapes=[table],
        compiler_params=settings(),
        name="last",
    )(place, ordered, message, moved, first, own, near, far)
    reply = exchange(reply)
    torques, gradients = pl.pallas_call(
        functools.partial(chain_kernel, devices, sub, planes, columns),
        out_shape=(shape_of(2, atoms), shape_of(6, atoms)),
        in_specs=whole(3),
        out_specs=whole(2),
        compiler_params=settings(),
        name="chains",
    )(reply, slot, home)
    return torques, gradients


def solution(mesh):
    return jax.shard_map(
        shards,
        mesh=mesh,
        in_specs=(
            P(("grp", "bx"), None, None),
            P(("grp", "bx")),
            P(None, ("grp", "bx")),
            P(None, ("grp", "bx")),
            P(("grp", "bx"), None),
            P(("grp", "bx")),
            P(("grp", "bx")),
            P(("grp", "bx")),
            P(("grp", "bx")),
        ),
        out_specs=(P(None, ("grp", "bx")), P(None, ("grp", "bx"))),
        check_vma=False,
    )
```

```python
import functools

import jax
import jax.numpy as jnp
from jax import lax
from jax.experimental import pallas as pl
from jax.experimental.pallas import tpu as pltpu
from jax.sharding import PartitionSpec as P

side_tap = 0.25
middle_tap = 0.5
probe_step = 0.2
lanes = 128
fields = 8
f32, bf16 = jnp.float32, jnp.bfloat16
room = 48 * 1024 * 1024


def dot_nt(left, right):
    return lax.dot_general(left, right, (((1,), (1,)), ((), ())), preferred_element_type=f32)


def dot_nn(left, right):
    return lax.dot_general(left, right, (((1,), (0,)), ((), ())), preferred_element_type=f32)


def halves(x):
    high = x.astype(bf16)
    return high, (x - high.astype(f32)).astype(bf16)


def thirds(x):
    high, rest = x.astype(bf16), None
    rest = x - high.astype(f32)
    middle = rest.astype(bf16)
    return high, middle, (rest - middle.astype(f32)).astype(bf16)


def down_rows(count, width):
    return lax.broadcasted_iota(jnp.int32, (count, width), 0)


def spread(row, count):
    tile = jnp.broadcast_to(row, (16, row.shape[1])).astype(bf16)
    return jnp.concatenate([tile] * (count // 16), 0)


def counting(count, width):
    part = down_rows(count, lanes).astype(f32).astype(bf16)
    return jnp.concatenate([part] * (width // lanes), 1)


def pack_kernel(devices, sub, planes, rows, *refs):
    hbm, (message_ref, slot_ref, home_ref), held = refs[:8], refs[8:11], refs[11:19]
    semaphores = refs[19]
    copies = [
        pltpu.make_async_copy(source, target, semaphores.at[i])
        for i, (source, target) in enumerate(zip(hbm, held))
    ]
    for copy in copies:
        copy.start()
    for copy in copies:
        copy.wait()
    owner_ref, plane_ref, row_ref, column_ref, chain_ref, amp_ref, frac_ref, axis_ref = held
    atoms = owner_ref.shape[1]
    blocks = atoms // lanes
    tiles = devices * sub
    owner, plane = owner_ref[...], plane_ref[...]
    chain = chain_ref[...].astype(f32)
    home_ref[0:1, :] = (owner * planes + plane).astype(f32)
    home_ref[1:2, :] = row_ref[...].astype(f32)
    home_ref[2:3, :] = column_ref[...].astype(f32)
    home_ref[3:6, :] = frac_ref[...]
    home_ref[6:7, :] = chain
    home_ref[7:10, :] = axis_ref[...]
    groups = planes * devices
    mine = down_rows(groups, atoms) == plane * devices + owner
    onehot = jnp.where(mine, 1.0, 0.0)
    stacked = jnp.concatenate(
        [onehot[:, j * lanes : (j + 1) * lanes] for j in range(blocks)], 0
    ).astype(bf16)
    k = lax.broadcasted_iota(jnp.int32, (lanes, 2 * lanes), 0)
    a = lax.broadcasted_iota(jnp.int32, (lanes, 2 * lanes), 1)
    before = jnp.where((k < a) | (a >= lanes), 1.0, 0.0).astype(bf16)
    counts = dot_nn(stacked, before)
    parts = [counts[j * groups : (j + 1) * groups] for j in range(blocks)]
    total = parts[0][:, lanes:]
    for part in parts[1:]:
        total = total + part[:, lanes:]
    held_by = [total[p * devices : (p + 1) * devices] for p in range(planes)]
    half = planes // 2
    none = jnp.zeros((devices, lanes), f32)
    offsets = [sum(held_by[:p], none) for p in range(half)]
    offsets += [sum(held_by[p + 1 :], none) for p in range(half, planes)]
    running = jnp.concatenate(offsets, 0)
    ranks = []
    for j, part in enumerate(parts):
        here = onehot[:, j * lanes : (j + 1) * lanes]
        ranks.append(jnp.sum((part[:, :lanes] + running) * here, 0, keepdims=True))
        running = running + part[:, lanes:]
    rank = jnp.concatenate(ranks, 1).astype(jnp.int32)
    rank = jnp.where(plane < half, rank, sub * lanes - 1 - rank)
    tile = owner * sub + lax.shift_right_logical(rank, 7)
    lane = rank & (lanes - 1)
    slot_ref[...] = jnp.concatenate([tile, lane], 0)
    values = jnp.concatenate(
        [
            (plane * rows + row_ref[...]).astype(f32),
            column_ref[...].astype(f32),
            frac_ref[...],
            amp_ref[...],
            chain,
            jnp.zeros((1, atoms), f32),
        ],
        0,
    )
    pieces = [piece.astype(f32) for piece in halves(values)]
    width = 512
    pair = lax.shift_right_logical(tile, 1)
    inside = (tile & 1) * lanes + lane
    total = None
    for c in range(atoms // width):
        at = slice(c * width, (c + 1) * width)
        spot = jnp.where(down_rows(2 * lanes, width) == inside[:, at], 1.0, 0.0).astype(bf16)
        which = jnp.broadcast_to(pair[:, at], (fields, width))
        picks = [which == t for t in range(tiles // 2)]
        left = jnp.concatenate(
            [jnp.where(pick, piece[:, at], 0.0) for piece in pieces for pick in picks], 0
        ).astype(bf16)
        one = dot_nt(left, spot)
        one = one[: one.shape[0] // 2] + one[one.shape[0] // 2 :]
        total = one if total is None else total + one
    for t in range(tiles):
        message_ref[t * fields : (t + 1) * fields, :] = total[
            t // 2 * fields : (t // 2 + 1) * fields, t % 2 * lanes : (t % 2 + 1) * lanes
        ]
    last = jnp.broadcast_to(chain[:, atoms - 1 :], (1, lanes))
    for b in range(devices):
        message_ref[b * sub * fields + fields - 1 : b * sub * fields + fields, :] = last
    if sorted_buckets(planes, sub):
        fits = 1.0
        lower, upper = held_by[0] + held_by[1], held_by[2] + held_by[3]
        limits = (lower, 2.0 * lanes), (upper, 2.0 * lanes), (held_by[0], lanes), (held_by[3], lanes)
        for amount, limit in limits:
            fits = fits * jnp.where(amount <= limit, 1.0, 0.0)
        for b in range(devices):
            row = (b * sub + 1) * fields + fields - 1
            message_ref[row : row + 1, :] = fits[b : b + 1]


def sorted_buckets(planes, sub):
    return planes == 4 and sub == 3


def neighbours_of(state, rows, columns):
    cell, column = state[0:1], state[1:2]
    plane = jnp.floor(cell * (1.0 / rows))
    row = cell - plane * rows
    next_row = jnp.where(row == rows - 1.0, 0.0, row + 1.0)
    next_column = jnp.where(column == columns - 1.0, 0.0, column + 1.0)
    return plane, row, next_row, column, next_column


def density_part(state, base, span, rows, columns):
    width = state.shape[1]
    plane, row, next_row, column, next_column = neighbours_of(state, rows, columns)
    fx, fy, fz, amplitude = (state[2 + i : 3 + i] for i in range(4))
    zero = jnp.zeros((), bf16)
    steps = counting(columns, width)
    here, there = steps == spread(column, columns), steps == spread(next_column, columns)

    def columns_of(near, far):
        return jnp.where(here, spread(near, columns), jnp.where(there, spread(far, columns), zero))

    near, far = halves(1.0 - fz), halves(fz)
    right_high = columns_of(near[0].astype(f32), far[0].astype(f32))
    right_low = columns_of(near[1].astype(f32), far[1].astype(f32))
    level = down_rows(fields, width).astype(f32) + float(base)
    along = amplitude * jnp.where(level == plane, 1.0 - fx, jnp.where(level == plane + 1.0, fx, 0.0))
    near, far = halves(along * (1.0 - fy)), halves(along * fy)
    steps = counting(rows, width)
    here, there = steps == spread(row, rows), steps == spread(next_row, rows)
    lefts = []
    for grade in range(2):
        first, second = near[grade].astype(f32), far[grade].astype(f32)
        lefts.append(
            jnp.concatenate(
                [
                    jnp.where(
                        here,
                        spread(first[p : p + 1], rows),
                        jnp.where(there, spread(second[p : p + 1], rows), zero),
                    )
                    for p in range(span + 1)
                ],
                0,
            )
        )
    both = dot_nt(jnp.concatenate(lefts, 0), right_high)
    count = lefts[0].shape[0]
    return both[:count] + both[count:] + dot_nt(lefts[0], right_low)


def gradient_part(state, table_ref, base, span, planes, rows, columns):
    width = state.shape[1]
    plane, row, next_row, column, _ = neighbours_of(state, rows, columns)
    fx, fy, fz, amplitude = (state[2 + i : 3 + i] for i in range(4))
    pair = jnp.floor(column * 0.5)
    spot = jnp.where(
        counting(columns // 2, width) == spread(pair, columns // 2),
        jnp.ones((), bf16),
        jnp.zeros((), bf16),
    )
    count = (span + 1) * rows
    starts = [(v * (planes + 1) + base) * rows for v in range(3)]
    table = jnp.concatenate([table_ref[start : start + count, :] for start in starts], 0)
    sampled = dot_nn(table, jnp.concatenate([spot, spot], 0))

    def eight(x):
        return jnp.broadcast_to(x, (8, width))

    level = down_rows(8, width).astype(f32)
    at_plane = [eight(plane) == float(base + p) for p in range(span)]
    eighths = [jnp.floor(at * 0.125) for at in (row, next_row)]
    at_eighth = [[eight(part) == float(j) for j in range(rows // 8)] for part in eighths]
    corner = {}
    odd = eight(column - 2.0 * pair) > 0.5
    picked = {}
    for v in range(3):
        for e0 in range(2):
            for j in range(rows // 8):
                at = (v * (span + 1) + e0) * rows + 8 * j
                pick = sampled[at : at + 8]
                for p in range(1, span):
                    pick = jnp.where(at_plane[p], sampled[at + p * rows : at + p * rows + 8], pick)
                picked[v, e0, j] = pick
    for e2 in range(2):
        for e0 in range(2):
            chosen = [
                jnp.where(odd, picked[e2 + 1, e0, j], picked[e2, e0, j]) for j in range(rows // 8)
            ]
            for e1 in range(2):
                pick = chosen[0]
                for j in range(1, rows // 8):
                    pick = jnp.where(at_eighth[e1][j], chosen[j], pick)
                corner[e0, e1, e2] = pick
    fx, fz = eight(fx), eight(fz)
    weights = (amplitude * (1.0 - fy), amplitude * fy)
    gx = gy = gz = 0.0
    for e1 in range(2):
        here = level == eight((row, next_row)[e1] - 8.0 * eighths[e1])
        weight = jnp.where(here, eight(weights[e1]), 0.0)
        signed = jnp.where(here, eight(amplitude), 0.0)
        drop = [corner[e0, e1, 1] - corner[e0, e1, 0] for e0 in range(2)]
        value = [corner[e0, e1, 0] + fz * drop[e0] for e0 in range(2)]
        slope = value[1] - value[0]
        gx = gx + weight * slope
        gz = gz + weight * (drop[0] + fx * (drop[1] - drop[0]))
        middle = signed * (value[0] + fx * slope)
        gy = gy + middle if e1 else gy - middle
    return jnp.concatenate([jnp.sum(g, 0, keepdims=True) for g in (gx, gy, gz)], 0)


def blur_sheet(sheet):
    rows, columns = sheet.shape
    sheet = middle_tap * sheet + side_tap * (pltpu.roll(sheet, 1, 0) + pltpu.roll(sheet, rows - 1, 0))
    return middle_tap * sheet + side_tap * (
        pltpu.roll(sheet, 1, 1) + pltpu.roll(sheet, columns - 1, 1)
    )


def blur_along(sheets):
    return [
        middle_tap * sheets[i] + side_tap * (sheets[i - 1] + sheets[i + 1])
        for i in range(1, len(sheets) - 1)
    ]


def edges(place_ref, devices):
    not_first = jnp.where(place_ref[0] == 0, 0.0, 1.0)
    not_last = jnp.where(place_ref[0] == devices - 1, 0.0, 1.0)
    return not_first, not_last


def share_misfit(place_ref, devices, planes, rows, density, map_ref, own_ref, near_ref, far_ref):
    _, not_last = edges(place_ref, devices)
    density[planes] = density[planes] * not_last
    density = [blur_sheet(sheet) for sheet in density]
    parts = [side_tap * density[0], middle_tap * density[0] + side_tap * density[1]]
    parts += blur_along(density)
    parts += [side_tap * density[planes - 1] + middle_tap * density[planes]]
    parts += [side_tap * density[planes]]
    for p in range(planes):
        parts[p + 1] = parts[p + 1] - map_ref[p]
    for p in range(planes + 3):
        own_ref[p * rows : (p + 1) * rows, :] = parts[p]
    even = place_ref[0] % 2 == 0
    for p in range(3):
        up, down = parts[planes + p], parts[p]
        near_ref[p * rows : (p + 1) * rows, :] = jnp.where(even, up, down)
        far_ref[p * rows : (p + 1) * rows, :] = jnp.where(even, down, up)


def make_table(place_ref, devices, planes, rows, columns, own_ref, near_ref, far_ref, table_ref):
    not_first, not_last = edges(place_ref, devices)
    misfit = [own_ref[p * rows : (p + 1) * rows, :] for p in range(planes + 3)]
    even = place_ref[0] % 2 == 0
    for p in range(3):
        near = near_ref[p * rows : (p + 1) * rows, :]
        far = far_ref[p * rows : (p + 1) * rows, :]
        misfit[p] = misfit[p] + jnp.where(even, far, near)
        misfit[planes + p] = misfit[planes + p] + jnp.where(even, near, far)
    misfit[0] = misfit[0] * not_first
    misfit[planes + 1] = misfit[planes + 1] * not_last
    misfit[planes + 2] = misfit[planes + 2] * not_last
    pulled = [blur_sheet(sheet) for sheet in blur_along(misfit)]
    pulled[planes] = pulled[planes] * not_last
    half = columns // 2
    source = down_rows(columns, 3 * half)
    target = lax.broadcasted_iota(jnp.int32, (columns, 3 * half), 1)
    turn = target // half
    spread = jnp.where(source == (2 * (target - half * turn) + turn) % columns, 1.0, 0.0).astype(bf16)
    for grade, piece in enumerate(halves(jnp.concatenate(pulled, 0))):
        sorted_columns = dot_nn(piece, spread).astype(bf16)
        count = (planes + 1) * rows
        for v in range(3):
            table_ref[v * count : (v + 1) * count, grade * half : (grade + 1) * half] = (
                sorted_columns[:, v * half : (v + 1) * half]
            )


def load_tiles(ref, tiles):
    return jnp.concatenate([ref[t * fields : (t + 1) * fields, :] for t in tiles], 1)


def store_tiles(ref, tiles, value):
    for i, t in enumerate(tiles):
        ref[t * fields : (t + 1) * fields, :] = value[:, i * lanes : (i + 1) * lanes]


def chunks(devices, sub, planes, ordered):
    if ordered:
        return [([b * sub + k for b in range(devices)], k, 2) for k in range(sub)]
    tiles = devices * sub
    batch = max(b for b in range(1, 25) if tiles % b == 0)
    return [(range(i, i + batch), 0, planes) for i in range(0, tiles, batch)]


def in_order(message_ref, devices, sub):
    rows = [(b * sub + 1) * fields + fields - 1 for b in range(devices)]
    flags = jnp.concatenate([message_ref[row : row + 1, :] for row in rows], 0)
    return jnp.min(flags) > 0.5


def either(ordered_ref, planes, sub, work):
    if not sorted_buckets(planes, sub):
        work(False)
        return
    ordered = ordered_ref[0] == 1

    @pl.when(ordered)
    def _():
        work(True)

    @pl.when(jnp.logical_not(ordered))
    def _():
        work(False)


def add_density(sheets, state, base, span, rows, columns):
    part = density_part(state, base, span, rows, columns)
    for p in range(span + 1):
        sheet = part[p * rows : (p + 1) * rows]
        sheets[base + p] = sheet if sheets[base + p] is None else sheets[base + p] + sheet


def density_kernel(
    devices, sub, planes, rows, columns, place_ref, message_ref, map_ref, own_ref, near_ref, far_ref,
    ordered_ref,
):
    if sorted_buckets(planes, sub):
        ordered_ref[0] = jnp.where(in_order(message_ref, devices, sub), 1, 0)
    else:
        ordered_ref[0] = 0

    def work(ordered):
        sheets = [None] * (planes + 1)
        for tiles, base, span in chunks(devices, sub, planes, ordered):
            add_density(sheets, load_tiles(message_ref, tiles), base, span, rows, columns)
        share_misfit(place_ref, devices, planes, rows, sheets, map_ref, own_ref, near_ref, far_ref)

    either(ordered_ref, planes, sub, work)


def middle_kernel(
    devices, sub, planes, rows, columns, place_ref, ordered_ref, message_ref, was_ref, from_near_ref,
    from_far_ref, map_ref, moved_ref, first_ref, own_ref, near_ref, far_ref, table_ref,
):
    make_table(
        place_ref, devices, planes, rows, columns, was_ref, from_near_ref, from_far_ref, table_ref
    )

    def work(ordered):
        sheets, waiting = [None] * (planes + 1), None
        for tiles, base, span in chunks(devices, sub, planes, ordered):
            state = load_tiles(message_ref, tiles)
            gradient = gradient_part(state, table_ref, base, span, planes, rows, columns)
            moved = jnp.concatenate(
                [state[0:2], state[2:5] - probe_step * jnp.tanh(gradient), state[5:8]], 0
            )
            store_tiles(moved_ref, tiles, moved)
            store_tiles(
                first_ref, tiles,
                jnp.concatenate([gradient, jnp.zeros((5, gradient.shape[1]), f32)], 0),
            )
            if waiting is not None:
                add_density(sheets, *waiting, rows, columns)
            waiting = (moved, base, span)
        add_density(sheets, *waiting, rows, columns)
        share_misfit(place_ref, devices, planes, rows, sheets, map_ref, own_ref, near_ref, far_ref)

    either(ordered_ref, planes, sub, work)


def cross_list(left, right):
    return [
        left[1] * right[2] - left[2] * right[1],
        left[2] * right[0] - left[0] * right[2],
        left[0] * right[1] - left[1] * right[0],
    ]


def last_kernel(
    devices, sub, planes, rows, columns, place_ref, ordered_ref, message_ref, moved_ref, first_ref,
    was_ref, from_near_ref, from_far_ref, reply_ref, table_ref, terms_ref,
):
    make_table(
        place_ref, devices, planes, rows, columns, was_ref, from_near_ref, from_far_ref, table_ref
    )
    tiles = devices * sub

    def work(ordered):
        for group, base, span in chunks(devices, sub, planes, ordered):
            first = load_tiles(first_ref, group)[0:3]
            moved = load_tiles(moved_ref, group)
            second = gradient_part(moved, table_ref, base, span, planes, rows, columns)
            rest = jnp.zeros((2, second.shape[1]), f32)
            store_tiles(reply_ref, group, jnp.concatenate([first, second, rest], 0))

    either(ordered_ref, planes, sub, work)

    def field(ref, f):
        return ref[pl.ds(f, tiles, stride=fields), :]

    cell = field(message_ref, 0)
    plane = jnp.floor(cell * (1.0 / rows))
    cells = (plane + (place_ref[0] * planes).astype(f32), cell - plane * rows, field(message_ref, 1))
    terms = []
    for e, ref in enumerate((message_ref, moved_ref)):
        g = [field(reply_ref, 3 * e + d) for d in range(3)]
        terms += g + cross_list([cells[d] + field(ref, 2 + d) for d in range(3)], g)
    terms.append(jnp.where(field(message_ref, 5) > 0.0, 1.0, 0.0))
    terms += [jnp.zeros_like(cell)] * 3
    for i, term in enumerate(terms):
        terms_ref[pl.ds(i, tiles, stride=16), :] = term
    last_of = jnp.concatenate(
        [
            message_ref[d * sub * fields + fields - 1 : d * sub * fields + fields, :]
            for d in range(devices)
        ],
        0,
    )
    receiver = down_rows(devices, lanes)
    sums = jnp.zeros((devices, 16), f32)
    batch = 16
    for i in range(0, tiles, batch):
        chosen = [
            jnp.where(
                (receiver < t // sub) & (last_of == message_ref[t * fields + 6 : t * fields + 7, :]),
                1.0,
                0.0,
            )
            for t in range(i, i + batch)
        ]
        chosen = jnp.concatenate(chosen, 1).astype(bf16)
        block = jnp.concatenate([terms_ref[t * 16 : (t + 1) * 16, :] for t in range(i, i + batch)], 1)
        sums = sums + sum(dot_nt(chosen, piece) for piece in thirds(block))
    sums = jnp.concatenate([sums, jnp.zeros((devices, lanes - 16), f32)], 1)
    for d in range(devices):
        reply_ref[d * sub * fields + fields - 1 : d * sub * fields + fields, :] = sums[d : d + 1]


def chain_kernel(
    devices, sub, planes, columns, reply_ref, slot_ref, home_ref, torque_ref, gradient_ref
):
    atoms = slot_ref.shape[1]
    blocks = atoms // lanes
    tiles = devices * sub
    high, low = halves(reply_ref[...])
    left = jnp.concatenate([high, low], 1)
    width = 512
    found = []
    for c in range(atoms // width):
        at = slice(c * width, (c + 1) * width)
        spot = jnp.where(down_rows(lanes, width) == slot_ref[1:2, at], 1.0, 0.0).astype(bf16)
        picked = dot_nn(left, jnp.concatenate([spot, spot], 0))
        which = jnp.broadcast_to(slot_ref[0:1, at], (fields, width))
        total = jnp.zeros((fields, width), f32)
        for t in range(tiles):
            total = jnp.where(which == t, picked[t * fields : (t + 1) * fields], total)
        found.append(total)
    gradients = jnp.concatenate(found, 1)[0:6]
    gradient_ref[...] = gradients
    fraction = home_ref[3:6, :]
    moved = fraction - probe_step * jnp.tanh(gradients[0:3])
    base = [home_ref[d : d + 1, :] for d in range(3)]
    axis = [home_ref[7 + d : 8 + d, :] for d in range(3)]
    positions = [[base[d] + offset[d : d + 1] for d in range(3)] for offset in (fraction, moved)]
    pieces = []
    for e in range(2):
        g = [gradients[3 * e + d : 3 * e + d + 1] for d in range(3)]
        pieces += g + cross_list(positions[e], g)
    pieces.append(jnp.ones((1, atoms), f32))
    pieces.append(jnp.zeros((3, atoms), f32))
    stacked = jnp.concatenate(thirds(jnp.concatenate(pieces, 0)), 0)

    def joined(x):
        return x[0:16] + x[16:32] + x[32:48]

    chain = home_ref[6:7, :]
    chain_rows = jnp.concatenate([chain[:, j * lanes : (j + 1) * lanes] for j in range(blocks)], 0)
    ends = jnp.broadcast_to(chain_rows[:, lanes - 1 :], (blocks, atoms))
    later = lax.broadcasted_iota(jnp.int32, (blocks, atoms), 1) >= lanes * (
        down_rows(blocks, atoms) + 1
    )
    bridge = jnp.where(later & (ends == chain), 1.0, 0.0).astype(bf16)
    carries = joined(dot_nt(stacked, bridge))
    arrived = jnp.zeros((1, lanes), f32)
    for d in range(devices):
        arrived = arrived + reply_ref[d * sub * fields + fields - 1 : d * sub * fields + fields, :]
    diagonal = down_rows(16, lanes) == lax.broadcasted_iota(jnp.int32, (16, lanes), 1)
    arrived = jnp.sum(jnp.where(diagonal, arrived, 0.0), 1, keepdims=True)
    padded = jnp.concatenate([chain_rows, jnp.zeros((lanes - blocks, lanes), f32)], 0)
    down_chain = jnp.transpose(padded)
    not_before = down_rows(lanes, lanes) >= lax.broadcasted_iota(jnp.int32, (lanes, lanes), 1)
    closing = chain[:, atoms - 1 :]
    sums = []
    for j in range(blocks):
        at = slice(j * lanes, (j + 1) * lanes)
        mask = not_before & (down_chain[:, j : j + 1] == chain[:, at])
        local = joined(dot_nn(stacked[:, at], jnp.where(mask, 1.0, 0.0).astype(bf16)))
        end = chain[:, (j + 1) * lanes - 1 : (j + 1) * lanes]
        carry = carries[:, j : j + 1] + jnp.where(end == closing, arrived, 0.0)
        sums.append(local + jnp.where(chain[:, at] == end, carry, 0.0))
    totals = jnp.concatenate(sums, 1)
    scale = 1.0 / (columns * jnp.sqrt(totals[12:13]))
    torques = []
    for e in range(2):
        force = [totals[6 * e + d : 6 * e + d + 1] for d in range(3)]
        lever = cross_list(positions[e], force)
        turn = 0.0
        for d in range(3):
            turn = turn + axis[d] * (totals[6 * e + 3 + d : 6 * e + 4 + d] - lever[d])
        torques.append(turn * scale)
    torque_ref[...] = jnp.concatenate(torques, 0)


def whole(count):
    return [pl.BlockSpec(memory_space=pltpu.VMEM)] * count


def settings():
    return pltpu.CompilerParams(vmem_limit_bytes=room)


def shape_of(*dims, dtype=f32):
    return jax.ShapeDtypeStruct(dims, dtype)


def swap_near(value):
    count = lax.axis_size("bx")
    return lax.ppermute(value, "bx", [(i, i ^ 1) for i in range(count)])


def swap_far(value):
    count = lax.axis_size("bx")
    pairs = []
    for i in range(1, count - 1, 2):
        pairs += [(i, i + 1), (i + 1, i)]
    return lax.ppermute(value, "bx", pairs)


def exchange(value):
    return lax.all_to_all(value, "bx", split_axis=0, concat_axis=0, tiled=True)


def shards(
    density_map,
    amplitude,
    fraction,
    torsion_axis,
    brick_owner,
    plane_offset,
    row_offset,
    column_offset,
    chain_index,
):
    planes, rows, columns = density_map.shape
    atoms = amplitude.shape[0]
    devices = lax.axis_size("bx")
    capacity = 3 * atoms // devices
    sub = -(-capacity // lanes)
    tiles = devices * sub
    grid = (planes, rows, columns)
    place = lax.axis_index("bx").astype(jnp.int32).reshape(1)
    scalar = [pl.BlockSpec(memory_space=pltpu.SMEM)]

    owner, plane, row, column, chain = (
        item.reshape(1, atoms)
        for item in (brick_owner, plane_offset, row_offset, column_offset, chain_index)
    )
    held = [pltpu.VMEM((1, atoms), jnp.int32)] * 5
    held += [pltpu.VMEM((1, atoms), f32)] + [pltpu.VMEM((3, atoms), f32)] * 2
    message, slot, home = pl.pallas_call(
        functools.partial(pack_kernel, devices, sub, planes, rows),
        out_shape=(
            shape_of(tiles * fields, lanes),
            shape_of(2, atoms, dtype=jnp.int32),
            shape_of(10, atoms),
        ),
        in_specs=[pl.BlockSpec(memory_space=pltpu.HBM)] * 8,
        out_specs=whole(3),
        scratch_shapes=held + [pltpu.SemaphoreType.DMA((8,))],
        name="pack",
    )(owner, plane, row, column, chain, amplitude.reshape(1, atoms), fraction, torsion_axis)
    message = exchange(message)

    own_shape = shape_of((planes + 3) * rows, columns)
    edge_shape = shape_of(3 * rows, columns)
    own, near, far, ordered = pl.pallas_call(
        functools.partial(density_kernel, devices, sub, *grid),
        out_shape=(own_shape, edge_shape, edge_shape, shape_of(1, dtype=jnp.int32)),
        in_specs=scalar + whole(2),
        out_specs=whole(3) + scalar,
        compiler_params=settings(),
        name="density",
    )(place, message, density_map)
    near, far = swap_near(near), swap_far(far)
    table = pltpu.VMEM((3 * (planes + 1) * rows, columns), bf16)
    moved, first, own, near, far = pl.pallas_call(
        functools.partial(middle_kernel, devices, sub, *grid),
        out_shape=(
            shape_of(tiles * fields, lanes),
            shape_of(tiles * fields, lanes),
            own_shape,
            edge_shape,
            edge_shape,
        ),
        in_specs=scalar * 2 + whole(5),
        out_specs=whole(5),
        scratch_shapes=[table],
        compiler_params=settings(),
        name="middle",
    )(place, ordered, message, own, near, far, density_map)
    near, far = swap_near(near), swap_far(far)
    reply = pl.pallas_call(
        functools.partial(last_kernel, devices, sub, *grid),
        out_shape=shape_of(tiles * fields, lanes),
        in_specs=scalar * 2 + whole(6),
        out_specs=whole(1)[0],
        scratch_shapes=[table, pltpu.VMEM((tiles * 16, lanes), f32)],
        compiler_params=settings(),
        name="last",
    )(place, ordered, message, moved, first, own, near, far)
    reply = exchange(reply)
    torques, gradients = pl.pallas_call(
        functools.partial(chain_kernel, devices, sub, planes, columns),
        out_shape=(shape_of(2, atoms), shape_of(6, atoms)),
        in_specs=whole(3),
        out_specs=whole(2),
        compiler_params=settings(),
        name="chains",
    )(reply, slot, home)
    return torques, gradients


def solution(mesh):
    return jax.shard_map(
        shards,
        mesh=mesh,
        in_specs=(
            P(("grp", "bx"), None, None),
            P(("grp", "bx")),
            P(None, ("grp", "bx")),
            P(None, ("grp", "bx")),
            P(("grp", "bx"), None),
            P(("grp", "bx")),
            P(("grp", "bx")),
            P(("grp", "bx")),
            P(("grp", "bx")),
        ),
        out_specs=(P(None, ("grp", "bx")), P(None, ("grp", "bx"))),
        check_vma=False,
    )
```

```python
import functools

import jax
import jax.numpy as jnp
from jax import lax
from jax.experimental import pallas as pl
from jax.experimental.pallas import tpu as pltpu
from jax.sharding import PartitionSpec as P

side_tap = 0.25
middle_tap = 0.5
probe_step = 0.2
lanes = 128
fields = 8
f32, bf16 = jnp.float32, jnp.bfloat16
room = 48 * 1024 * 1024


def dot_nt(left, right):
    return lax.dot_general(left, right, (((1,), (1,)), ((), ())), preferred_element_type=f32)


def dot_nn(left, right):
    return lax.dot_general(left, right, (((1,), (0,)), ((), ())), preferred_element_type=f32)


def halves(x):
    high = x.astype(bf16)
    return high, (x - high.astype(f32)).astype(bf16)


def thirds(x):
    high, rest = x.astype(bf16), None
    rest = x - high.astype(f32)
    middle = rest.astype(bf16)
    return high, middle, (rest - middle.astype(f32)).astype(bf16)


def down_rows(count, width):
    return lax.broadcasted_iota(jnp.int32, (count, width), 0)


def spread(row, count):
    tile = jnp.broadcast_to(row, (16, row.shape[1])).astype(bf16)
    return jnp.concatenate([tile] * (count // 16), 0)


def counting(count, width):
    part = down_rows(count, lanes).astype(f32).astype(bf16)
    return jnp.concatenate([part] * (width // lanes), 1)


def pack_kernel(devices, sub, planes, rows, *refs):
    hbm, (message_ref, slot_ref, home_ref), held = refs[:8], refs[8:11], refs[11:19]
    semaphores = refs[19]
    copies = [
        pltpu.make_async_copy(source, target, semaphores.at[i])
        for i, (source, target) in enumerate(zip(hbm, held))
    ]
    for copy in copies:
        copy.start()
    for copy in copies[:2]:
        copy.wait()
    owner_ref, plane_ref, row_ref, column_ref, chain_ref, amp_ref, frac_ref, axis_ref = held
    atoms = owner_ref.shape[1]
    blocks = atoms // lanes
    tiles = devices * sub
    owner, plane = owner_ref[...], plane_ref[...]
    home_ref[0:1, :] = (owner * planes + plane).astype(f32)
    groups = planes * devices
    mine = down_rows(groups, atoms) == plane * devices + owner
    onehot = jnp.where(mine, 1.0, 0.0)
    stacked = jnp.concatenate(
        [onehot[:, j * lanes : (j + 1) * lanes] for j in range(blocks)], 0
    ).astype(bf16)
    k = lax.broadcasted_iota(jnp.int32, (lanes, 2 * lanes), 0)
    a = lax.broadcasted_iota(jnp.int32, (lanes, 2 * lanes), 1)
    before = jnp.where((k < a) | (a >= lanes), 1.0, 0.0).astype(bf16)
    counts = dot_nn(stacked, before)
    parts = [counts[j * groups : (j + 1) * groups] for j in range(blocks)]
    total = parts[0][:, lanes:]
    for part in parts[1:]:
        total = total + part[:, lanes:]
    held_by = [total[p * devices : (p + 1) * devices] for p in range(planes)]
    half = planes // 2
    none = jnp.zeros((devices, lanes), f32)
    offsets = [sum(held_by[:p], none) for p in range(half)]
    offsets += [sum(held_by[p + 1 :], none) for p in range(half, planes)]
    running = jnp.concatenate(offsets, 0)
    ranks = []
    for j, part in enumerate(parts):
        here = onehot[:, j * lanes : (j + 1) * lanes]
        ranks.append(jnp.sum((part[:, :lanes] + running) * here, 0, keepdims=True))
        running = running + part[:, lanes:]
    rank = jnp.concatenate(ranks, 1).astype(jnp.int32)
    rank = jnp.where(plane < half, rank, sub * lanes - 1 - rank)
    tile = owner * sub + lax.shift_right_logical(rank, 7)
    lane = rank & (lanes - 1)
    slot_ref[...] = jnp.concatenate([tile, lane], 0)
    for copy in copies[2:]:
        copy.wait()
    chain = chain_ref[...].astype(f32)
    home_ref[1:2, :] = row_ref[...].astype(f32)
    home_ref[2:3, :] = column_ref[...].astype(f32)
    home_ref[3:6, :] = frac_ref[...]
    home_ref[6:7, :] = chain
    home_ref[7:10, :] = axis_ref[...]
    values = jnp.concatenate(
        [
            (plane * rows + row_ref[...]).astype(f32),
            column_ref[...].astype(f32),
            frac_ref[...],
            amp_ref[...],
            chain,
            jnp.zeros((1, atoms), f32),
        ],
        0,
    )
    pieces = [piece.astype(f32) for piece in halves(values)]
    width = 512
    pair = lax.shift_right_logical(tile, 1)
    inside = (tile & 1) * lanes + lane
    total = None
    for c in range(atoms // width):
        at = slice(c * width, (c + 1) * width)
        spot = jnp.where(down_rows(2 * lanes, width) == inside[:, at], 1.0, 0.0).astype(bf16)
        which = jnp.broadcast_to(pair[:, at], (fields, width))
        picks = [which == t for t in range(tiles // 2)]
        left = jnp.concatenate(
            [jnp.where(pick, piece[:, at], 0.0) for piece in pieces for pick in picks], 0
        ).astype(bf16)
        one = dot_nt(left, spot)
        one = one[: one.shape[0] // 2] + one[one.shape[0] // 2 :]
        total = one if total is None else total + one
    for t in range(tiles):
        message_ref[t * fields : (t + 1) * fields, :] = total[
            t // 2 * fields : (t // 2 + 1) * fields, t % 2 * lanes : (t % 2 + 1) * lanes
        ]
    last = jnp.broadcast_to(chain[:, atoms - 1 :], (1, lanes))
    for b in range(devices):
        message_ref[b * sub * fields + fields - 1 : b * sub * fields + fields, :] = last
    if sorted_buckets(planes, sub):
        fits = 1.0
        lower, upper = held_by[0] + held_by[1], held_by[2] + held_by[3]
        limits = (lower, 2.0 * lanes), (upper, 2.0 * lanes), (held_by[0], lanes), (held_by[3], lanes)
        for amount, limit in limits:
            fits = fits * jnp.where(amount <= limit, 1.0, 0.0)
        for b in range(devices):
            row = (b * sub + 1) * fields + fields - 1
            message_ref[row : row + 1, :] = fits[b : b + 1]


def sorted_buckets(planes, sub):
    return planes == 4 and sub == 3


def neighbours_of(state, rows, columns):
    cell, column = state[0:1], state[1:2]
    plane = jnp.floor(cell * (1.0 / rows))
    row = cell - plane * rows
    next_row = jnp.where(row == rows - 1.0, 0.0, row + 1.0)
    next_column = jnp.where(column == columns - 1.0, 0.0, column + 1.0)
    return plane, row, next_row, column, next_column


def density_part(state, base, span, rows, columns):
    width = state.shape[1]
    plane, row, next_row, column, next_column = neighbours_of(state, rows, columns)
    fx, fy, fz, amplitude = (state[2 + i : 3 + i] for i in range(4))
    zero = jnp.zeros((), bf16)
    steps = counting(columns, width)
    here, there = steps == spread(column, columns), steps == spread(next_column, columns)

    def columns_of(near, far):
        return jnp.where(here, spread(near, columns), jnp.where(there, spread(far, columns), zero))

    near, far = halves(1.0 - fz), halves(fz)
    right_high = columns_of(near[0].astype(f32), far[0].astype(f32))
    right_low = columns_of(near[1].astype(f32), far[1].astype(f32))
    level = down_rows(fields, width).astype(f32) + float(base)
    along = amplitude * jnp.where(level == plane, 1.0 - fx, jnp.where(level == plane + 1.0, fx, 0.0))
    near, far = halves(along * (1.0 - fy)), halves(along * fy)
    steps = counting(rows, width)
    here, there = steps == spread(row, rows), steps == spread(next_row, rows)
    lefts = []
    for grade in range(2):
        first, second = near[grade].astype(f32), far[grade].astype(f32)
        lefts.append(
            jnp.concatenate(
                [
                    jnp.where(
                        here,
                        spread(first[p : p + 1], rows),
                        jnp.where(there, spread(second[p : p + 1], rows), zero),
                    )
                    for p in range(span + 1)
                ],
                0,
            )
        )
    both = dot_nt(jnp.concatenate(lefts, 0), right_high)
    count = lefts[0].shape[0]
    return both[:count] + both[count:] + dot_nt(lefts[0], right_low)


def gradient_part(state, table_ref, base, span, planes, rows, columns):
    width = state.shape[1]
    plane, row, next_row, column, _ = neighbours_of(state, rows, columns)
    fx, fy, fz, amplitude = (state[2 + i : 3 + i] for i in range(4))
    pair = jnp.floor(column * 0.5)
    spot = jnp.where(
        counting(columns // 2, width) == spread(pair, columns // 2),
        jnp.ones((), bf16),
        jnp.zeros((), bf16),
    )
    count = (span + 1) * rows
    starts = [(v * (planes + 1) + base) * rows for v in range(3)]
    table = jnp.concatenate([table_ref[start : start + count, :] for start in starts], 0)
    sampled = dot_nn(table, jnp.concatenate([spot, spot], 0))

    def eight(x):
        return jnp.broadcast_to(x, (8, width))

    level = down_rows(8, width).astype(f32)
    at_plane = [eight(plane) == float(base + p) for p in range(span)]
    eighths = [jnp.floor(at * 0.125) for at in (row, next_row)]
    at_eighth = [[eight(part) == float(j) for j in range(rows // 8)] for part in eighths]
    corner = {}
    odd = eight(column - 2.0 * pair) > 0.5
    picked = {}
    for v in range(3):
        for e0 in range(2):
            for j in range(rows // 8):
                at = (v * (span + 1) + e0) * rows + 8 * j
                pick = sampled[at : at + 8]
                for p in range(1, span):
                    pick = jnp.where(at_plane[p], sampled[at + p * rows : at + p * rows + 8], pick)
                picked[v, e0, j] = pick
    for e2 in range(2):
        for e0 in range(2):
            chosen = [
                jnp.where(odd, picked[e2 + 1, e0, j], picked[e2, e0, j]) for j in range(rows // 8)
            ]
            for e1 in range(2):
                pick = chosen[0]
                for j in range(1, rows // 8):
                    pick = jnp.where(at_eighth[e1][j], chosen[j], pick)
                corner[e0, e1, e2] = pick
    fx, fz = eight(fx), eight(fz)
    weights = (amplitude * (1.0 - fy), amplitude * fy)
    gx = gy = gz = 0.0
    for e1 in range(2):
        here = level == eight((row, next_row)[e1] - 8.0 * eighths[e1])
        weight = jnp.where(here, eight(weights[e1]), 0.0)
        signed = jnp.where(here, eight(amplitude), 0.0)
        drop = [corner[e0, e1, 1] - corner[e0, e1, 0] for e0 in range(2)]
        value = [corner[e0, e1, 0] + fz * drop[e0] for e0 in range(2)]
        slope = value[1] - value[0]
        gx = gx + weight * slope
        gz = gz + weight * (drop[0] + fx * (drop[1] - drop[0]))
        middle = signed * (value[0] + fx * slope)
        gy = gy + middle if e1 else gy - middle
    return jnp.concatenate([jnp.sum(g, 0, keepdims=True) for g in (gx, gy, gz)], 0)


def blur_sheet(sheet):
    rows, columns = sheet.shape
    sheet = middle_tap * sheet + side_tap * (pltpu.roll(sheet, 1, 0) + pltpu.roll(sheet, rows - 1, 0))
    return middle_tap * sheet + side_tap * (
        pltpu.roll(sheet, 1, 1) + pltpu.roll(sheet, columns - 1, 1)
    )


def blur_along(sheets):
    return [
        middle_tap * sheets[i] + side_tap * (sheets[i - 1] + sheets[i + 1])
        for i in range(1, len(sheets) - 1)
    ]


def edges(place_ref, devices):
    not_first = jnp.where(place_ref[0] == 0, 0.0, 1.0)
    not_last = jnp.where(place_ref[0] == devices - 1, 0.0, 1.0)
    return not_first, not_last


def share_misfit(place_ref, devices, planes, rows, density, map_ref, own_ref, near_ref, far_ref):
    _, not_last = edges(place_ref, devices)
    density[planes] = density[planes] * not_last
    density = [blur_sheet(sheet) for sheet in density]
    parts = [side_tap * density[0], middle_tap * density[0] + side_tap * density[1]]
    parts += blur_along(density)
    parts += [side_tap * density[planes - 1] + middle_tap * density[planes]]
    parts += [side_tap * density[planes]]
    for p in range(planes):
        parts[p + 1] = parts[p + 1] - map_ref[p]
    for p in range(planes + 3):
        own_ref[p * rows : (p + 1) * rows, :] = parts[p]
    even = place_ref[0] % 2 == 0
    for p in range(3):
        up, down = parts[planes + p], parts[p]
        near_ref[p * rows : (p + 1) * rows, :] = jnp.where(even, up, down)
        far_ref[p * rows : (p + 1) * rows, :] = jnp.where(even, down, up)


def make_table(place_ref, devices, planes, rows, columns, own_ref, near_ref, far_ref, table_ref):
    not_first, not_last = edges(place_ref, devices)
    misfit = [own_ref[p * rows : (p + 1) * rows, :] for p in range(planes + 3)]
    even = place_ref[0] % 2 == 0
    for p in range(3):
        near = near_ref[p * rows : (p + 1) * rows, :]
        far = far_ref[p * rows : (p + 1) * rows, :]
        misfit[p] = misfit[p] + jnp.where(even, far, near)
        misfit[planes + p] = misfit[planes + p] + jnp.where(even, near, far)
    misfit[0] = misfit[0] * not_first
    misfit[planes + 1] = misfit[planes + 1] * not_last
    misfit[planes + 2] = misfit[planes + 2] * not_last
    pulled = [blur_sheet(sheet) for sheet in blur_along(misfit)]
    pulled[planes] = pulled[planes] * not_last
    half = columns // 2
    source = down_rows(columns, 3 * half)
    target = lax.broadcasted_iota(jnp.int32, (columns, 3 * half), 1)
    turn = target // half
    spread = jnp.where(source == (2 * (target - half * turn) + turn) % columns, 1.0, 0.0).astype(bf16)
    for grade, piece in enumerate(halves(jnp.concatenate(pulled, 0))):
        sorted_columns = dot_nn(piece, spread).astype(bf16)
        count = (planes + 1) * rows
        for v in range(3):
            table_ref[v * count : (v + 1) * count, grade * half : (grade + 1) * half] = (
                sorted_columns[:, v * half : (v + 1) * half]
            )


def load_tiles(ref, tiles):
    return jnp.concatenate([ref[t * fields : (t + 1) * fields, :] for t in tiles], 1)


def store_tiles(ref, tiles, value):
    for i, t in enumerate(tiles):
        ref[t * fields : (t + 1) * fields, :] = value[:, i * lanes : (i + 1) * lanes]


def chunks(devices, sub, planes, ordered):
    if ordered:
        return [([b * sub + k for b in range(devices)], k, 2) for k in range(sub)]
    tiles = devices * sub
    batch = max(b for b in range(1, 25) if tiles % b == 0)
    return [(range(i, i + batch), 0, planes) for i in range(0, tiles, batch)]


def in_order(message_ref, devices, sub):
    rows = [(b * sub + 1) * fields + fields - 1 for b in range(devices)]
    flags = jnp.concatenate([message_ref[row : row + 1, :] for row in rows], 0)
    return jnp.min(flags) > 0.5


def either(ordered_ref, planes, sub, work):
    if not sorted_buckets(planes, sub):
        work(False)
        return
    ordered = ordered_ref[0] == 1

    @pl.when(ordered)
    def _():
        work(True)

    @pl.when(jnp.logical_not(ordered))
    def _():
        work(False)


def add_density(sheets, state, base, span, rows, columns):
    part = density_part(state, base, span, rows, columns)
    for p in range(span + 1):
        sheet = part[p * rows : (p + 1) * rows]
        sheets[base + p] = sheet if sheets[base + p] is None else sheets[base + p] + sheet


def density_kernel(
    devices, sub, planes, rows, columns, place_ref, message_ref, map_ref, own_ref, near_ref, far_ref,
    ordered_ref,
):
    if sorted_buckets(planes, sub):
        ordered_ref[0] = jnp.where(in_order(message_ref, devices, sub), 1, 0)
    else:
        ordered_ref[0] = 0

    def work(ordered):
        sheets = [None] * (planes + 1)
        for tiles, base, span in chunks(devices, sub, planes, ordered):
            add_density(sheets, load_tiles(message_ref, tiles), base, span, rows, columns)
        share_misfit(place_ref, devices, planes, rows, sheets, map_ref, own_ref, near_ref, far_ref)

    either(ordered_ref, planes, sub, work)


def middle_kernel(
    devices, sub, planes, rows, columns, place_ref, ordered_ref, message_ref, was_ref, from_near_ref,
    from_far_ref, map_ref, moved_ref, first_ref, own_ref, near_ref, far_ref, table_ref,
):
    make_table(
        place_ref, devices, planes, rows, columns, was_ref, from_near_ref, from_far_ref, table_ref
    )

    def work(ordered):
        sheets, waiting = [None] * (planes + 1), None
        for tiles, base, span in chunks(devices, sub, planes, ordered):
            state = load_tiles(message_ref, tiles)
            gradient = gradient_part(state, table_ref, base, span, planes, rows, columns)
            moved = jnp.concatenate(
                [state[0:2], state[2:5] - probe_step * jnp.tanh(gradient), state[5:8]], 0
            )
            store_tiles(moved_ref, tiles, moved)
            store_tiles(
                first_ref, tiles,
                jnp.concatenate([gradient, jnp.zeros((5, gradient.shape[1]), f32)], 0),
            )
            if waiting is not None:
                add_density(sheets, *waiting, rows, columns)
            waiting = (moved, base, span)
        add_density(sheets, *waiting, rows, columns)
        share_misfit(place_ref, devices, planes, rows, sheets, map_ref, own_ref, near_ref, far_ref)

    either(ordered_ref, planes, sub, work)


def cross_list(left, right):
    return [
        left[1] * right[2] - left[2] * right[1],
        left[2] * right[0] - left[0] * right[2],
        left[0] * right[1] - left[1] * right[0],
    ]


def last_kernel(
    devices, sub, planes, rows, columns, place_ref, ordered_ref, message_ref, moved_ref, first_ref,
    was_ref, from_near_ref, from_far_ref, reply_ref, table_ref, terms_ref,
):
    make_table(
        place_ref, devices, planes, rows, columns, was_ref, from_near_ref, from_far_ref, table_ref
    )
    tiles = devices * sub

    def work(ordered):
        for group, base, span in chunks(devices, sub, planes, ordered):
            first = load_tiles(first_ref, group)[0:3]
            moved = load_tiles(moved_ref, group)
            second = gradient_part(moved, table_ref, base, span, planes, rows, columns)
            rest = jnp.zeros((2, second.shape[1]), f32)
            store_tiles(reply_ref, group, jnp.concatenate([first, second, rest], 0))

    either(ordered_ref, planes, sub, work)

    def field(ref, f):
        return ref[pl.ds(f, tiles, stride=fields), :]

    cell = field(message_ref, 0)
    plane = jnp.floor(cell * (1.0 / rows))
    cells = (plane + (place_ref[0] * planes).astype(f32), cell - plane * rows, field(message_ref, 1))
    terms = []
    for e, ref in enumerate((message_ref, moved_ref)):
        g = [field(reply_ref, 3 * e + d) for d in range(3)]
        terms += g + cross_list([cells[d] + field(ref, 2 + d) for d in range(3)], g)
    terms.append(jnp.where(field(message_ref, 5) > 0.0, 1.0, 0.0))
    terms += [jnp.zeros_like(cell)] * 3
    for i, term in enumerate(terms):
        terms_ref[pl.ds(i, tiles, stride=16), :] = term
    last_of = jnp.concatenate(
        [
            message_ref[d * sub * fields + fields - 1 : d * sub * fields + fields, :]
            for d in range(devices)
        ],
        0,
    )
    receiver = down_rows(devices, lanes)
    sums = jnp.zeros((devices, 16), f32)
    batch = 16
    for i in range(0, tiles, batch):
        chosen = [
            jnp.where(
                (receiver < t // sub) & (last_of == message_ref[t * fields + 6 : t * fields + 7, :]),
                1.0,
                0.0,
            )
            for t in range(i, i + batch)
        ]
        chosen = jnp.concatenate(chosen, 1).astype(bf16)
        block = jnp.concatenate([terms_ref[t * 16 : (t + 1) * 16, :] for t in range(i, i + batch)], 1)
        sums = sums + sum(dot_nt(chosen, piece) for piece in thirds(block))
    sums = jnp.concatenate([sums, jnp.zeros((devices, lanes - 16), f32)], 1)
    for d in range(devices):
        reply_ref[d * sub * fields + fields - 1 : d * sub * fields + fields, :] = sums[d : d + 1]


def chain_kernel(
    devices, sub, planes, columns, reply_ref, slot_ref, home_ref, torque_ref, gradient_ref
):
    atoms = slot_ref.shape[1]
    blocks = atoms // lanes
    tiles = devices * sub
    high, low = halves(reply_ref[...])
    left = jnp.concatenate([high, low], 1)
    width = 512
    found = []
    for c in range(atoms // width):
        at = slice(c * width, (c + 1) * width)
        spot = jnp.where(down_rows(lanes, width) == slot_ref[1:2, at], 1.0, 0.0).astype(bf16)
        picked = dot_nn(left, jnp.concatenate([spot, spot], 0))
        which = jnp.broadcast_to(slot_ref[0:1, at], (fields, width))
        total = jnp.zeros((fields, width), f32)
        for t in range(tiles):
            total = jnp.where(which == t, picked[t * fields : (t + 1) * fields], total)
        found.append(total)
    gradients = jnp.concatenate(found, 1)[0:6]
    gradient_ref[...] = gradients
    fraction = home_ref[3:6, :]
    moved = fraction - probe_step * jnp.tanh(gradients[0:3])
    base = [home_ref[d : d + 1, :] for d in range(3)]
    axis = [home_ref[7 + d : 8 + d, :] for d in range(3)]
    positions = [[base[d] + offset[d : d + 1] for d in range(3)] for offset in (fraction, moved)]
    pieces = []
    for e in range(2):
        g = [gradients[3 * e + d : 3 * e + d + 1] for d in range(3)]
        pieces += g + cross_list(positions[e], g)
    pieces.append(jnp.ones((1, atoms), f32))
    pieces.append(jnp.zeros((3, atoms), f32))
    stacked = jnp.concatenate(thirds(jnp.concatenate(pieces, 0)), 0)

    def joined(x):
        return x[0:16] + x[16:32] + x[32:48]

    chain = home_ref[6:7, :]
    chain_rows = jnp.concatenate([chain[:, j * lanes : (j + 1) * lanes] for j in range(blocks)], 0)
    ends = jnp.broadcast_to(chain_rows[:, lanes - 1 :], (blocks, atoms))
    later = lax.broadcasted_iota(jnp.int32, (blocks, atoms), 1) >= lanes * (
        down_rows(blocks, atoms) + 1
    )
    bridge = jnp.where(later & (ends == chain), 1.0, 0.0).astype(bf16)
    carries = joined(dot_nt(stacked, bridge))
    arrived = jnp.zeros((1, lanes), f32)
    for d in range(devices):
        arrived = arrived + reply_ref[d * sub * fields + fields - 1 : d * sub * fields + fields, :]
    diagonal = down_rows(16, lanes) == lax.broadcasted_iota(jnp.int32, (16, lanes), 1)
    arrived = jnp.sum(jnp.where(diagonal, arrived, 0.0), 1, keepdims=True)
    padded = jnp.concatenate([chain_rows, jnp.zeros((lanes - blocks, lanes), f32)], 0)
    down_chain = jnp.transpose(padded)
    not_before = down_rows(lanes, lanes) >= lax.broadcasted_iota(jnp.int32, (lanes, lanes), 1)
    closing = chain[:, atoms - 1 :]
    sums = []
    for j in range(blocks):
        at = slice(j * lanes, (j + 1) * lanes)
        mask = not_before & (down_chain[:, j : j + 1] == chain[:, at])
        local = joined(dot_nn(stacked[:, at], jnp.where(mask, 1.0, 0.0).astype(bf16)))
        end = chain[:, (j + 1) * lanes - 1 : (j + 1) * lanes]
        carry = carries[:, j : j + 1] + jnp.where(end == closing, arrived, 0.0)
        sums.append(local + jnp.where(chain[:, at] == end, carry, 0.0))
    totals = jnp.concatenate(sums, 1)
    scale = 1.0 / (columns * jnp.sqrt(totals[12:13]))
    torques = []
    for e in range(2):
        force = [totals[6 * e + d : 6 * e + d + 1] for d in range(3)]
        lever = cross_list(positions[e], force)
        turn = 0.0
        for d in range(3):
            turn = turn + axis[d] * (totals[6 * e + 3 + d : 6 * e + 4 + d] - lever[d])
        torques.append(turn * scale)
    torque_ref[...] = jnp.concatenate(torques, 0)


def whole(count):
    return [pl.BlockSpec(memory_space=pltpu.VMEM)] * count


def settings():
    return pltpu.CompilerParams(vmem_limit_bytes=room)


def shape_of(*dims, dtype=f32):
    return jax.ShapeDtypeStruct(dims, dtype)


def swap_near(value):
    count = lax.axis_size("bx")
    return lax.ppermute(value, "bx", [(i, i ^ 1) for i in range(count)])


def swap_far(value):
    count = lax.axis_size("bx")
    pairs = []
    for i in range(1, count - 1, 2):
        pairs += [(i, i + 1), (i + 1, i)]
    return lax.ppermute(value, "bx", pairs)


def exchange(value):
    return lax.all_to_all(value, "bx", split_axis=0, concat_axis=0, tiled=True)


def shards(
    density_map,
    amplitude,
    fraction,
    torsion_axis,
    brick_owner,
    plane_offset,
    row_offset,
    column_offset,
    chain_index,
):
    planes, rows, columns = density_map.shape
    atoms = amplitude.shape[0]
    devices = lax.axis_size("bx")
    capacity = 3 * atoms // devices
    sub = -(-capacity // lanes)
    tiles = devices * sub
    grid = (planes, rows, columns)
    place = lax.axis_index("bx").astype(jnp.int32).reshape(1)
    scalar = [pl.BlockSpec(memory_space=pltpu.SMEM)]

    owner, plane, row, column, chain = (
        item.reshape(1, atoms)
        for item in (brick_owner, plane_offset, row_offset, column_offset, chain_index)
    )
    held = [pltpu.VMEM((1, atoms), jnp.int32)] * 5
    held += [pltpu.VMEM((1, atoms), f32)] + [pltpu.VMEM((3, atoms), f32)] * 2
    message, slot, home = pl.pallas_call(
        functools.partial(pack_kernel, devices, sub, planes, rows),
        out_shape=(
            shape_of(tiles * fields, lanes),
            shape_of(2, atoms, dtype=jnp.int32),
            shape_of(10, atoms),
        ),
        in_specs=[pl.BlockSpec(memory_space=pltpu.HBM)] * 8,
        out_specs=whole(3),
        scratch_shapes=held + [pltpu.SemaphoreType.DMA((8,))],
        name="pack",
    )(owner, plane, row, column, chain, amplitude.reshape(1, atoms), fraction, torsion_axis)
    message = exchange(message)

    own_shape = shape_of((planes + 3) * rows, columns)
    edge_shape = shape_of(3 * rows, columns)
    own, near, far, ordered = pl.pallas_call(
        functools.partial(density_kernel, devices, sub, *grid),
        out_shape=(own_shape, edge_shape, edge_shape, shape_of(1, dtype=jnp.int32)),
        in_specs=scalar + whole(2),
        out_specs=whole(3) + scalar,
        compiler_params=settings(),
        name="density",
    )(place, message, density_map)
    near, far = swap_near(near), swap_far(far)
    table = pltpu.VMEM((3 * (planes + 1) * rows, columns), bf16)
    moved, first, own, near, far = pl.pallas_call(
        functools.partial(middle_kernel, devices, sub, *grid),
        out_shape=(
            shape_of(tiles * fields, lanes),
            shape_of(tiles * fields, lanes),
            own_shape,
            edge_shape,
            edge_shape,
        ),
        in_specs=scalar * 2 + whole(5),
        out_specs=whole(5),
        scratch_shapes=[table],
        compiler_params=settings(),
        name="middle",
    )(place, ordered, message, own, near, far, density_map)
    near, far = swap_near(near), swap_far(far)
    reply = pl.pallas_call(
        functools.partial(last_kernel, devices, sub, *grid),
        out_shape=shape_of(tiles * fields, lanes),
        in_specs=scalar * 2 + whole(6),
        out_specs=whole(1)[0],
        scratch_shapes=[table, pltpu.VMEM((tiles * 16, lanes), f32)],
        compiler_params=settings(),
        name="last",
    )(place, ordered, message, moved, first, own, near, far)
    reply = exchange(reply)
    torques, gradients = pl.pallas_call(
        functools.partial(chain_kernel, devices, sub, planes, columns),
        out_shape=(shape_of(2, atoms), shape_of(6, atoms)),
        in_specs=whole(3),
        out_specs=whole(2),
        compiler_params=settings(),
        name="chains",
    )(reply, slot, home)
    return torques, gradients


def solution(mesh):
    return jax.shard_map(
        shards,
        mesh=mesh,
        in_specs=(
            P(("grp", "bx"), None, None),
            P(("grp", "bx")),
            P(None, ("grp", "bx")),
            P(None, ("grp", "bx")),
            P(("grp", "bx"), None),
            P(("grp", "bx")),
            P(("grp", "bx")),
            P(("grp", "bx")),
            P(("grp", "bx")),
        ),
        out_specs=(P(None, ("grp", "bx")), P(None, ("grp", "bx"))),
        check_vma=False,
    )
```
